32 devices in a mesh: dp: 8 (over z, x), etp: 4 (over y, core).
Axes of the slice: x: 2, y: 2, z: 4, core: 2. Of those that a mesh axis runs over, the one named last changes fastest.
Arguments:
- tokens: bfloat16 [16384, 5120], P(('dp', 'etp')), may hold values from -6 to 6
- slots: int32 [2048], P(('dp', 'etp')), may hold values from 0 to 511, as said below
- gate_probs: bfloat16 [2048], P(('dp', 'etp')), may hold values from 0.099609375 to 1
- w_gate: bfloat16 [5120, 1536], P('dp', 'etp'), may hold values from -0.078125 to 0.078125
- w_up: bfloat16 [5120, 1536], P('dp', 'etp'), may hold values from -0.078125 to 0.078125
- d_hidden: bfloat16 [2048, 1536], P('dp', 'etp'), may hold values from -6 to 6
Outputs:
- hidden: bfloat16 [2048, 1536], P('dp', 'etp')
- grad_tokens: bfloat16 [16384, 5120], P(('dp', 'etp'))
- grad_gate: float32 [5120, 1536], P('dp', 'etp')
- grad_up: float32 [5120, 1536], P('dp', 'etp')
The draws below stay inside these ranges and needn't reach their ends.
Inputs may be any that keep to these rules, and one draw needn't show every extreme that they name: `slots`: within each aligned block of 64 entries (one device's) the values are distinct; every block holds 0 and 511.
All inputs are finite; a program needn't handle non-finite values.
Results may differ from the reference program's by a relative error of at most 0.0049.
Values may be sent and summed in bfloat16 or wider, within the bound.
No kernel may reach another device: no remote copies, remote signals or barrier semaphores. Data moves between devices by JAX's collectives and lax.ppermute only.
A program may use at most 128 MiB of HBM per device.

```python
import jax
import jax.numpy as jnp
from jax import lax

D = 5120
FF = 1536
TOK_DEV = 512
CAP_DEV = 64
TOKENS = 16384
SLOTS = 2048


def draw_slots(key, part):
    key = jax.random.fold_in(key, 7)
    blocks = SLOTS // CAP_DEV
    block_keys = jax.random.split(key, blocks)

    def single_block(block_key):
        first_key, second_key = jax.random.split(block_key)
        middle_rows = jax.random.permutation(first_key, TOK_DEV - 2)[:CAP_DEV - 2].astype(jnp.int32) + 1
        picked = jnp.concatenate([jnp.zeros((1,), jnp.int32), jnp.full((1,), TOK_DEV - 1, jnp.int32), middle_rows])
        return picked[jax.random.permutation(second_key, CAP_DEV)]
    return jax.vmap(single_block)(block_keys).reshape(-1).astype(jnp.int32)


def strengthened(entries, own_key, source, target, blocks, factor):
    def block_of(dim):
        return (jnp.arange(entries.shape[dim]) // (entries.shape[dim] // blocks)).reshape((-1,) + (1,) * (entries.ndim - 1 - dim))

    near = jax.random.permutation(own_key, blocks)[block_of(target)]
    second = (block_of(target) + blocks // 2) % blocks
    return jnp.where((block_of(source) == near) | (block_of(source) == second), factor * entries, entries)


def steps_of(stream_key, shape, shards, least, top_value):
    factor_of, own = 1.0, jax.random.fold_in(stream_key, 6)
    for position, shards_of in shards:
        draws = jnp.exp(jax.random.uniform(jax.random.fold_in(own, position), (shards_of,), jnp.float32, least / len(shards), top_value / len(shards)))
        factor_of = factor_of * jnp.repeat(draws, shape[position] // shards_of).reshape([-1 if axis == position else 1 for axis in range(len(shape))])
    return factor_of


def noise(own_key, extent, deviation, most, shards=(), kind=jnp.bfloat16):
    gain = steps_of(own_key, extent, shards, -0.22, 0.18) if shards else 1.0
    values = jax.random.normal(own_key, extent, jnp.float32) * deviation * gain
    return jnp.minimum(jnp.maximum(values, -most), most).astype(kind)


def noise_with(key, shape, width, bound, pieces, heavy, kind=jnp.bfloat16):
    array = width * jax.random.normal(key, shape, jnp.float32)
    if pieces:
        array = array * steps_of(key, shape, pieces, -0.22, 0.18)
    return jnp.clip(strengthened(array, jax.random.fold_in(key, 3), *heavy), -bound, bound).astype(kind)


def setup_inputs(seed: int = 0) -> dict:
    arg_keys = jax.random.split(jax.random.key(seed), 7)
    return {
        "tokens": noise_with(arg_keys[0], (TOKENS, D), 1.0, 6.0, ((0, 32),), (0, 1, 32, 2.75)),
        "slots": draw_slots(jax.random.fold_in(arg_keys[6], 71), 0),
        "gate_probs": jnp.clip(0.099609375 + 0.9003906 * jax.random.uniform(arg_keys[2], (SLOTS,), jnp.float32) ** steps_of(arg_keys[2], (SLOTS,), ((0, 32),), -0.2, 0.2), 0.099609375, 1.0).astype(jnp.bfloat16),
        "w_gate": noise(arg_keys[3], (D, FF), D ** -0.5, 0.078125, ((0, 8), (1, 4))),
        "w_up": noise(arg_keys[4], (D, FF), D ** -0.5, 0.078125, ((0, 8), (1, 4))),
        "d_hidden": noise(arg_keys[5], (SLOTS, FF), 1.0, 6.0, ((0, 8), (1, 4))),
    }


def reference(tokens, slots, gate_probs, w_gate, w_up, d_hidden):
    owner = jnp.arange(SLOTS, dtype=jnp.int32) // CAP_DEV
    rows = (owner * TOK_DEV + slots).astype(jnp.int32)
    inputs = tokens[rows]
    gate_pre = jnp.dot(inputs, w_gate, preferred_element_type=jnp.float32)
    up_pre = jnp.dot(inputs, w_up, preferred_element_type=jnp.float32)
    prob = gate_probs.astype(jnp.float32)[:, None]
    sig = jax.nn.sigmoid(gate_pre)
    act = gate_pre * sig
    hidden = (prob * act * up_pre).astype(jnp.bfloat16)
    scaled = d_hidden.astype(jnp.float32) * prob
    gate_grad = (scaled * up_pre * sig * (1.0 + gate_pre * (1.0 - sig))).astype(jnp.bfloat16)
    up_grad = (scaled * act).astype(jnp.bfloat16)
    contract_rows = (((0,), (0,)), ((), ()))
    grad_gate = lax.dot_general(inputs, gate_grad, contract_rows, preferred_element_type=jnp.float32)
    grad_up = lax.dot_general(inputs, up_grad, contract_rows, preferred_element_type=jnp.float32)
    contract_cols = (((1,), (1,)), ((), ()))
    input_grad = lax.dot_general(gate_grad, w_gate, contract_cols, preferred_element_type=jnp.float32)
    input_grad = input_grad + lax.dot_general(up_grad, w_up, contract_cols, preferred_element_type=jnp.float32)
    grad_tokens = jnp.zeros((TOKENS, D), jnp.bfloat16).at[rows].set(input_grad.astype(jnp.bfloat16))
    return hidden, grad_tokens, grad_gate, grad_up
```

```python
import jax
import jax.numpy as jnp
from jax import lax
from jax.sharding import PartitionSpec as P

F32 = jnp.float32
BF16 = jnp.bfloat16


def split_dp(dp):
    outer = 1
    while 4 * outer * outer <= 2 * dp:
        outer *= 2
    return outer, dp // outer


def make_shards(dp_size, etp_size):
    outer, inner = split_dp(dp_size)

    def over_outer(value, k):
        pairs = [(i, i ^ (k * inner)) for i in range(dp_size)]
        return lax.ppermute(value, "dp", pairs)

    def over_inner(value, j):
        pairs = [(i, i ^ j) for i in range(dp_size)]
        return lax.ppermute(value, "dp", pairs)

    def over_etp(value, e):
        pairs = [(i, i ^ e) for i in range(etp_size)]
        return lax.ppermute(value, "etp", pairs)

    chunk_order = [0]
    bit = etp_size // 2
    bits = []
    while bit:
        bits.append(bit)
        chunk_order = chunk_order + [c ^ bit for c in chunk_order]
        bit //= 2

    def gather_etp(value):
        for b in bits:
            value = jnp.concatenate([value, over_etp(value, b)], axis=0)
        return value

    def reduce_etp(value):
        for b in reversed(bits):
            half = value.shape[0] // 2
            sent = over_etp(value[half:].astype(BF16), b)
            value = value[:half] + sent.astype(F32)
        return value

    far_first = sorted(range(1, outer), key=lambda k: -k)

    def shards(tokens, slots, gate_probs, w_gate, w_up, d_hidden):
        dp = lax.axis_index("dp")
        etp = lax.axis_index("etp")
        a, b = dp // inner, dp % inner
        depth, width = w_gate.shape
        cap = slots.shape[0]
        tok = tokens.shape[0]
        span = depth * inner

        weights = jnp.zeros((inner, depth, 2 * width), BF16)
        for j in range(inner):
            gate_j = over_inner(w_gate, j) if j else w_gate
            up_j = over_inner(w_up, j) if j else w_up
            both = jnp.concatenate([gate_j, up_j], axis=1)[None]
            weights = lax.dynamic_update_slice(weights, both, (b ^ j, 0, 0))
        weights = weights.reshape(span, 2 * width)

        onehot = (slots[:, None] == jnp.arange(tok, dtype=slots.dtype)[None, :]).astype(BF16)
        rows = jnp.dot(onehot, tokens, preferred_element_type=F32).astype(BF16)
        x_chunks = [None] * outer
        for k in far_first + [0]:
            piece = lax.dynamic_slice(rows, (0, (a ^ k) * span), (cap, span))
            x_chunks[k] = over_outer(piece, k) if k else piece
        x_chunks = [gather_etp(c) for c in x_chunks]
        probs = gather_etp(gate_probs)

        pre = jnp.dot(x_chunks[0], weights, preferred_element_type=F32)
        parts = {
            k: over_outer(jnp.dot(x_chunks[k], weights, preferred_element_type=F32).astype(BF16), k)
            for k in far_first
        }
        for k in far_first:
            pre = pre + parts[k].astype(F32)
        gate_pre, up_pre = pre[:, :width], pre[:, width:]

        order = etp ^ jnp.array(chunk_order, jnp.int32)
        d_own = jnp.take(d_hidden.reshape(etp_size, cap, width), order, axis=0).reshape(-1, width)
        prob = probs.astype(F32)[:, None]
        sig = jax.nn.sigmoid(gate_pre)
        act = gate_pre * sig
        hidden = (prob * act * up_pre).astype(BF16)
        scaled = d_own.astype(F32) * prob
        gate_grad = (scaled * up_pre * sig * (1.0 + gate_pre * (1.0 - sig))).astype(BF16)
        up_grad = (scaled * act).astype(BF16)
        paired = jnp.concatenate([gate_grad, up_grad], axis=1)
        inverse = jnp.zeros((etp_size,), jnp.int32).at[order].set(jnp.arange(etp_size, dtype=jnp.int32))
        hidden = jnp.take(hidden.reshape(etp_size, cap, width), inverse, axis=0).reshape(-1, width)

        grads = [over_outer(paired, k) if k else paired for k in range(outer)]

        dx = jnp.zeros((cap, outer * span), BF16)
        for k in range(outer):
            partial = lax.dot_general(
                grads[k], weights, (((1,), (1,)), ((), ())), preferred_element_type=F32
            )
            own = reduce_etp(partial).astype(BF16)
            own = over_outer(own, k) if k else own
            dx = lax.dynamic_update_slice(dx, own, (0, (a ^ k) * span))
        grad_tokens = lax.dot_general(
            onehot, dx, (((0,), (0,)), ((), ())), preferred_element_type=F32
        ).astype(BF16)

        summed = lax.dot_general(
            jnp.concatenate(x_chunks, axis=0),
            jnp.concatenate(grads, axis=0),
            (((0,), (0,)), ((), ())),
            preferred_element_type=F32,
        )
        total = lax.dynamic_slice(summed, (b * depth, 0), (depth, 2 * width))
        for j in range(1, inner):
            part = lax.dynamic_slice(summed, ((b ^ j) * depth, 0), (depth, 2 * width))
            total = total + over_inner(part.astype(BF16), j).astype(F32)
        return (hidden, grad_tokens, total[:, :width], total[:, width:])

    return shards


def solution(mesh):
    in_specs = (
        P(("dp", "etp"), None),
        P(("dp", "etp")),
        P(("dp", "etp")),
        P("dp", "etp"),
        P("dp", "etp"),
        P("dp", "etp"),
    )
    out_specs = (P("dp", "etp"), P(("dp", "etp"), None), P("dp", "etp"), P("dp", "etp"))
    shards = make_shards(mesh.shape["dp"], mesh.shape["etp"])
    return jax.shard_map(shards, mesh=mesh, in_specs=in_specs, out_specs=out_specs, check_vma=False)
```

```python
import functools

import jax
import jax.numpy as jnp
from jax import lax
from jax.experimental import pallas as pl
from jax.experimental.pallas import tpu as pltpu
from jax.sharding import PartitionSpec as P

F32 = jnp.float32
BF16 = jnp.bfloat16


def split_dp(dp):
    outer = 1
    while 4 * outer * outer <= 2 * dp:
        outer *= 2
    return outer, dp // outer


def after(value, *others):
    return lax.optimization_barrier((value,) + others)[0]


def gate_kernel(steps, order_ref, pre_ref, prob_ref, cot_ref, *refs):
    part_refs, (hidden_ref, grad_ref) = refs[:-2], refs[-2:]
    rows, width = cot_ref.shape
    cap = rows // steps
    for i in range(steps):
        here = pl.ds(i * cap, cap)
        there = pl.ds(pl.multiple_of(order_ref[i] * cap, cap), cap)
        total = pre_ref[here, :]
        for part_ref in part_refs:
            total = total + part_ref[here, :].astype(F32)
        gate, up = total[:, :width], total[:, width:]
        prob = prob_ref[here, :].astype(F32)
        sig = jax.nn.sigmoid(gate)
        act = gate * sig
        hidden_ref[there, :] = (prob * act * up).astype(BF16)
        scaled = cot_ref[there, :].astype(F32) * prob
        grad_ref[here, :width] = (scaled * up * sig * (1.0 + gate * (1.0 - sig))).astype(BF16)
        grad_ref[here, width:] = (scaled * act).astype(BF16)


def gate_call(order, pre, prob, cotangent, parts):
    rows, width = cotangent.shape
    steps = order.shape[0]
    vmem = pl.BlockSpec(memory_space=pltpu.VMEM)
    return pl.pallas_call(
        functools.partial(gate_kernel, steps),
        out_shape=(
            jax.ShapeDtypeStruct((rows, width), BF16),
            jax.ShapeDtypeStruct((rows, 2 * width), BF16),
        ),
        in_specs=[pl.BlockSpec(memory_space=pltpu.SMEM)] + [vmem] * (3 + len(parts)),
        out_specs=(vmem, vmem),
        compiler_params=pltpu.CompilerParams(vmem_limit_bytes=24 * 2**20),
        cost_estimate=pl.CostEstimate(
            flops=20 * rows * width, bytes_accessed=rows * width * 30, transcendentals=rows * width
        ),
    )(order, pre, prob, cotangent, *parts)


def make_shards(dp_size, etp_size):
    outer, inner = split_dp(dp_size)

    def over_outer(value, k):
        pairs = [(i, i ^ (k * inner)) for i in range(dp_size)]
        return lax.ppermute(value, "dp", pairs)

    def over_inner(value, j):
        pairs = [(i, i ^ j) for i in range(dp_size)]
        return lax.ppermute(value, "dp", pairs)

    def over_etp(value, e):
        pairs = [(i, i ^ e) for i in range(etp_size)]
        return lax.ppermute(value, "etp", pairs)

    chunk_order = [0]
    bit = etp_size // 2
    bits = []
    while bit:
        bits.append(bit)
        chunk_order = chunk_order + [c ^ bit for c in chunk_order]
        bit //= 2

    def gather_etp(value):
        for b in bits:
            value = jnp.concatenate([value, over_etp(value, b)], axis=0)
        return value

    def reduce_etp(value):
        for b in reversed(bits):
            half = value.shape[0] // 2
            sent = over_etp(value[half:].astype(BF16), b)
            value = value[:half] + sent.astype(F32)
        return value

    far_first = sorted(range(1, outer), key=lambda k: -k)
    near_first = sorted(range(1, outer))

    def shards(tokens, slots, gate_probs, w_gate, w_up, d_hidden):
        dp = lax.axis_index("dp")
        etp = lax.axis_index("etp")
        a, b = dp // inner, dp % inner
        depth, width = w_gate.shape
        cap = slots.shape[0]
        tok = tokens.shape[0]
        span = depth * inner

        weights = [jnp.concatenate([w_gate, w_up], axis=1)]
        for j in range(1, inner):
            weights.append(jnp.concatenate([over_inner(w_gate, j), over_inner(w_up, j)], axis=1))
        weights = jnp.concatenate(weights, axis=0)

        onehot = (slots[:, None] == jnp.arange(tok, dtype=slots.dtype)[None, :]).astype(BF16)
        rows = jnp.dot(onehot, tokens, preferred_element_type=F32).astype(BF16)
        pieces = {}
        for k in far_first + [0]:
            pieces[k] = jnp.concatenate(
                [
                    lax.dynamic_slice(rows, (0, (a ^ k) * span + (b ^ j) * depth), (cap, depth))
                    for j in range(inner)
                ],
                axis=1,
            )
        got = {k: over_outer(pieces[k], k) for k in far_first}
        x_chunks = {k: gather_etp(got[k]) for k in far_first}
        x_chunks[0] = gather_etp(after(pieces[0], got[near_first[0]]))
        probs = gather_etp(after(gate_probs, x_chunks[0]))

        parts = {
            k: over_outer(jnp.dot(x_chunks[k], weights, preferred_element_type=F32).astype(BF16), k)
            for k in far_first
        }
        pre = jnp.dot(x_chunks[0], weights, preferred_element_type=F32)
        order = etp ^ jnp.array(chunk_order, jnp.int32)
        hidden, paired = gate_call(
            order, pre, probs[:, None], d_hidden, [parts[k] for k in near_first]
        )

        grads = {k: over_outer(paired, k) for k in far_first}
        grads[0] = paired

        dx = jnp.zeros((cap, outer * span), BF16)
        last = paired
        for k in [0] + near_first:
            partial = lax.dot_general(
                after(grads[k], last), weights, (((1,), (1,)), ((), ())), preferred_element_type=F32
            )
            last = partial
            own = reduce_etp(partial).astype(BF16)
            own = over_outer(own, k) if k else own
            for j in range(inner):
                block = own[:, j * depth : (j + 1) * depth]
                dx = lax.dynamic_update_slice(dx, block, (0, (a ^ k) * span + (b ^ j) * depth))
        grad_tokens = lax.dot_general(
            onehot, dx, (((0,), (0,)), ((), ())), preferred_element_type=F32
        ).astype(BF16)

        keys = [0] + near_first
        summed = lax.dot_general(
            jnp.concatenate([x_chunks[k] for k in keys], axis=0),
            after(jnp.concatenate([grads[k] for k in keys], axis=0), last),
            (((0,), (0,)), ((), ())),
            preferred_element_type=F32,
        )
        total = summed[:depth]
        for j in range(1, inner):
            part = summed[j * depth : (j + 1) * depth]
            total = total + over_inner(part.astype(BF16), j).astype(F32)
        return (hidden, grad_tokens, total[:, :width], total[:, width:])

    return shards


def solution(mesh):
    in_specs = (
        P(("dp", "etp"), None),
        P(("dp", "etp")),
        P(("dp", "etp")),
        P("dp", "etp"),
        P("dp", "etp"),
        P("dp", "etp"),
    )
    out_specs = (P("dp", "etp"), P(("dp", "etp"), None), P("dp", "etp"), P("dp", "etp"))
    shards = make_shards(mesh.shape["dp"], mesh.shape["etp"])
    return jax.shard_map(shards, mesh=mesh, in_specs=in_specs, out_specs=out_specs, check_vma=False)
```

```python
import functools

import jax
import jax.numpy as jnp
from jax import lax
from jax.experimental import pallas as pl
from jax.experimental.pallas import tpu as pltpu
from jax.sharding import PartitionSpec as P

F32 = jnp.float32
BF16 = jnp.bfloat16


def split_dp(dp):
    outer = 1
    while 4 * outer * outer <= 2 * dp:
        outer *= 2
    return outer, dp // outer


def after(value, *others):
    return lax.optimization_barrier((value,) + others)[0]


def gate_kernel(steps, order_ref, pre_ref, prob_ref, cot_ref, *refs):
    part_refs, (hidden_ref, grad_ref) = refs[:-2], refs[-2:]
    rows, width = cot_ref.shape
    cap = rows // steps
    for i in range(steps):
        here = pl.ds(i * cap, cap)
        there = pl.ds(pl.multiple_of(order_ref[i] * cap, cap), cap)
        total = pre_ref[here, :]
        for part_ref in part_refs:
            total = total + part_ref[here, :].astype(F32)
        gate, up = total[:, :width], total[:, width:]
        prob = prob_ref[here, :].astype(F32)
        sig = jax.nn.sigmoid(gate)
        act = gate * sig
        hidden_ref[there, :] = (prob * act * up).astype(BF16)
        scaled = cot_ref[there, :].astype(F32) * prob
        grad_ref[here, :width] = (scaled * up * sig * (1.0 + gate * (1.0 - sig))).astype(BF16)
        grad_ref[here, width:] = (scaled * act).astype(BF16)


def gate_call(order, pre, prob, cotangent, parts):
    rows, width = cotangent.shape
    steps = order.shape[0]
    vmem = pl.BlockSpec(memory_space=pltpu.VMEM)
    return pl.pallas_call(
        functools.partial(gate_kernel, steps),
        out_shape=(
            jax.ShapeDtypeStruct((rows, width), BF16),
            jax.ShapeDtypeStruct((rows, 2 * width), BF16),
        ),
        in_specs=[pl.BlockSpec(memory_space=pltpu.SMEM)] + [vmem] * (3 + len(parts)),
        out_specs=(vmem, vmem),
        compiler_params=pltpu.CompilerParams(vmem_limit_bytes=24 * 2**20),
        cost_estimate=pl.CostEstimate(
            flops=20 * rows * width, bytes_accessed=rows * width * 30, transcendentals=rows * width
        ),
    )(order, pre, prob, cotangent, *parts)


def place_kernel(place_ref, slots_ref, chunk_ref, *refs):
    out_ref = refs[-1]
    rows = lax.broadcasted_iota(jnp.int32, (out_ref.shape[0], slots_ref.shape[1]), 0)
    onehot = (rows == slots_ref[...]).astype(BF16)
    out_ref[...] = jnp.dot(onehot, chunk_ref[...], preferred_element_type=F32).astype(BF16)


def place_call(place, slots, chunk, tok, columns, buffer):
    cap = chunk.shape[0]
    blocks = place.shape[0]
    depth = chunk.shape[1] // blocks
    in_specs = [
        pl.BlockSpec((1, cap), lambda i, place: (0, 0)),
        pl.BlockSpec((cap, depth), lambda i, place: (0, i)),
    ]
    operands = [place, slots[None, :], chunk]
    aliases = {}
    if buffer is not None:
        in_specs.append(pl.BlockSpec(memory_space=pl.ANY))
        operands.append(buffer)
        aliases = {3: 0}
    return pl.pallas_call(
        place_kernel,
        out_shape=jax.ShapeDtypeStruct((tok, columns), BF16),
        grid_spec=pltpu.PrefetchScalarGridSpec(
            num_scalar_prefetch=1,
            grid=(blocks,),
            in_specs=in_specs,
            out_specs=pl.BlockSpec((tok, depth), lambda i, place: (0, place[i])),
        ),
        input_output_aliases=aliases,
        compiler_params=pltpu.CompilerParams(vmem_limit_bytes=16 * 2**20),
        cost_estimate=pl.CostEstimate(
            flops=2 * tok * cap * chunk.shape[1], bytes_accessed=2 * tok * chunk.shape[1], transcendentals=0
        ),
    )(*operands)


def make_shards(dp_size, etp_size):
    outer, inner = split_dp(dp_size)
    relay = outer == 4

    def over_outer(value, k):
        pairs = [(i, i ^ (k * inner)) for i in range(dp_size)]
        return lax.ppermute(value, "dp", pairs)

    def outer_pairs(value, pairs):
        pairs = [(s * inner + i, t * inner + i) for s, t in pairs for i in range(inner)]
        return lax.ppermute(value, "dp", pairs)

    def over_inner(value, j):
        pairs = [(i, i ^ j) for i in range(dp_size)]
        return lax.ppermute(value, "dp", pairs)

    def over_etp(value, e):
        pairs = [(i, i ^ e) for i in range(etp_size)]
        return lax.ppermute(value, "etp", pairs)

    chunk_order = [0]
    bit = etp_size // 2
    bits = []
    while bit:
        bits.append(bit)
        chunk_order = chunk_order + [c ^ bit for c in chunk_order]
        bit //= 2

    def gather_etp(value):
        for b in bits:
            value = jnp.concatenate([value, over_etp(value, b)], axis=0)
        return value

    def reduce_etp(value):
        for b in reversed(bits):
            half = value.shape[0] // 2
            sent = over_etp(value[half:].astype(BF16), b)
            value = value[:half] + sent.astype(F32)
        return value

    near_first = sorted(range(1, outer))
    far_first = near_first[::-1]

    def sum_outer(products):
        if not relay:
            return [over_outer(products[k].astype(BF16), k) for k in far_first]
        far = products[3].astype(BF16)
        carried = outer_pairs(far, [(0, 1), (3, 2)])
        middle = outer_pairs(far, [(1, 2), (2, 1)])
        two = over_outer((products[2] + carried.astype(F32)).astype(BF16), 2)
        one = over_outer(after(products[1].astype(BF16), carried), 1)
        return [middle, one, two]

    def shards(tokens, slots, gate_probs, w_gate, w_up, d_hidden):
        dp = lax.axis_index("dp")
        etp = lax.axis_index("etp")
        a, b = dp // inner, dp % inner
        depth, width = w_gate.shape
        cap = slots.shape[0]
        tok = tokens.shape[0]
        span = depth * inner

        onehot = (slots[:, None] == jnp.arange(tok, dtype=slots.dtype)[None, :]).astype(BF16)
        rows = jnp.dot(onehot, tokens, preferred_element_type=F32).astype(BF16)
        pieces = {}
        for k in far_first + [0]:
            pieces[k] = jnp.concatenate(
                [
                    lax.dynamic_slice(rows, (0, (a ^ k) * span + (b ^ j) * depth), (cap, depth))
                    for j in range(inner)
                ],
                axis=1,
            )
        got = {k: over_outer(pieces[k], k) for k in far_first}

        weights = [jnp.concatenate([w_gate, w_up], axis=1)]
        for j in range(1, inner):
            sent = [over_inner(after(w, rows), j) for w in (w_gate, w_up)]
            weights.append(jnp.concatenate(sent, axis=1))
        weights = jnp.concatenate(weights, axis=0)

        x_chunks = {}
        last = got[far_first[0]]
        for k in far_first:
            x_chunks[k] = gather_etp(after(got[k], last))
            last = got[k]
        x_chunks[0] = gather_etp(after(pieces[0], got[1] if outer > 1 else pieces[0]))
        probs = gather_etp(after(gate_probs, x_chunks[0]))

        products = {
            k: jnp.dot(x_chunks[k], weights, preferred_element_type=F32) for k in far_first + [0]
        }
        parts = sum_outer(products)

        x_other = {
            (k, j): over_inner(x_chunks[k][:, j * depth : (j + 1) * depth], j)
            for k in far_first + [0]
            for j in range(1, inner)
        }
        probs = after(probs, *x_other.values())
        order = etp ^ jnp.array(chunk_order, jnp.int32)
        hidden, paired = gate_call(order, products[0], probs[:, None], d_hidden, parts)

        keys = [0] + near_first
        grads = {0: paired}
        if relay:
            grads[2] = over_outer(paired, 2)
            grads[1] = over_outer(paired, 1)
        else:
            for k in near_first:
                grads[k] = over_outer(paired, k)
        grads_other = {}
        partials = {}

        def advance(k, last):
            for j in range(1, inner):
                grads_other[k, j] = over_inner(grads[k], j)
            partials[k] = lax.dot_general(
                after(grads[k], last), weights, (((1,), (1,)), ((), ())), preferred_element_type=F32
            )
            return partials[k]

        last = grads[near_first[0]] if outer > 1 else paired
        for k in keys:
            if relay and k == 2:
                turn = after(grads[2], last)
                ends = outer_pairs(turn, [(2, 3), (1, 0)])
                middle = outer_pairs(after(paired, turn), [(1, 2), (2, 1)])
                last = grads_other[1, 1] if inner > 1 else last
                grads[3] = middle + ends
            last = advance(k, last)

        wide = depth % 128 == 0
        grad_tokens = None
        dx = jnp.zeros((cap, outer * span), BF16)
        for k in keys:
            own = reduce_etp(partials[k]).astype(BF16)
            own = over_outer(own, k) if k else own
            if wide:
                place = dp ^ (k * inner + jnp.arange(inner, dtype=jnp.int32))
                grad_tokens = place_call(place, slots, own, tok, outer * span, grad_tokens)
            else:
                for j in range(inner):
                    block = own[:, j * depth : (j + 1) * depth]
                    dx = lax.dynamic_update_slice(dx, block, (0, (a ^ k) * span + (b ^ j) * depth))
        if not wide:
            grad_tokens = lax.dot_general(
                onehot, dx, (((0,), (0,)), ((), ())), preferred_element_type=F32
            ).astype(BF16)

        gate_total = up_total = jnp.zeros((), F32)
        for k in keys:
            for j in range(inner):
                x_part = x_other[k, j] if j else x_chunks[k][:, :depth]
                grad_part = grads_other[k, j] if j else grads[k]
                product = lax.dot_general(
                    x_part, grad_part, (((0,), (0,)), ((), ())), preferred_element_type=F32
                )
                gate_total = gate_total + product[:, :width]
                up_total = up_total + product[:, width:]
        return (hidden, grad_tokens, gate_total, up_total)

    return shards


def solution(mesh):
    in_specs = (
        P(("dp", "etp"), None),
        P(("dp", "etp")),
        P(("dp", "etp")),
        P("dp", "etp"),
        P("dp", "etp"),
        P("dp", "etp"),
    )
    out_specs = (P("dp", "etp"), P(("dp", "etp"), None), P("dp", "etp"), P("dp", "etp"))
    shards = make_shards(mesh.shape["dp"], mesh.shape["etp"])
    return jax.shard_map(shards, mesh=mesh, in_specs=in_specs, out_specs=out_specs, check_vma=False)
```

```python
import functools

import jax
import jax.numpy as jnp
from jax import lax
from jax.experimental import pallas as pl
from jax.experimental.pallas import tpu as pltpu
from jax.sharding import PartitionSpec as P

F32 = jnp.float32
BF16 = jnp.bfloat16
HALVES = 2
VMEM = pl.BlockSpec(memory_space=pltpu.VMEM)
SMEM = pl.BlockSpec(memory_space=pltpu.SMEM)
PARAMS = pltpu.CompilerParams(vmem_limit_bytes=40 * 2**20)


def split_dp(dp):
    outer = 1
    while 4 * outer * outer <= 2 * dp:
        outer *= 2
    return outer, dp // outer


def after(value, *others):
    return lax.optimization_barrier((value,) + others)[0]


def shape(rows, columns, kind):
    return jax.ShapeDtypeStruct((rows, columns), kind)


def cost(flops, size):
    return pl.CostEstimate(flops=flops, bytes_accessed=size, transcendentals=0)


def forward_kernel(parts, outer, n, *refs):
    x_refs, w_refs = refs[:parts], refs[parts : -outer - 1]
    out_refs, keep_ref = refs[-outer - 1 : -1], refs[-1]
    etp = 0
    for x_ref in x_refs:
        for first in range(0, x_ref.shape[0], outer * n):
            x = x_ref[first : first + outer * n, :]
            total, start = None, 0
            for w_ref in w_refs:
                stop = start + w_ref.shape[0]
                product = jnp.dot(x[:, start:stop], w_ref[...], preferred_element_type=F32)
                total = product if total is None else total + product
                start = stop
            for k in range(outer):
                rows = slice(k * n, (k + 1) * n)
                out_refs[k][etp * n : (etp + 1) * n, :] = total[rows].astype(out_refs[k].dtype)
                at = (k * keep_ref.shape[0] // outer) + etp * n
                keep_ref[at : at + n, :] = x[rows]
            etp += 1


def forward_call(x_parts, w_parts, outer):
    rows = sum(x.shape[0] for x in x_parts)
    span, columns = x_parts[0].shape[1], w_parts[0].shape[1]
    n = x_parts[0].shape[0] // outer
    each = rows // outer
    kinds = [F32] + [BF16] * (outer - 1)
    return pl.pallas_call(
        functools.partial(forward_kernel, len(x_parts), outer, n),
        out_shape=[shape(each, columns, kind) for kind in kinds] + [shape(rows, span, BF16)],
        in_specs=[VMEM] * (len(x_parts) + len(w_parts)),
        out_specs=[VMEM] * (outer + 1),
        compiler_params=PARAMS,
        cost_estimate=cost(2 * rows * span * columns, 2 * (2 * rows * span + span * columns)),
    )(*x_parts, *w_parts)


def gate_kernel(steps, half, order_ref, pre_ref, prob_ref, cot_ref, *refs):
    part_refs, (hidden_ref, grad_ref) = refs[:-2], refs[-2:]
    if half:
        hidden_ref[...] = part_refs[0][...]
        part_refs = part_refs[1:]
    rows, width = cot_ref.shape
    cap = rows // steps
    n = cap // HALVES
    for i in range(steps):
        here = slice(i * n, (i + 1) * n)
        there = pl.ds(pl.multiple_of(order_ref[i] * cap + half * n, n), n)
        total = pre_ref[here, :]
        for part_ref in part_refs:
            total = total + part_ref[here, :].astype(F32)
        gate, up = total[:, :width], total[:, width:]
        prob = prob_ref[i * cap + half * n : i * cap + (half + 1) * n, :].astype(F32)
        sig = jax.nn.sigmoid(gate)
        act = gate * sig
        hidden_ref[there, :] = (prob * act * up).astype(BF16)
        scaled = cot_ref[there, :].astype(F32) * prob
        grad_ref[here, :width] = (scaled * up * sig * (1.0 + gate * (1.0 - sig))).astype(BF16)
        grad_ref[here, width:] = (scaled * act).astype(BF16)


def gate_call(half, order, pre, prob, cotangent, before, parts):
    rows, width = cotangent.shape
    operands = [pre, prob, cotangent] + ([before] if half else []) + parts
    return pl.pallas_call(
        functools.partial(gate_kernel, order.shape[0], half),
        out_shape=(shape(rows, width, BF16), shape(pre.shape[0], 2 * width, BF16)),
        in_specs=[SMEM] + [VMEM] * len(operands),
        out_specs=(VMEM, VMEM),
        compiler_params=PARAMS,
        cost_estimate=cost(20 * rows * width, rows * width * 8),
    )(order, *operands)


def backward_kernel(outer, steps, n, *refs):
    grad_refs, w_refs = refs[:outer], refs[outer : -steps // 2 - 2]
    keep_refs, (send_ref, all_ref) = refs[-steps // 2 - 2 : -2], refs[-2:]
    each = steps * n
    contract = (((1,), (1,)), ((), ()))
    for k in range(outer):
        grad = grad_refs[k][...]
        all_ref[k * each : (k + 1) * each, :] = grad
        start = 0
        for w_ref in w_refs:
            stop = start + w_ref.shape[0]
            product = lax.dot_general(grad, w_ref[...], contract, preferred_element_type=F32)
            for i in range(steps):
                part = product[i * n : (i + 1) * n]
                if i < steps // 2:
                    keep_refs[i][k * n : (k + 1) * n, start:stop] = part
                else:
                    at = ((i - steps // 2) * outer + k) * n
                    send_ref[at : at + n, start:stop] = part.astype(BF16)
            start = stop


def backward_call(grads, w_parts, steps):
    outer = len(grads)
    n = grads[0].shape[0] // steps
    rows, columns = outer * grads[0].shape[0], grads[0].shape[1]
    span = sum(w.shape[0] for w in w_parts)
    return pl.pallas_call(
        functools.partial(backward_kernel, outer, steps, n),
        out_shape=[shape(outer * n, span, F32)] * (steps // 2)
        + [shape(rows // 2, span, BF16), shape(rows, columns, BF16)],
        in_specs=[VMEM] * (outer + len(w_parts)),
        out_specs=[VMEM] * (steps // 2 + 2),
        compiler_params=PARAMS,
        cost_estimate=cost(2 * rows * span * columns, 2 * (2 * rows * span + span * columns)),
    )(*grads, *w_parts)


def place_kernel(outer, inner, place_ref, slots_ref, *refs):
    out_ref = refs[-1]
    depth = out_ref.shape[1]
    rows = lax.broadcasted_iota(jnp.int32, (out_ref.shape[0], slots_ref.shape[1]), 0)
    onehot = (rows == slots_ref[...]).astype(BF16)
    for i in range(outer * inner):
        k, j = i // inner, i % inner

        @pl.when(pl.program_id(0) == i)
        def _():
            columns = slice(j * depth, (j + 1) * depth)
            halves = [refs[k * HALVES + h][:, columns] for h in range(HALVES)]
            block = jnp.concatenate(halves, axis=0)
            out_ref[...] = jnp.dot(onehot, block, preferred_element_type=F32).astype(BF16)


def place_call(place, slots, chunks, tok, outer, inner):
    span = chunks[0].shape[1]
    depth = span // inner
    whole = lambda array: pl.BlockSpec(array.shape, lambda i, place: (0, 0))
    slots = slots[None, :]
    return pl.pallas_call(
        functools.partial(place_kernel, outer, inner),
        out_shape=shape(tok, outer * span, BF16),
        grid_spec=pltpu.PrefetchScalarGridSpec(
            num_scalar_prefetch=1,
            grid=(outer * inner,),
            in_specs=[whole(slots)] + [whole(c) for c in chunks],
            out_specs=pl.BlockSpec((tok, depth), lambda i, place: (0, place[i])),
        ),
        compiler_params=PARAMS,
        cost_estimate=cost(2 * tok * slots.shape[1] * outer * span, 2 * tok * outer * span),
    )(place, slots, *chunks)


def make_shards(dp_size, etp_size):
    outer, inner = split_dp(dp_size)

    def over_outer(value, k):
        pairs = [(i, i ^ (k * inner)) for i in range(dp_size)]
        return lax.ppermute(value, "dp", pairs)

    def over_inner(value, j):
        pairs = [(i, i ^ j) for i in range(dp_size)]
        return lax.ppermute(value, "dp", pairs)

    def over_etp(value, e):
        pairs = [(i, i ^ e) for i in range(etp_size)]
        return lax.ppermute(value, "etp", pairs)

    part_order = [0]
    bit = etp_size // 2
    bits = []
    while bit:
        bits.append(bit)
        part_order = part_order + [c ^ bit for c in part_order]
        bit //= 2

    def gather_etp(value, order=None):
        pieces = [value]
        for i, b in enumerate(bits):
            joined = jnp.concatenate(pieces, axis=0) if len(pieces) > 1 else pieces[0]
            if order:
                joined = after(joined, order[i + 1])
            pieces = pieces + [over_etp(joined, b)]
        return pieces

    def reduce_etp(keep, sent):
        for b in reversed(bits):
            got = over_etp(sent, b)
            n = keep[0].shape[0]
            keep = [own + got[i * n : (i + 1) * n].astype(F32) for i, own in enumerate(keep)]
            half = len(keep) // 2
            if half:
                sent = jnp.concatenate([v.astype(BF16) for v in keep[half:]], axis=0)
                keep = keep[:half]
        return keep[0].astype(BF16)

    near_first = sorted(range(1, outer))
    far_first = near_first[::-1]
    keys = [0] + near_first
    halves = range(HALVES)

    def shards(tokens, slots, gate_probs, w_gate, w_up, d_hidden):
        dp = lax.axis_index("dp")
        etp = lax.axis_index("etp")
        a, b = dp // inner, dp % inner
        depth, width = w_gate.shape
        cap = slots.shape[0]
        n = cap // HALVES
        tok = tokens.shape[0]
        span = depth * inner
        wide = depth % 128 == 0

        onehot = (slots[:, None] == jnp.arange(tok, dtype=slots.dtype)[None, :]).astype(BF16)
        rows = jnp.dot(onehot, tokens, preferred_element_type=F32).astype(BF16)
        pieces = {}
        for h in halves:
            for k in keys:
                blocks = [
                    lax.dynamic_slice(rows, (h * n, (a ^ k) * span + (b ^ j) * depth), (n, depth))
                    for j in range(inner)
                ]
                pieces[h, k] = jnp.concatenate(blocks, axis=1)

        w_own = jnp.concatenate([w_gate, w_up], axis=1)
        w_parts = [w_own] + [over_inner(after(w_own, rows), j) for j in range(1, inner)]
        if not wide:
            w_parts = [jnp.concatenate(w_parts, axis=0)]

        x_parts = []
        for h in halves:
            got = {k: over_outer(pieces[h, k], k) for k in far_first}
            mine = jnp.concatenate([pieces[h, 0]] + [got[k] for k in near_first], axis=0)
            x_parts.append(gather_etp(mine, x_parts[0] if h else None))
        probs = jnp.concatenate(gather_etp(after(gate_probs, x_parts[0][-1])), axis=0)[:, None]
        order = etp ^ jnp.array(part_order, jnp.int32)

        kept, grads, hidden = [], [], None
        products = []
        for h in halves:
            if h:
                x_parts[h][0] = after(x_parts[h][0], products[0][0])
            *product, x_all = forward_call(x_parts[h], w_parts, outer)
            kept.append(x_all)
            parts = [over_outer(product[k], k) for k in far_first]
            products.append((product[0], parts))
        probs = after(probs, products[1][0])
        for h in halves:
            if h and outer > 1:
                probs = after(probs, grads[0][1])
            hidden, paired = gate_call(h, order, products[h][0], probs, d_hidden, hidden, products[h][1])
            grads.append([over_outer(paired, k) if k else paired for k in keys])

        chunks = [None] * (outer * HALVES)
        totals = [None] * inner
        for h in halves:
            grads[h][0] = after(grads[h][0], own if h else grads[1][0])
            *keep, sent, grad_all = backward_call(grads[h], w_parts, etp_size)
            own = reduce_etp(keep, sent)
            for k in far_first + [0]:
                block = own[k * n : (k + 1) * n]
                chunks[k * HALVES + h] = over_outer(block, k) if k else block
            for j in reversed(range(inner)):
                product = lax.dot_general(
                    kept[h][:, j * depth : (j + 1) * depth],
                    grad_all,
                    (((0,), (0,)), ((), ())),
                    preferred_element_type=F32,
                )
                totals[j] = product if h == 0 else totals[j] + product
        total = totals[0]
        for j in range(1, inner):
            total = total + over_inner(totals[j].astype(BF16), j).astype(F32)

        if wide:
            place = dp ^ jnp.arange(outer * inner, dtype=jnp.int32)
            grad_tokens = place_call(place, slots, chunks, tok, outer, inner)
        else:
            dx = jnp.zeros((cap, outer * span), BF16)
            for k in keys:
                chunk = jnp.concatenate(chunks[k * HALVES : (k + 1) * HALVES], axis=0)
                for j in range(inner):
                    block = chunk[:, j * depth : (j + 1) * depth]
                    dx = lax.dynamic_update_slice(dx, block, (0, (a ^ k) * span + (b ^ j) * depth))
            grad_tokens = lax.dot_general(
                onehot, dx, (((0,), (0,)), ((), ())), preferred_element_type=F32
            ).astype(BF16)
        return (hidden, grad_tokens, total[:, :width], total[:, width:])

    return shards


def solution(mesh):
    in_specs = (
        P(("dp", "etp"), None),
        P(("dp", "etp")),
        P(("dp", "etp")),
        P("dp", "etp"),
        P("dp", "etp"),
        P("dp", "etp"),
    )
    out_specs = (P("dp", "etp"), P(("dp", "etp"), None), P("dp", "etp"), P("dp", "etp"))
    shards = make_shards(mesh.shape["dp"], mesh.shape["etp"])
    return jax.shard_map(shards, mesh=mesh, in_specs=in_specs, out_specs=out_specs, check_vma=False)
```

```python
import functools

import jax
import jax.numpy as jnp
from jax import lax
from jax.experimental import pallas as pl
from jax.experimental.pallas import tpu as pltpu
from jax.sharding import PartitionSpec as P

F32 = jnp.float32
BF16 = jnp.bfloat16


def split_dp(dp):
    outer = 1
    while 4 * outer * outer <= 2 * dp:
        outer *= 2
    return outer, dp // outer


def after(value, *others):
    return lax.optimization_barrier((value,) + others)[0]


def gate_kernel(steps, order_ref, pre_ref, prob_ref, cot_ref, *refs):
    part_refs, (hidden_ref, grad_ref) = refs[:-2], refs[-2:]
    rows, width = cot_ref.shape
    cap = rows // steps
    for i in range(steps):
        here = pl.ds(i * cap, cap)
        there = pl.ds(pl.multiple_of(order_ref[i] * cap, cap), cap)
        total = pre_ref[here, :]
        for part_ref in part_refs:
            total = total + part_ref[here, :].astype(F32)
        gate, up = total[:, :width], total[:, width:]
        prob = prob_ref[here, :].astype(F32)
        sig = jax.nn.sigmoid(gate)
        act = gate * sig
        hidden_ref[there, :] = (prob * act * up).astype(BF16)
        scaled = cot_ref[there, :].astype(F32) * prob
        grad_ref[here, :width] = (scaled * up * sig * (1.0 + gate * (1.0 - sig))).astype(BF16)
        grad_ref[here, width:] = (scaled * act).astype(BF16)


def gate_call(order, pre, prob, cotangent, parts):
    rows, width = cotangent.shape
    steps = order.shape[0]
    vmem = pl.BlockSpec(memory_space=pltpu.VMEM)
    return pl.pallas_call(
        functools.partial(gate_kernel, steps),
        out_shape=(
            jax.ShapeDtypeStruct((rows, width), BF16),
            jax.ShapeDtypeStruct((rows, 2 * width), BF16),
        ),
        in_specs=[pl.BlockSpec(memory_space=pltpu.SMEM)] + [vmem] * (3 + len(parts)),
        out_specs=(vmem, vmem),
        compiler_params=pltpu.CompilerParams(vmem_limit_bytes=24 * 2**20),
        cost_estimate=pl.CostEstimate(
            flops=20 * rows * width, bytes_accessed=rows * width * 30, transcendentals=rows * width
        ),
    )(order, pre, prob, cotangent, *parts)


def make_shards(dp_size, etp_size):
    outer, inner = split_dp(dp_size)

    def over_outer(value, k):
        pairs = [(i, i ^ (k * inner)) for i in range(dp_size)]
        return lax.ppermute(value, "dp", pairs)

    def over_inner(value, j):
        pairs = [(i, i ^ j) for i in range(dp_size)]
        return lax.ppermute(value, "dp", pairs)

    def over_etp(value, e):
        pairs = [(i, i ^ e) for i in range(etp_size)]
        return lax.ppermute(value, "etp", pairs)

    chunk_order = [0]
    bit = etp_size // 2
    bits = []
    while bit:
        bits.append(bit)
        chunk_order = chunk_order + [c ^ bit for c in chunk_order]
        bit //= 2

    def gather_etp(value):
        for b in bits:
            value = jnp.concatenate([value, over_etp(value, b)], axis=0)
        return value

    def reduce_etp(value):
        for b in reversed(bits):
            half = value.shape[0] // 2
            sent = over_etp(value[half:].astype(BF16), b)
            value = value[:half] + sent.astype(F32)
        return value

    far_first = sorted(range(1, outer), key=lambda k: -k)
    near_first = sorted(range(1, outer))
    keys = [0] + near_first
    outer_groups = [[i * inner + j for i in range(outer)] for j in range(inner)]
    inner_groups = [[i * inner + j for j in range(inner)] for i in range(outer)]

    def shards(tokens, slots, gate_probs, w_gate, w_up, d_hidden):
        dp = lax.axis_index("dp")
        etp = lax.axis_index("etp")
        a, b = dp // inner, dp % inner
        depth, width = w_gate.shape
        cap = slots.shape[0]
        tok = tokens.shape[0]
        span = depth * inner
        each = cap * etp_size

        weights = jnp.concatenate([w_gate, w_up], axis=1)
        if inner > 1:
            weights = lax.all_gather(weights, "dp", axis_index_groups=inner_groups, axis=0, tiled=True)

        onehot = (slots[:, None] == jnp.arange(tok, dtype=slots.dtype)[None, :]).astype(BF16)
        rows = jnp.dot(onehot, tokens, preferred_element_type=F32).astype(BF16)
        pieces = {k: lax.dynamic_slice(rows, (0, (a ^ k) * span), (cap, span)) for k in far_first + [0]}
        got = {k: over_outer(pieces[k], k) for k in far_first}
        x_chunks = {k: gather_etp(got[k]) for k in far_first}
        x_chunks[0] = gather_etp(after(pieces[0], got[near_first[0]]))
        probs = gather_etp(after(gate_probs, x_chunks[0]))

        parts = {
            k: over_outer(jnp.dot(x_chunks[k], weights, preferred_element_type=F32).astype(BF16), k)
            for k in far_first
        }
        pre = jnp.dot(x_chunks[0], weights, preferred_element_type=F32)
        order = etp ^ jnp.array(chunk_order, jnp.int32)
        x_all = jnp.zeros((outer * each, span), BF16)
        for k in keys:
            x_all = lax.dynamic_update_slice(x_all, x_chunks[k], ((a ^ k) * each, 0))
        hidden, paired = gate_call(
            order, pre, after(probs, x_all)[:, None], d_hidden, [parts[k] for k in near_first]
        )
        grads = lax.all_gather(paired, "dp", axis_index_groups=outer_groups, axis=0, tiled=True)

        def weight_grad(j):
            x_part = lax.dynamic_slice(x_all, (0, (b ^ j) * depth), (outer * each, depth))
            return lax.dot_general(
                x_part, grads, (((0,), (0,)), ((), ())), preferred_element_type=F32
            )

        leaving = [weight_grad(j).astype(BF16) for j in range(1, inner)]
        arriving = [over_inner(leaving[j - 1], j) for j in range(1, inner)]

        dx = jnp.zeros((cap, outer * span), BF16)
        last = leaving[0] if inner > 1 else grads
        for k in far_first + [0]:
            block = lax.dynamic_slice(after(grads, last), ((a ^ k) * each, 0), (each, 2 * width))
            partial = lax.dot_general(
                block, weights, (((1,), (1,)), ((), ())), preferred_element_type=F32
            )
            last = partial
            own = reduce_etp(partial).astype(BF16)
            own = over_outer(own, k) if k else own
            dx = lax.dynamic_update_slice(dx, own, (0, (a ^ k) * span))
        grad_tokens = lax.dot_general(
            onehot, dx, (((0,), (0,)), ((), ())), preferred_element_type=F32
        ).astype(BF16)
        total = after(weight_grad(0), last)
        gate_total, up_total = total[:, :width], total[:, width:]
        for part in arriving:
            gate_total = gate_total + part[:, :width].astype(F32)
            up_total = up_total + part[:, width:].astype(F32)
        return (hidden, grad_tokens, gate_total, up_total)

    return shards


def solution(mesh):
    in_specs = (
        P(("dp", "etp"), None),
        P(("dp", "etp")),
        P(("dp", "etp")),
        P("dp", "etp"),
        P("dp", "etp"),
        P("dp", "etp"),
    )
    out_specs = (P("dp", "etp"), P(("dp", "etp"), None), P("dp", "etp"), P("dp", "etp"))
    shards = make_shards(mesh.shape["dp"], mesh.shape["etp"])
    return jax.shard_map(shards, mesh=mesh, in_specs=in_specs, out_specs=out_specs, check_vma=False)
```

```python
import functools

import jax
import jax.numpy as jnp
from jax import lax
from jax.experimental import pallas as pl
from jax.experimental.pallas import tpu as pltpu
from jax.sharding import PartitionSpec as P

F32 = jnp.float32
BF16 = jnp.bfloat16


def split_dp(dp):
    outer = 1
    while 4 * outer * outer <= 2 * dp:
        outer *= 2
    return outer, dp // outer


def after(value, *others):
    return lax.optimization_barrier((value,) + others)[0]


def gate_kernel(steps, order_ref, pre_ref, prob_ref, cot_ref, *refs):
    part_refs, (hidden_ref, grad_ref) = refs[:-2], refs[-2:]
    rows, width = cot_ref.shape
    cap = rows // steps
    for i in range(steps):
        here = pl.ds(i * cap, cap)
        there = pl.ds(pl.multiple_of(order_ref[i] * cap, cap), cap)
        total = pre_ref[here, :]
        for part_ref in part_refs:
            total = total + part_ref[here, :].astype(F32)
        gate, up = total[:, :width], total[:, width:]
        prob = prob_ref[here, :].astype(F32)
        sig = jax.nn.sigmoid(gate)
        act = gate * sig
        hidden_ref[there, :] = (prob * act * up).astype(BF16)
        scaled = cot_ref[there, :].astype(F32) * prob
        grad_ref[here, :width] = (scaled * up * sig * (1.0 + gate * (1.0 - sig))).astype(BF16)
        grad_ref[here, width:] = (scaled * act).astype(BF16)


def gate_call(order, pre, prob, cotangent, parts):
    rows, width = cotangent.shape
    steps = order.shape[0]
    vmem = pl.BlockSpec(memory_space=pltpu.VMEM)
    return pl.pallas_call(
        functools.partial(gate_kernel, steps),
        out_shape=(
            jax.ShapeDtypeStruct((rows, width), BF16),
            jax.ShapeDtypeStruct((rows, 2 * width), BF16),
        ),
        in_specs=[pl.BlockSpec(memory_space=pltpu.SMEM)] + [vmem] * (3 + len(parts)),
        out_specs=(vmem, vmem),
        compiler_params=pltpu.CompilerParams(vmem_limit_bytes=24 * 2**20),
        cost_estimate=pl.CostEstimate(
            flops=20 * rows * width, bytes_accessed=rows * width * 30, transcendentals=rows * width
        ),
    )(order, pre, prob, cotangent, *parts)


def make_shards(dp_size, etp_size):
    outer, inner = split_dp(dp_size)

    def over_outer(value, k):
        pairs = [(i, i ^ (k * inner)) for i in range(dp_size)]
        return lax.ppermute(value, "dp", pairs)

    def over_inner(value, j):
        pairs = [(i, i ^ j) for i in range(dp_size)]
        return lax.ppermute(value, "dp", pairs)

    def over_etp(value, e):
        pairs = [(i, i ^ e) for i in range(etp_size)]
        return lax.ppermute(value, "etp", pairs)

    chunk_order = [0]
    bit = etp_size // 2
    bits = []
    while bit:
        bits.append(bit)
        chunk_order = chunk_order + [c ^ bit for c in chunk_order]
        bit //= 2

    def gather_etp(value):
        for b in bits:
            value = jnp.concatenate([value, over_etp(value, b)], axis=0)
        return value

    def reduce_etp(value):
        for b in reversed(bits):
            half = value.shape[0] // 2
            sent = over_etp(value[half:].astype(BF16), b)
            value = value[:half] + sent.astype(F32)
        return value

    near_first = sorted(range(1, outer))
    far_first = near_first[::-1]
    keys = [0] + near_first
    relay = outer == 4

    def outer_pairs(value, pairs):
        pairs = [(s * inner + i, t * inner + i) for s, t in pairs for i in range(inner)]
        return lax.ppermute(value, "dp", pairs)

    def shards(tokens, slots, gate_probs, w_gate, w_up, d_hidden):
        dp = lax.axis_index("dp")
        etp = lax.axis_index("etp")
        a, b = dp // inner, dp % inner
        depth, width = w_gate.shape
        cap = slots.shape[0]
        tok = tokens.shape[0]
        span = depth * inner

        weights = [jnp.concatenate([w_gate, w_up], axis=1)]
        for j in range(1, inner):
            weights.append(jnp.concatenate([over_inner(w_gate, j), over_inner(w_up, j)], axis=1))
        weights = jnp.concatenate(weights, axis=0)

        onehot = (slots[:, None] == jnp.arange(tok, dtype=slots.dtype)[None, :]).astype(BF16)
        rows = jnp.dot(onehot, tokens, preferred_element_type=F32).astype(BF16)
        pieces = {}
        for k in keys:
            blocks = [
                lax.dynamic_slice(rows, (0, (a ^ k) * span + (b ^ j) * depth), (cap, depth))
                for j in range(inner)
            ]
            pieces[k] = jnp.concatenate(blocks, axis=1)
        got = {}
        for k in far_first:
            got[k] = over_outer(after(pieces[k], got[3]) if relay and k == 1 else pieces[k], k)
        got[0] = pieces[0]

        x_chunks, products, last = {}, {}, rows
        for k in far_first + [0]:
            x_chunks[k] = gather_etp(after(got[k], last))
            product = jnp.dot(x_chunks[k], weights, preferred_element_type=F32)
            products[k] = last = product.astype(BF16) if k and not (relay and k == 2) else product
            if relay and k == 3:
                carried = outer_pairs(products[3], [(0, 1), (3, 2)])
                middle = outer_pairs(products[3], [(1, 2), (2, 1)])
            if relay and k == 2:
                last = after(products[2], carried, middle)
        if relay:
            two = over_outer((products[2] + carried.astype(F32)).astype(BF16), 2)
            one = over_outer(after(products[1], carried), 1)
            parts = [middle, one, two]
        else:
            parts = [over_outer(products[k], k) for k in far_first]
        probs = gather_etp(after(gate_probs, products[0]))
        order = etp ^ jnp.array(chunk_order, jnp.int32)
        hidden, paired = gate_call(order, products[0], probs[:, None], d_hidden, parts)

        grads = {0: paired}
        if relay:
            grads[2] = over_outer(paired, 2)
            grads[1] = over_outer(paired, 1)
        else:
            for k in near_first:
                grads[k] = over_outer(paired, k)
        sums, partials = {}, {}

        def advance(k, last):
            partials[k] = lax.dot_general(
                after(grads[k], last), weights, (((1,), (1,)), ((), ())), preferred_element_type=F32
            )
            sums[k] = reduce_etp(partials[k]).astype(BF16)
            return partials[k]

        def weight_grad(ks, j, last):
            x_part = jnp.concatenate([x_chunks[k][:, j * depth : (j + 1) * depth] for k in ks], axis=0)
            grad_part = jnp.concatenate([grads[k] for k in ks], axis=0)
            return lax.dot_general(
                x_part, after(grad_part, last), (((0,), (0,)), ((), ())), preferred_element_type=F32
            )

        early, late = keys[: max(outer - 1, 1)], keys[max(outer - 1, 1) :]
        last = grads[near_first[0]] if outer > 1 else paired
        for k in [0] + near_first[:1]:
            last = advance(k, last)
        if relay:
            turn = after(grads[2], last)
            ends = outer_pairs(turn, [(2, 3), (1, 0)])
            middle = outer_pairs(after(paired, turn), [(1, 2), (2, 1)])
            last = sums[1]
            advance(2, last)
            last = sums[2]
            early_sums = [weight_grad(early, j, last) for j in range(1, inner)]
            grads[3] = middle + after(ends, *early_sums)
        else:
            for k in early[2:]:
                last = advance(k, last)
            early_sums = [weight_grad(early, j, last) for j in range(1, inner)]

        leaving = [
            ((early_sums[j - 1] + weight_grad(late, j, grads[late[-1]])) if late else early_sums[j - 1])
            for j in range(1, inner)
        ]
        leaving = [v.astype(BF16) for v in leaving]
        arriving = [over_inner(leaving[j - 1], j) for j in range(1, inner)]
        last = leaving[0] if inner > 1 else last
        for k in late:
            last = advance(k, last)
        total = weight_grad(keys, 0, last)
        gate_total, up_total = total[:, :width], total[:, width:]
        for part in arriving:
            gate_total = gate_total + part[:, :width].astype(F32)
            up_total = up_total + part[:, width:].astype(F32)

        dx = jnp.zeros((cap, outer * span), BF16)
        for k in keys:
            own = over_outer(sums[k], k) if k else sums[k]
            for j in range(inner):
                block = own[:, j * depth : (j + 1) * depth]
                dx = lax.dynamic_update_slice(dx, block, (0, (a ^ k) * span + (b ^ j) * depth))
        grad_tokens = lax.dot_general(
            onehot, dx, (((0,), (0,)), ((), ())), preferred_element_type=F32
        ).astype(BF16)
        return (hidden, grad_tokens, gate_total, up_total)

    return shards


def solution(mesh):
    in_specs = (
        P(("dp", "etp"), None),
        P(("dp", "etp")),
        P(("dp", "etp")),
        P("dp", "etp"),
        P("dp", "etp"),
        P("dp", "etp"),
    )
    out_specs = (P("dp", "etp"), P(("dp", "etp"), None), P("dp", "etp"), P("dp", "etp"))
    shards = make_shards(mesh.shape["dp"], mesh.shape["etp"])
    return jax.shard_map(shards, mesh=mesh, in_specs=in_specs, out_specs=out_specs, check_vma=False)
```

```python
import functools

import jax
import jax.numpy as jnp
from jax import lax
from jax.experimental import pallas as pl
from jax.experimental.pallas import tpu as pltpu
from jax.sharding import PartitionSpec as P

F32 = jnp.float32
BF16 = jnp.bfloat16


def split_dp(dp):
    outer = 1
    while 4 * outer * outer <= 2 * dp:
        outer *= 2
    return outer, dp // outer


def after(value, *others):
    return lax.optimization_barrier((value,) + others)[0]


def gate_kernel(steps, order_ref, pre_ref, prob_ref, cot_ref, *refs):
    part_refs, (hidden_ref, grad_ref) = refs[:-2], refs[-2:]
    rows, width = cot_ref.shape
    cap = rows // steps
    for i in range(steps):
        here = pl.ds(i * cap, cap)
        there = pl.ds(pl.multiple_of(order_ref[i] * cap, cap), cap)
        total = pre_ref[here, :]
        for part_ref in part_refs:
            total = total + part_ref[here, :].astype(F32)
        gate, up = total[:, :width], total[:, width:]
        prob = prob_ref[here, :].astype(F32)
        sig = jax.nn.sigmoid(gate)
        act = gate * sig
        hidden_ref[there, :] = (prob * act * up).astype(BF16)
        scaled = cot_ref[there, :].astype(F32) * prob
        grad_ref[here, :width] = (scaled * up * sig * (1.0 + gate * (1.0 - sig))).astype(BF16)
        grad_ref[here, width:] = (scaled * act).astype(BF16)


def gate_call(order, pre, prob, cotangent, parts):
    rows, width = cotangent.shape
    steps = order.shape[0]
    vmem = pl.BlockSpec(memory_space=pltpu.VMEM)
    return pl.pallas_call(
        functools.partial(gate_kernel, steps),
        out_shape=(
            jax.ShapeDtypeStruct((rows, width), BF16),
            jax.ShapeDtypeStruct((rows, 2 * width), BF16),
        ),
        in_specs=[pl.BlockSpec(memory_space=pltpu.SMEM)] + [vmem] * (3 + len(parts)),
        out_specs=(vmem, vmem),
        compiler_params=pltpu.CompilerParams(vmem_limit_bytes=24 * 2**20),
        cost_estimate=pl.CostEstimate(
            flops=20 * rows * width, bytes_accessed=rows * width * 30, transcendentals=rows * width
        ),
    )(order, pre, prob, cotangent, *parts)


def make_shards(dp_size, etp_size):
    outer, inner = split_dp(dp_size)

    def over_outer(value, k):
        pairs = [(i, i ^ (k * inner)) for i in range(dp_size)]
        return lax.ppermute(value, "dp", pairs)

    def over_inner(value, j):
        pairs = [(i, i ^ j) for i in range(dp_size)]
        return lax.ppermute(value, "dp", pairs)

    def over_etp(value, e):
        pairs = [(i, i ^ e) for i in range(etp_size)]
        return lax.ppermute(value, "etp", pairs)

    chunk_order = [0]
    bit = etp_size // 2
    bits = []
    while bit:
        bits.append(bit)
        chunk_order = chunk_order + [c ^ bit for c in chunk_order]
        bit //= 2

    def gather_etp(value):
        for b in bits:
            value = jnp.concatenate([value, over_etp(value, b)], axis=0)
        return value

    def reduce_etp(value):
        for b in reversed(bits):
            half = value.shape[0] // 2
            sent = over_etp(value[half:].astype(BF16), b)
            value = value[:half] + sent.astype(F32)
        return value

    near_first = sorted(range(1, outer))
    far_first = near_first[::-1]
    keys = [0] + near_first
    relay = outer == 4

    def outer_pairs(value, pairs):
        pairs = [(s * inner + i, t * inner + i) for s, t in pairs for i in range(inner)]
        return lax.ppermute(value, "dp", pairs)

    def shards(tokens, slots, gate_probs, w_gate, w_up, d_hidden):
        dp = lax.axis_index("dp")
        etp = lax.axis_index("etp")
        a, b = dp // inner, dp % inner
        depth, width = w_gate.shape
        cap = slots.shape[0]
        tok = tokens.shape[0]
        span = depth * inner

        weights = [jnp.concatenate([w_gate, w_up], axis=1)]
        for j in range(1, inner):
            weights.append(jnp.concatenate([over_inner(w_gate, j), over_inner(w_up, j)], axis=1))
        weights = jnp.concatenate(weights, axis=0)

        onehot = (slots[:, None] == jnp.arange(tok, dtype=slots.dtype)[None, :]).astype(BF16)
        rows = jnp.dot(onehot, tokens, preferred_element_type=F32).astype(BF16)
        pieces = {}
        for k in keys:
            blocks = [
                lax.dynamic_slice(rows, (0, (a ^ k) * span + (b ^ j) * depth), (cap, depth))
                for j in range(inner)
            ]
            pieces[k] = jnp.concatenate(blocks, axis=1)
        got = {}
        for k in far_first:
            got[k] = over_outer(pieces[k], k)
        got[0] = pieces[0]

        x_chunks, products = {}, {}

        def multiply(k, last):
            return jnp.dot(after(x_chunks[k], last), weights, preferred_element_type=F32)

        if relay:
            x_chunks[3] = gather_etp(got[3])
            far = multiply(3, rows).astype(BF16)
            carried = outer_pairs(far, [(0, 1), (3, 2)])
            middle = outer_pairs(far, [(1, 2), (2, 1)])
            x_chunks[2] = gather_etp(after(got[2], far))
            product = multiply(2, far)
            x_chunks[1] = gather_etp(after(got[1], product))
            summed = (product + carried.astype(F32)).astype(BF16)
            two = over_outer(summed, 2)
            one = over_outer(multiply(1, summed).astype(BF16), 1)
            x_chunks[0] = gather_etp(after(got[0], summed))
            own = multiply(0, summed)
            parts = [after(middle, own), one, two]
        else:
            last, parts = rows, []
            for k in far_first:
                x_chunks[k] = gather_etp(after(got[k], last))
                last = multiply(k, last).astype(BF16)
                parts.append(over_outer(last, k))
            x_chunks[0] = gather_etp(after(got[0], last))
            own = multiply(0, last)
        probs = gather_etp(after(gate_probs, own))
        order = etp ^ jnp.array(chunk_order, jnp.int32)
        hidden, paired = gate_call(order, own, probs[:, None], d_hidden, parts)

        grads = {0: paired}
        if relay:
            grads[2] = over_outer(paired, 2)
            grads[1] = over_outer(paired, 1)
        else:
            for k in near_first:
                grads[k] = over_outer(paired, k)
        sums, partials = {}, {}

        def advance(k, last):
            partials[k] = lax.dot_general(
                after(grads[k], last), weights, (((1,), (1,)), ((), ())), preferred_element_type=F32
            )
            sums[k] = reduce_etp(partials[k]).astype(BF16)
            return partials[k]

        def weight_grad(ks, j, last):
            x_part = jnp.concatenate([x_chunks[k][:, j * depth : (j + 1) * depth] for k in ks], axis=0)
            grad_part = jnp.concatenate([grads[k] for k in ks], axis=0)
            return lax.dot_general(
                x_part, after(grad_part, last), (((0,), (0,)), ((), ())), preferred_element_type=F32
            )

        early, late = keys[: max(outer - 1, 1)], keys[max(outer - 1, 1) :]
        last = grads[near_first[0]] if outer > 1 else paired
        for k in [0] + near_first[:1]:
            last = advance(k, last)
        if relay:
            turn = after(grads[2], last)
            ends = outer_pairs(turn, [(2, 3), (1, 0)])
            middle = outer_pairs(after(paired, turn), [(1, 2), (2, 1)])
            last = advance(2, last)
            early_sums = [weight_grad(early, j, last) for j in range(1, inner)]
            grads[3] = middle + after(ends, *early_sums)
        else:
            for k in early[2:]:
                last = advance(k, last)
            early_sums = [weight_grad(early, j, last) for j in range(1, inner)]

        leaving = [
            ((early_sums[j - 1] + weight_grad(late, j, grads[late[-1]])) if late else early_sums[j - 1])
            for j in range(1, inner)
        ]
        leaving = [v.astype(BF16) for v in leaving]
        arriving = [over_inner(leaving[j - 1], j) for j in range(1, inner)]
        last = leaving[0] if inner > 1 else last
        for k in late:
            last = advance(k, last)
        total = weight_grad(keys, 0, last)
        gate_total, up_total = total[:, :width], total[:, width:]
        for part in arriving:
            gate_total = gate_total + part[:, :width].astype(F32)
            up_total = up_total + part[:, width:].astype(F32)

        dx = jnp.zeros((cap, outer * span), BF16)
        for k in keys:
            own = over_outer(sums[k], k) if k else sums[k]
            for j in range(inner):
                block = own[:, j * depth : (j + 1) * depth]
                dx = lax.dynamic_update_slice(dx, block, (0, (a ^ k) * span + (b ^ j) * depth))
        grad_tokens = lax.dot_general(
            onehot, dx, (((0,), (0,)), ((), ())), preferred_element_type=F32
        ).astype(BF16)
        return (hidden, grad_tokens, gate_total, up_total)

    return shards


def solution(mesh):
    in_specs = (
        P(("dp", "etp"), None),
        P(("dp", "etp")),
        P(("dp", "etp")),
        P("dp", "etp"),
        P("dp", "etp"),
        P("dp", "etp"),
    )
    out_specs = (P("dp", "etp"), P(("dp", "etp"), None), P("dp", "etp"), P("dp", "etp"))
    shards = make_shards(mesh.shape["dp"], mesh.shape["etp"])
    return jax.shard_map(shards, mesh=mesh, in_specs=in_specs, out_specs=out_specs, check_vma=False)
```

```python
import functools

import jax
import jax.numpy as jnp
from jax import lax
from jax.experimental import pallas as pl
from jax.experimental.pallas import tpu as pltpu
from jax.sharding import PartitionSpec as P

F32 = jnp.float32
BF16 = jnp.bfloat16


def split_dp(dp):
    outer = 1
    while 4 * outer * outer <= 2 * dp:
        outer *= 2
    return outer, dp // outer


def after(value, *others):
    return lax.optimization_barrier((value,) + others)[0]


def gate_kernel(steps, order_ref, pre_ref, prob_ref, cot_ref, *refs):
    part_refs, (hidden_ref, grad_ref) = refs[:-2], refs[-2:]
    rows, width = cot_ref.shape
    cap = rows // steps
    for i in range(steps):
        here = pl.ds(i * cap, cap)
        there = pl.ds(pl.multiple_of(order_ref[i] * cap, cap), cap)
        total = pre_ref[here, :]
        for part_ref in part_refs:
            total = total + part_ref[here, :].astype(F32)
        gate, up = total[:, :width], total[:, width:]
        prob = prob_ref[here, :].astype(F32)
        sig = jax.nn.sigmoid(gate)
        act = gate * sig
        hidden_ref[there, :] = (prob * act * up).astype(BF16)
        scaled = cot_ref[there, :].astype(F32) * prob
        grad_ref[here, :width] = (scaled * up * sig * (1.0 + gate * (1.0 - sig))).astype(BF16)
        grad_ref[here, width:] = (scaled * act).astype(BF16)


def gate_call(order, pre, prob, cotangent, parts):
    rows, width = cotangent.shape
    steps = order.shape[0]
    vmem = pl.BlockSpec(memory_space=pltpu.VMEM)
    return pl.pallas_call(
        functools.partial(gate_kernel, steps),
        out_shape=(
            jax.ShapeDtypeStruct((rows, width), BF16),
            jax.ShapeDtypeStruct((rows, 2 * width), BF16),
        ),
        in_specs=[pl.BlockSpec(memory_space=pltpu.SMEM)] + [vmem] * (3 + len(parts)),
        out_specs=(vmem, vmem),
        compiler_params=pltpu.CompilerParams(vmem_limit_bytes=24 * 2**20),
        cost_estimate=pl.CostEstimate(
            flops=20 * rows * width, bytes_accessed=rows * width * 30, transcendentals=rows * width
        ),
    )(order, pre, prob, cotangent, *parts)


def make_shards(dp_size, etp_size):
    outer, inner = split_dp(dp_size)

    def over_outer(value, k):
        pairs = [(i, i ^ (k * inner)) for i in range(dp_size)]
        return lax.ppermute(value, "dp", pairs)

    def over_inner(value, j):
        pairs = [(i, i ^ j) for i in range(dp_size)]
        return lax.ppermute(value, "dp", pairs)

    def over_etp(value, e):
        pairs = [(i, i ^ e) for i in range(etp_size)]
        return lax.ppermute(value, "etp", pairs)

    chunk_order = [0]
    bit = etp_size // 2
    bits = []
    while bit:
        bits.append(bit)
        chunk_order = chunk_order + [c ^ bit for c in chunk_order]
        bit //= 2

    def gather_etp(value):
        for b in bits:
            value = jnp.concatenate([value, over_etp(value, b)], axis=0)
        return value

    def reduce_etp(value):
        for b in reversed(bits):
            half = value.shape[0] // 2
            sent = over_etp(value[half:].astype(BF16), b)
            value = value[:half] + sent.astype(F32)
        return value

    near_first = sorted(range(1, outer))
    far_first = near_first[::-1]
    keys = [0] + near_first
    relay = outer == 4

    def outer_pairs(value, pairs):
        pairs = [(s * inner + i, t * inner + i) for s, t in pairs for i in range(inner)]
        return lax.ppermute(value, "dp", pairs)

    swap = [(0, 1), (1, 0), (2, 3), (3, 2)]
    cycle = [(0, 2), (2, 3), (3, 1), (1, 0)]
    back = [(t, s) for s, t in cycle]
    middle = [(1, 2), (2, 1)]
    inward = [(0, 2), (3, 1)]
    outward = [(2, 0), (1, 3)]

    def shards(tokens, slots, gate_probs, w_gate, w_up, d_hidden):
        dp = lax.axis_index("dp")
        etp = lax.axis_index("etp")
        a, b = dp // inner, dp % inner
        at_end = (a == 0) | (a == outer - 1)
        depth, width = w_gate.shape
        cap = slots.shape[0]
        tok = tokens.shape[0]
        span = depth * inner

        def pick(first, second):
            return jnp.where(at_end, first, second)

        weights = [jnp.concatenate([w_gate, w_up], axis=1)]
        for j in range(1, inner):
            weights.append(jnp.concatenate([over_inner(w_gate, j), over_inner(w_up, j)], axis=1))
        weights = jnp.concatenate(weights, axis=0)

        onehot = (slots[:, None] == jnp.arange(tok, dtype=slots.dtype)[None, :]).astype(BF16)
        rows = jnp.dot(onehot, tokens, preferred_element_type=F32).astype(BF16)
        pieces = {}
        for k in keys:
            blocks = [
                lax.dynamic_slice(rows, (0, (a ^ k) * span + (b ^ j) * depth), (cap, depth))
                for j in range(inner)
            ]
            pieces[k] = jnp.concatenate(blocks, axis=1)
        got = {k: over_outer(pieces[k], k) for k in far_first}
        if relay:
            got[3], got[1] = pick(got[3], got[1]), pick(got[1], got[3])
        got[0] = pieces[0]

        x_chunks = {}

        def multiply(k, last):
            x_chunks[k] = gather_etp(after(got[k], last))
            return jnp.dot(x_chunks[k], weights, preferred_element_type=F32)

        if relay:
            far = multiply(3, rows).astype(BF16)
            swapped = outer_pairs(far, swap)
            near = after(multiply(1, rows).astype(BF16), far)
            crossed = outer_pairs(near, middle)
            two = after(multiply(2, near), near)
            inwards = outer_pairs(after(two.astype(BF16), near), inward)
            own = multiply(0, two)
            relayed = pick(near, (two + swapped.astype(F32)).astype(BF16))
            cycled = outer_pairs(relayed, back)
            own = own + crossed.astype(F32) + inwards.astype(F32)
            own = own + jnp.where(at_end, swapped.astype(F32), 0.0)
            parts = [cycled]
        else:
            last, parts = rows, []
            for k in far_first:
                last = multiply(k, last).astype(BF16)
                parts.append(over_outer(last, k))
            own = multiply(0, last)
        probs = gather_etp(after(gate_probs, x_chunks[0]))
        order = etp ^ jnp.array(chunk_order, jnp.int32)
        hidden, paired = gate_call(order, own, probs[:, None], d_hidden, parts)

        grads, sums = {0: paired}, {}

        def advance(k, last):
            partial = lax.dot_general(
                after(grads[k], last), weights, (((1,), (1,)), ((), ())), preferred_element_type=F32
            )
            sums[k] = reduce_etp(partial).astype(BF16)
            return partial

        def weight_grad(ks, j, last):
            x_part = jnp.concatenate([x_chunks[k][:, j * depth : (j + 1) * depth] for k in ks], axis=0)
            grad_part = jnp.concatenate([grads[k] for k in ks], axis=0)
            return lax.dot_general(
                x_part, after(grad_part, last), (((0,), (0,)), ((), ())), preferred_element_type=F32
            )

        if relay:
            cycled = outer_pairs(paired, cycle)
            last = advance(0, paired)
            crossed = outer_pairs(after(paired, last), middle)
            outwards = outer_pairs(after(paired, sums[0]), outward)
            turn = after(pick(paired, cycled), paired)
            grads[3] = outer_pairs(turn, swap)
            grads[1] = pick(after(cycled, turn), crossed)
            grads[2] = pick(outwards, after(cycled, grads[1]))
            sequence = [0, 1, 3, 2]
            last = turn
        else:
            for k in near_first:
                grads[k] = over_outer(paired, k)
            sequence = keys
            last = grads[near_first[0]] if outer > 1 else paired
        early, late = sequence[: max(outer - 1, 1)], sequence[max(outer - 1, 1) :]
        for k in early:
            last = advance(k, last) if k not in sums else last

        leaving = []
        for j in range(1, inner):
            value = weight_grad(early, j, last)
            for k in late:
                value = after(value, last) + weight_grad([k], j, value)
            leaving.append(value.astype(BF16))
        arriving = [over_inner(leaving[j - 1], j) for j in range(1, inner)]
        last = leaving[0] if inner > 1 else last
        for k in late:
            last = advance(k, last)
        total = weight_grad(sequence, 0, last)
        gate_total, up_total = total[:, :width], total[:, width:]
        for part in arriving:
            gate_total = gate_total + part[:, :width].astype(F32)
            up_total = up_total + part[:, width:].astype(F32)

        last = sums[sequence[-1]]
        if relay:
            sums[3], sums[1] = pick(sums[3], sums[1]), pick(sums[1], sums[3])
        dx = jnp.zeros((cap, outer * span), BF16)
        for k in keys:
            own = over_outer(sums[k], k) if k else sums[k]
            if k != sequence[-1]:
                own = after(own, last)
            for j in range(inner):
                block = own[:, j * depth : (j + 1) * depth]
                dx = lax.dynamic_update_slice(dx, block, (0, (a ^ k) * span + (b ^ j) * depth))
        grad_tokens = lax.dot_general(
            onehot, dx, (((0,), (0,)), ((), ())), preferred_element_type=F32
        ).astype(BF16)
        return (hidden, grad_tokens, gate_total, up_total)

    return shards


def solution(mesh):
    in_specs = (
        P(("dp", "etp"), None),
        P(("dp", "etp")),
        P(("dp", "etp")),
        P("dp", "etp"),
        P("dp", "etp"),
        P("dp", "etp"),
    )
    out_specs = (P("dp", "etp"), P(("dp", "etp"), None), P("dp", "etp"), P("dp", "etp"))
    shards = make_shards(mesh.shape["dp"], mesh.shape["etp"])
    return jax.shard_map(shards, mesh=mesh, in_specs=in_specs, out_specs=out_specs, check_vma=False)
```

```python
import functools

import jax
import jax.numpy as jnp
from jax import lax
from jax.experimental import pallas as pl
from jax.experimental.pallas import tpu as pltpu
from jax.sharding import PartitionSpec as P

F32 = jnp.float32
BF16 = jnp.bfloat16


def split_dp(dp):
    outer = 1
    while 4 * outer * outer <= 2 * dp:
        outer *= 2
    return outer, dp // outer


def after(value, *others):
    return lax.optimization_barrier((value,) + others)[0]


def gate_kernel(steps, order_ref, pre_ref, prob_ref, cot_ref, *refs):
    part_refs, (hidden_ref, grad_ref) = refs[:-2], refs[-2:]
    rows, width = cot_ref.shape
    cap = rows // steps
    for i in range(steps):
        here = pl.ds(i * cap, cap)
        there = pl.ds(pl.multiple_of(order_ref[i] * cap, cap), cap)
        total = pre_ref[here, :]
        for part_ref in part_refs:
            total = total + part_ref[here, :].astype(F32)
        gate, up = total[:, :width], total[:, width:]
        prob = prob_ref[here, :].astype(F32)
        sig = jax.nn.sigmoid(gate)
        act = gate * sig
        hidden_ref[there, :] = (prob * act * up).astype(BF16)
        scaled = cot_ref[there, :].astype(F32) * prob
        grad_ref[here, :width] = (scaled * up * sig * (1.0 + gate * (1.0 - sig))).astype(BF16)
        grad_ref[here, width:] = (scaled * act).astype(BF16)


def gate_call(order, pre, prob, cotangent, parts):
    rows, width = cotangent.shape
    steps = order.shape[0]
    vmem = pl.BlockSpec(memory_space=pltpu.VMEM)
    return pl.pallas_call(
        functools.partial(gate_kernel, steps),
        out_shape=(
            jax.ShapeDtypeStruct((rows, width), BF16),
            jax.ShapeDtypeStruct((rows, 2 * width), BF16),
        ),
        in_specs=[pl.BlockSpec(memory_space=pltpu.SMEM)] + [vmem] * (3 + len(parts)),
        out_specs=(vmem, vmem),
        compiler_params=pltpu.CompilerParams(vmem_limit_bytes=24 * 2**20),
        cost_estimate=pl.CostEstimate(
            flops=20 * rows * width, bytes_accessed=rows * width * 30, transcendentals=rows * width
        ),
    )(order, pre, prob, cotangent, *parts)


def make_shards(dp_size, etp_size):
    outer, inner = split_dp(dp_size)

    def over_outer(value, k):
        pairs = [(i, i ^ (k * inner)) for i in range(dp_size)]
        return lax.ppermute(value, "dp", pairs)

    def over_inner(value, j):
        pairs = [(i, i ^ j) for i in range(dp_size)]
        return lax.ppermute(value, "dp", pairs)

    def over_etp(value, e):
        pairs = [(i, i ^ e) for i in range(etp_size)]
        return lax.ppermute(value, "etp", pairs)

    chunk_order = [0]
    bit = etp_size // 2
    bits = []
    while bit:
        bits.append(bit)
        chunk_order = chunk_order + [c ^ bit for c in chunk_order]
        bit //= 2

    def gather_etp(value, ties=()):
        for i, b in enumerate(bits):
            value = after(value, *ties[i]) if i < len(ties) else value
            value = jnp.concatenate([value, over_etp(value, b)], axis=0)
        return value

    def reduce_etp(value):
        for b in reversed(bits):
            half = value.shape[0] // 2
            sent = over_etp(value[half:].astype(BF16), b)
            value = value[:half] + sent.astype(F32)
        return value

    near_first = sorted(range(1, outer))
    far_first = near_first[::-1]
    keys = [0] + near_first
    relay = outer == 4

    def outer_pairs(value, pairs):
        pairs = [(s * inner + i, t * inner + i) for s, t in pairs for i in range(inner)]
        return lax.ppermute(value, "dp", pairs)

    swap = [(0, 1), (1, 0), (2, 3), (3, 2)]
    cycle = [(0, 2), (2, 3), (3, 1), (1, 0)]
    back = [(t, s) for s, t in cycle]
    middle = [(1, 2), (2, 1)]
    inward = [(0, 2), (3, 1)]
    outward = [(2, 0), (1, 3)]

    def shards(tokens, slots, gate_probs, w_gate, w_up, d_hidden):
        dp = lax.axis_index("dp")
        etp = lax.axis_index("etp")
        a, b = dp // inner, dp % inner
        at_end = (a == 0) | (a == outer - 1)
        depth, width = w_gate.shape
        cap = slots.shape[0]
        tok = tokens.shape[0]
        span = depth * inner

        def pick(first, second):
            return jnp.where(at_end, first, second)

        weights = [jnp.concatenate([w_gate, w_up], axis=1)]
        weights += [over_inner(weights[0], j) for j in range(1, inner)]
        weights = jnp.concatenate(weights, axis=0)

        onehot = (slots[:, None] == jnp.arange(tok, dtype=slots.dtype)[None, :]).astype(BF16)
        rows = jnp.dot(onehot, tokens, preferred_element_type=F32).astype(BF16)
        pieces = {}
        for k in keys:
            blocks = [
                lax.dynamic_slice(rows, (0, (a ^ k) * span + (b ^ j) * depth), (cap, depth))
                for j in range(inner)
            ]
            pieces[k] = jnp.concatenate(blocks, axis=1)
        got = {k: over_outer(pieces[k], k) for k in far_first}
        if relay:
            got[3], got[1] = pick(got[3], got[1]), pick(got[1], got[3])
        got[0] = pieces[0]

        x_chunks = {}

        def multiply(k, *ties):
            x_chunks[k] = after(x_chunks[k], *ties)
            return jnp.dot(x_chunks[k], weights, preferred_element_type=F32)

        if relay:
            x_chunks[3] = gather_etp(got[3])
            x_chunks[1] = gather_etp(got[1])
            far = multiply(3).astype(BF16)
            swapped = outer_pairs(far, swap)
            near = after(multiply(1, far).astype(BF16), far)
            crossed = outer_pairs(near, middle)
            x_chunks[2] = gather_etp(got[2], [[], [near]])
            x_chunks[0] = gather_etp(got[0], [[got[2]], [near]])
            two = after(multiply(2, swapped, crossed), swapped)
            inwards = outer_pairs(two.astype(BF16), inward)
            relayed = pick(near, (after(two, swapped) + swapped.astype(F32)).astype(BF16))
            cycled = outer_pairs(relayed, back)
            own = multiply(0, relayed) + crossed.astype(F32) + inwards.astype(F32)
            own = own + jnp.where(at_end, swapped.astype(F32), 0.0)
            parts = [cycled]
            last = relayed
        else:
            last, parts = rows, []
            x_chunks[0] = gather_etp(got[0])
            for k in far_first:
                x_chunks[k] = gather_etp(got[k], [[last]])
                last = multiply(k).astype(BF16)
                parts.append(over_outer(last, k))
            own = multiply(0, last)
        probs = gather_etp(after(gate_probs, last))
        order = etp ^ jnp.array(chunk_order, jnp.int32)
        hidden, paired = gate_call(order, own, probs[:, None], d_hidden, parts)

        grads, sums = {0: paired}, {}

        def advance(k, last):
            partial = lax.dot_general(
                after(grads[k], last), weights, (((1,), (1,)), ((), ())), preferred_element_type=F32
            )
            sums[k] = reduce_etp(partial).astype(BF16)
            return partial

        def weight_grad(ks, j, last):
            x_part = jnp.concatenate([x_chunks[k][:, j * depth : (j + 1) * depth] for k in ks], axis=0)
            grad_part = jnp.concatenate([grads[k] for k in ks], axis=0)
            return lax.dot_general(
                x_part, after(grad_part, last), (((0,), (0,)), ((), ())), preferred_element_type=F32
            )

        if relay:
            cycled = outer_pairs(paired, cycle)
            last = advance(0, paired)
            crossed = outer_pairs(after(paired, last), middle)
            outwards = outer_pairs(after(paired, last), outward)
            turn = after(pick(paired, cycled), paired)
            grads[3] = outer_pairs(turn, swap)
            grads[2] = pick(outwards, after(cycled, turn))
            grads[1] = pick(after(cycled, grads[2]), crossed)
            sequence = [0, 2, 3, 1]
            early, late = [0, 2], [3, 1]
            last = turn
        else:
            for k in near_first:
                grads[k] = over_outer(paired, k)
            sequence = keys
            early, late = keys[: max(outer - 1, 1)], keys[max(outer - 1, 1) :]
            last = grads[near_first[0]] if outer > 1 else paired
        for k in early:
            last = advance(k, last) if k not in sums else last

        leaving = []
        for j in range(1, inner):
            value = weight_grad(early, j, last)
            if late:
                value = after(value, last) + weight_grad(late, j, value)
            leaving.append(value.astype(BF16))
        arriving = [over_inner(leaving[j - 1], j) for j in range(1, inner)]
        last = leaving[0] if inner > 1 else last
        for k in late:
            last = advance(k, last)
        total = weight_grad(sequence, 0, last)
        gate_total, up_total = total[:, :width], total[:, width:]
        for part in arriving:
            gate_total = gate_total + part[:, :width].astype(F32)
            up_total = up_total + part[:, width:].astype(F32)

        last = sums[sequence[-1]]
        if relay:
            sums[3], sums[1] = pick(sums[3], sums[1]), pick(sums[1], sums[3])
        dx = jnp.zeros((cap, outer * span), BF16)
        for k in keys:
            own = over_outer(sums[k], k) if k else sums[k]
            if k != sequence[-1]:
                own = after(own, last)
            for j in range(inner):
                block = own[:, j * depth : (j + 1) * depth]
                dx = lax.dynamic_update_slice(dx, block, (0, (a ^ k) * span + (b ^ j) * depth))
        grad_tokens = lax.dot_general(
            onehot, dx, (((0,), (0,)), ((), ())), preferred_element_type=F32
        ).astype(BF16)
        return (hidden, grad_tokens, gate_total, up_total)

    return shards


def solution(mesh):
    in_specs = (
        P(("dp", "etp"), None),
        P(("dp", "etp")),
        P(("dp", "etp")),
        P("dp", "etp"),
        P("dp", "etp"),
        P("dp", "etp"),
    )
    out_specs = (P("dp", "etp"), P(("dp", "etp"), None), P("dp", "etp"), P("dp", "etp"))
    shards = make_shards(mesh.shape["dp"], mesh.shape["etp"])
    return jax.shard_map(shards, mesh=mesh, in_specs=in_specs, out_specs=out_specs, check_vma=False)
```

```python
import functools

import jax
import jax.numpy as jnp
from jax import lax
from jax.experimental import pallas as pl
from jax.experimental.pallas import tpu as pltpu
from jax.sharding import PartitionSpec as P

F32 = jnp.float32
BF16 = jnp.bfloat16


def split_dp(dp):
    outer = 1
    while 4 * outer * outer <= 2 * dp:
        outer *= 2
    return outer, dp // outer


def after(value, *others):
    return lax.optimization_barrier((value,) + others)[0]


def tied(value, *others):
    for other in others:
        first = other[(0,) * other.ndim]
        value = jnp.where(first != first, first.astype(value.dtype), value)
    return value


def gate_kernel(steps, order_ref, pre_ref, prob_ref, cot_ref, *refs):
    part_refs, (hidden_ref, grad_ref) = refs[:-2], refs[-2:]
    rows, width = cot_ref.shape
    cap = rows // steps
    for i in range(steps):
        here = pl.ds(i * cap, cap)
        there = pl.ds(pl.multiple_of(order_ref[i] * cap, cap), cap)
        total = pre_ref[here, :]
        for part_ref in part_refs:
            total = total + part_ref[here, :].astype(F32)
        gate, up = total[:, :width], total[:, width:]
        prob = prob_ref[here, :].astype(F32)
        sig = jax.nn.sigmoid(gate)
        act = gate * sig
        hidden_ref[there, :] = (prob * act * up).astype(BF16)
        scaled = cot_ref[there, :].astype(F32) * prob
        grad_ref[here, :width] = (scaled * up * sig * (1.0 + gate * (1.0 - sig))).astype(BF16)
        grad_ref[here, width:] = (scaled * act).astype(BF16)


def gate_call(order, pre, prob, cotangent, parts):
    rows, width = cotangent.shape
    steps = order.shape[0]
    vmem = pl.BlockSpec(memory_space=pltpu.VMEM)
    return pl.pallas_call(
        functools.partial(gate_kernel, steps),
        out_shape=(
            jax.ShapeDtypeStruct((rows, width), BF16),
            jax.ShapeDtypeStruct((rows, 2 * width), BF16),
        ),
        in_specs=[pl.BlockSpec(memory_space=pltpu.SMEM)] + [vmem] * (3 + len(parts)),
        out_specs=(vmem, vmem),
        compiler_params=pltpu.CompilerParams(vmem_limit_bytes=24 * 2**20),
        cost_estimate=pl.CostEstimate(
            flops=20 * rows * width, bytes_accessed=rows * width * 30, transcendentals=rows * width
        ),
    )(order, pre, prob, cotangent, *parts)


def make_shards(dp_size, etp_size):
    outer, inner = split_dp(dp_size)

    def over_outer(value, k):
        pairs = [(i, i ^ (k * inner)) for i in range(dp_size)]
        return lax.ppermute(value, "dp", pairs)

    def over_inner(value, j):
        pairs = [(i, i ^ j) for i in range(dp_size)]
        return lax.ppermute(value, "dp", pairs)

    def over_etp(value, e):
        pairs = [(i, i ^ e) for i in range(etp_size)]
        return lax.ppermute(value, "etp", pairs)

    chunk_order = [0]
    bit = etp_size // 2
    bits = []
    while bit:
        bits.append(bit)
        chunk_order = chunk_order + [c ^ bit for c in chunk_order]
        bit //= 2

    def gather_etp(value, ties=()):
        for i, b in enumerate(bits):
            value = tied(value, *ties[i]) if i < len(ties) else value
            value = jnp.concatenate([value, over_etp(value, b)], axis=0)
        return value

    def reduce_etp(*values):
        for b in reversed(bits):
            half = values[0].shape[0] // 2
            leaving = [value[half:].astype(BF16) for value in values]
            got = over_etp(jnp.concatenate(leaving, axis=0) if len(leaving) > 1 else leaving[0], b)
            values = [v[:half] + got[i * half : (i + 1) * half].astype(F32) for i, v in enumerate(values)]
        return [value.astype(BF16) for value in values]

    near_first = sorted(range(1, outer))
    far_first = near_first[::-1]
    keys = [0] + near_first
    relay = outer == 4

    def outer_pairs(value, pairs):
        pairs = [(s * inner + i, t * inner + i) for s, t in pairs for i in range(inner)]
        return lax.ppermute(value, "dp", pairs)

    swap = [(0, 1), (1, 0), (2, 3), (3, 2)]
    cycle = [(0, 2), (2, 3), (3, 1), (1, 0)]
    back = [(t, s) for s, t in cycle]
    middle = [(1, 2), (2, 1)]
    inward = [(0, 2), (3, 1)]
    outward = [(2, 0), (1, 3)]

    def shards(tokens, slots, gate_probs, w_gate, w_up, d_hidden):
        dp = lax.axis_index("dp")
        etp = lax.axis_index("etp")
        a, b = dp // inner, dp % inner
        at_end = (a == 0) | (a == outer - 1)
        depth, width = w_gate.shape
        cap = slots.shape[0]
        tok = tokens.shape[0]
        span = depth * inner

        def pick(first, second):
            return jnp.where(at_end, first, second)

        weights = [jnp.concatenate([w_gate, w_up], axis=1)]
        weights += [over_inner(weights[0], j) for j in range(1, inner)]
        weights = jnp.concatenate(weights, axis=0)

        onehot = (slots[:, None] == jnp.arange(tok, dtype=slots.dtype)[None, :]).astype(BF16)
        rows = jnp.dot(onehot, tokens, preferred_element_type=F32).astype(BF16)
        pieces = {}
        for k in keys:
            blocks = [
                lax.dynamic_slice(rows, (0, (a ^ k) * span + (b ^ j) * depth), (cap, depth))
                for j in range(inner)
            ]
            pieces[k] = jnp.concatenate(blocks, axis=1)
        got = {k: over_outer(pieces[k], k) for k in far_first}
        if relay:
            got[3], got[1] = pick(got[3], got[1]), pick(got[1], got[3])
        got[0] = pieces[0]

        x_chunks = {}

        def multiply(k, *ties):
            x_chunks[k] = after(x_chunks[k], *ties)
            return jnp.dot(x_chunks[k], weights, preferred_element_type=F32)

        if relay:
            x_chunks[3] = gather_etp(got[3], [[], [weights[-1:]]])
            x_chunks[1] = gather_etp(got[1])
            far = multiply(3).astype(BF16)
            swapped = outer_pairs(far, swap)
            near = after(multiply(1, far).astype(BF16), far)
            crossed = outer_pairs(near, middle)
            x_chunks[2] = gather_etp(got[2], [[], [swapped, crossed]])
            x_chunks[0] = gather_etp(got[0], [[], [swapped, crossed]])
            two = after(multiply(2, swapped, crossed), swapped)
            inwards = outer_pairs(two.astype(BF16), inward)
            relayed = pick(near, (after(two, swapped) + swapped.astype(F32)).astype(BF16))
            cycled = outer_pairs(relayed, back)
            own = multiply(0, relayed) + crossed.astype(F32) + inwards.astype(F32)
            own = own + jnp.where(at_end, swapped.astype(F32), 0.0)
            parts = [cycled]
            last = relayed
        else:
            last, parts = rows, []
            x_chunks[0] = gather_etp(got[0])
            for k in far_first:
                x_chunks[k] = gather_etp(got[k], [[last]])
                last = multiply(k).astype(BF16)
                parts.append(over_outer(last, k))
            own = multiply(0, last)
        probs = gather_etp(after(gate_probs, last))
        order = etp ^ jnp.array(chunk_order, jnp.int32)
        hidden, paired = gate_call(order, own, probs[:, None], d_hidden, parts)

        grads, sums = {0: paired}, {}

        def advance(ks, last):
            partials = [
                lax.dot_general(
                    after(grads[k], last), weights, (((1,), (1,)), ((), ())), preferred_element_type=F32
                )
                for k in ks
            ]
            sums.update(zip(ks, reduce_etp(*partials)))
            return partials[-1]

        def weight_grad(ks, j, last):
            x_part = jnp.concatenate([x_chunks[k][:, j * depth : (j + 1) * depth] for k in ks], axis=0)
            grad_part = jnp.concatenate([grads[k] for k in ks], axis=0)
            return lax.dot_general(
                x_part, after(grad_part, last), (((0,), (0,)), ((), ())), preferred_element_type=F32
            )

        if relay:
            cycled = outer_pairs(paired, cycle)
            last = advance([0], paired)
            crossed = outer_pairs(after(paired, last), middle)
            outwards = outer_pairs(after(paired, last), outward)
            turn = after(pick(paired, cycled), paired)
            grads[3] = outer_pairs(turn, swap)
            grads[2] = pick(outwards, after(cycled, turn))
            grads[1] = pick(after(cycled, grads[2]), crossed)
            sequence = [0, 2, 3, 1]
            early, late = [0, 2], [3, 1]
            last = turn
        else:
            for k in near_first:
                grads[k] = over_outer(paired, k)
            sequence = keys
            early, late = keys[: max(outer - 1, 1)], keys[max(outer - 1, 1) :]
            last = grads[near_first[0]] if outer > 1 else paired
        for k in early:
            last = advance([k], last) if k not in sums else last

        leaving = []
        for j in range(1, inner):
            value = weight_grad(early, j, last)
            if late:
                value = after(value, last) + weight_grad(late, j, value)
            leaving.append(value.astype(BF16))
        arriving = [over_inner(leaving[j - 1], j) for j in range(1, inner)]
        last = leaving[0] if inner > 1 else last
        if late:
            last = advance(late, last)
        total = weight_grad(sequence, 0, last)
        gate_total, up_total = total[:, :width], total[:, width:]
        for part in arriving:
            gate_total = gate_total + part[:, :width].astype(F32)
            up_total = up_total + part[:, width:].astype(F32)

        last = sums[sequence[-1]]
        if relay:
            sums[3], sums[1] = pick(sums[3], sums[1]), pick(sums[1], sums[3])
        dx = jnp.zeros((cap, outer * span), BF16)
        for k in keys:
            own = over_outer(sums[k], k) if k else sums[k]
            if k != sequence[-1]:
                own = after(own, last)
            for j in range(inner):
                block = own[:, j * depth : (j + 1) * depth]
                dx = lax.dynamic_update_slice(dx, block, (0, (a ^ k) * span + (b ^ j) * depth))
        grad_tokens = lax.dot_general(
            onehot, dx, (((0,), (0,)), ((), ())), preferred_element_type=F32
        ).astype(BF16)
        return (hidden, grad_tokens, gate_total, up_total)

    return shards


def solution(mesh):
    in_specs = (
        P(("dp", "etp"), None),
        P(("dp", "etp")),
        P(("dp", "etp")),
        P("dp", "etp"),
        P("dp", "etp"),
        P("dp", "etp"),
    )
    out_specs = (P("dp", "etp"), P(("dp", "etp"), None), P("dp", "etp"), P("dp", "etp"))
    shards = make_shards(mesh.shape["dp"], mesh.shape["etp"])
    return jax.shard_map(shards, mesh=mesh, in_specs=in_specs, out_specs=out_specs, check_vma=False)
```

```python
import functools

import jax
import jax.numpy as jnp
from jax import lax
from jax.experimental import pallas as pl
from jax.experimental.pallas import tpu as pltpu
from jax.sharding import PartitionSpec as P

F32 = jnp.float32
BF16 = jnp.bfloat16


def split_dp(dp):
    outer = 1
    while 4 * outer * outer <= 2 * dp:
        outer *= 2
    return outer, dp // outer


def after(value, *others):
    return lax.optimization_barrier((value,) + others)[0]


def gate_kernel(steps, order_ref, pre_ref, prob_ref, cot_ref, *refs):
    part_refs, (hidden_ref, grad_ref) = refs[:-2], refs[-2:]
    rows, width = cot_ref.shape
    cap = rows // steps
    for i in range(steps):
        here = pl.ds(i * cap, cap)
        there = pl.ds(pl.multiple_of(order_ref[i] * cap, cap), cap)
        total = pre_ref[here, :]
        for part_ref in part_refs:
            total = total + part_ref[here, :].astype(F32)
        gate, up = total[:, :width], total[:, width:]
        prob = prob_ref[here, :].astype(F32)
        sig = jax.nn.sigmoid(gate)
        act = gate * sig
        hidden_ref[there, :] = (prob * act * up).astype(BF16)
        scaled = cot_ref[there, :].astype(F32) * prob
        grad_ref[here, :width] = (scaled * up * sig * (1.0 + gate * (1.0 - sig))).astype(BF16)
        grad_ref[here, width:] = (scaled * act).astype(BF16)


def gate_call(order, pre, prob, cotangent, parts):
    rows, width = cotangent.shape
    steps = order.shape[0]
    vmem = pl.BlockSpec(memory_space=pltpu.VMEM)
    return pl.pallas_call(
        functools.partial(gate_kernel, steps),
        out_shape=(
            jax.ShapeDtypeStruct((rows, width), BF16),
            jax.ShapeDtypeStruct((rows, 2 * width), BF16),
        ),
        in_specs=[pl.BlockSpec(memory_space=pltpu.SMEM)] + [vmem] * (3 + len(parts)),
        out_specs=(vmem, vmem),
        compiler_params=pltpu.CompilerParams(vmem_limit_bytes=24 * 2**20),
        cost_estimate=pl.CostEstimate(
            flops=20 * rows * width, bytes_accessed=rows * width * 30, transcendentals=rows * width
        ),
    )(order, pre, prob, cotangent, *parts)


def make_shards(dp_size, etp_size):
    outer, inner = split_dp(dp_size)

    def over_outer(value, k):
        pairs = [(i, i ^ (k * inner)) for i in range(dp_size)]
        return lax.ppermute(value, "dp", pairs)

    def over_inner(value, j):
        pairs = [(i, i ^ j) for i in range(dp_size)]
        return lax.ppermute(value, "dp", pairs)

    def over_etp(value, e):
        pairs = [(i, i ^ e) for i in range(etp_size)]
        return lax.ppermute(value, "etp", pairs)

    chunk_order = [0]
    bit = etp_size // 2
    bits = []
    while bit:
        bits.append(bit)
        chunk_order = chunk_order + [c ^ bit for c in chunk_order]
        bit //= 2

    def gather_etp(value, ties=()):
        for i, b in enumerate(bits):
            value = after(value, *ties[i]) if i < len(ties) else value
            value = jnp.concatenate([value, over_etp(value, b)], axis=0)
        return value

    def reduce_etp(*values):
        for b in reversed(bits):
            half = values[0].shape[0] // 2
            leaving = [value[half:].astype(BF16) for value in values]
            got = over_etp(jnp.concatenate(leaving, axis=0) if len(leaving) > 1 else leaving[0], b)
            values = [v[:half] + got[i * half : (i + 1) * half].astype(F32) for i, v in enumerate(values)]
        return [value.astype(BF16) for value in values]

    near_first = sorted(range(1, outer))
    far_first = near_first[::-1]
    keys = [0] + near_first
    relay = outer == 4

    def outer_pairs(value, pairs):
        pairs = [(s * inner + i, t * inner + i) for s, t in pairs for i in range(inner)]
        return lax.ppermute(value, "dp", pairs)

    swap = [(0, 1), (1, 0), (2, 3), (3, 2)]
    cycle = [(0, 2), (2, 3), (3, 1), (1, 0)]
    back = [(t, s) for s, t in cycle]
    middle = [(1, 2), (2, 1)]
    inward = [(0, 2), (3, 1)]
    outward = [(2, 0), (1, 3)]

    def shards(tokens, slots, gate_probs, w_gate, w_up, d_hidden):
        dp = lax.axis_index("dp")
        etp = lax.axis_index("etp")
        a, b = dp // inner, dp % inner
        at_end = (a == 0) | (a == outer - 1)
        depth, width = w_gate.shape
        cap = slots.shape[0]
        tok = tokens.shape[0]
        span = depth * inner

        def pick(first, second):
            return jnp.where(at_end, first, second)

        weights = [jnp.concatenate([w_gate, w_up], axis=1)]
        weights += [over_inner(weights[0], j) for j in range(1, inner)]
        weights = jnp.concatenate(weights, axis=0)

        onehot = (slots[:, None] == jnp.arange(tok, dtype=slots.dtype)[None, :]).astype(BF16)
        rows = jnp.dot(onehot, tokens, preferred_element_type=F32).astype(BF16)
        pieces = {}
        for k in keys:
            blocks = [
                lax.dynamic_slice(rows, (0, (a ^ k) * span + (b ^ j) * depth), (cap, depth))
                for j in range(inner)
            ]
            pieces[k] = jnp.concatenate(blocks, axis=1)
        got = {k: over_outer(pieces[k], k) for k in far_first}
        if relay:
            got[3], got[1] = pick(got[3], got[1]), pick(got[1], got[3])
        got[0] = pieces[0]

        x_chunks = {}

        def multiply(k, *ties):
            x_chunks[k] = after(x_chunks[k], *ties)
            return jnp.dot(x_chunks[k], weights, preferred_element_type=F32)

        if relay:
            x_chunks[3] = gather_etp(got[3])
            x_chunks[1] = gather_etp(got[1])
            far = multiply(3).astype(BF16)
            swapped = outer_pairs(far, swap)
            near = after(multiply(1, far).astype(BF16), far)
            crossed = outer_pairs(near, middle)
            x_chunks[2] = gather_etp(got[2], [[], [near]])
            x_chunks[0] = gather_etp(after(got[0], near))
            two = after(multiply(2, swapped, crossed), swapped)
            inwards = outer_pairs(two.astype(BF16), inward)
            relayed = pick(near, (after(two, swapped) + swapped.astype(F32)).astype(BF16))
            cycled = outer_pairs(relayed, back)
            own = multiply(0, relayed) + crossed.astype(F32) + inwards.astype(F32)
            own = own + jnp.where(at_end, swapped.astype(F32), 0.0)
            parts = [cycled]
            last = relayed
        else:
            last, parts = rows, []
            x_chunks[0] = gather_etp(got[0])
            for k in far_first:
                x_chunks[k] = gather_etp(got[k], [[last]])
                last = multiply(k).astype(BF16)
                parts.append(over_outer(last, k))
            own = multiply(0, last)
        probs = gather_etp(after(gate_probs, rows))
        order = etp ^ jnp.array(chunk_order, jnp.int32)
        hidden, paired = gate_call(order, own, probs[:, None], d_hidden, parts)

        grads, sums = {0: paired}, {}

        def advance(ks, last):
            partials = [
                lax.dot_general(
                    after(grads[k], last), weights, (((1,), (1,)), ((), ())), preferred_element_type=F32
                )
                for k in ks
            ]
            sums.update(zip(ks, reduce_etp(*partials)))
            return partials[-1]

        def weight_grad(ks, j, last):
            x_part = jnp.concatenate([x_chunks[k][:, j * depth : (j + 1) * depth] for k in ks], axis=0)
            grad_part = jnp.concatenate([grads[k] for k in ks], axis=0)
            return lax.dot_general(
                x_part, after(grad_part, last), (((0,), (0,)), ((), ())), preferred_element_type=F32
            )

        if relay:
            cycled = outer_pairs(paired, cycle)
            last = advance([0], paired)
            crossed = outer_pairs(after(paired, last), middle)
            outwards = outer_pairs(after(paired, last), outward)
            turn = after(pick(paired, cycled), paired)
            grads[3] = outer_pairs(turn, swap)
            grads[2] = pick(outwards, after(cycled, turn))
            grads[1] = pick(after(cycled, grads[2]), crossed)
            sequence = [0, 2, 3, 1]
            early, late = [0, 2], [3, 1]
            last = turn
        else:
            for k in near_first:
                grads[k] = over_outer(paired, k)
            sequence = keys
            early, late = keys[: max(outer - 1, 1)], keys[max(outer - 1, 1) :]
            last = grads[near_first[0]] if outer > 1 else paired
        for k in early:
            last = advance([k], last) if k not in sums else last

        leaving = []
        for j in range(1, inner):
            value = weight_grad(early, j, last)
            if late:
                value = after(value, last) + weight_grad(late, j, value)
            leaving.append(value.astype(BF16))
        arriving = [over_inner(leaving[j - 1], j) for j in range(1, inner)]
        last = leaving[0] if inner > 1 else last
        if late:
            last = advance(late, last)
        total = weight_grad(sequence, 0, last)
        gate_total, up_total = total[:, :width], total[:, width:]
        for part in arriving:
            gate_total = gate_total + part[:, :width].astype(F32)
            up_total = up_total + part[:, width:].astype(F32)

        last = sums[sequence[-1]]
        if relay:
            sums[3], sums[1] = pick(sums[3], sums[1]), pick(sums[1], sums[3])
        dx = jnp.zeros((cap, outer * span), BF16)
        for k in keys:
            own = over_outer(sums[k], k) if k else sums[k]
            if k != sequence[-1]:
                own = after(own, last)
            for j in range(inner):
                block = own[:, j * depth : (j + 1) * depth]
                dx = lax.dynamic_update_slice(dx, block, (0, (a ^ k) * span + (b ^ j) * depth))
        grad_tokens = lax.dot_general(
            onehot, dx, (((0,), (0,)), ((), ())), preferred_element_type=F32
        ).astype(BF16)
        return (hidden, grad_tokens, gate_total, up_total)

    return shards


def solution(mesh):
    in_specs = (
        P(("dp", "etp"), None),
        P(("dp", "etp")),
        P(("dp", "etp")),
        P("dp", "etp"),
        P("dp", "etp"),
        P("dp", "etp"),
    )
    out_specs = (P("dp", "etp"), P(("dp", "etp"), None), P("dp", "etp"), P("dp", "etp"))
    shards = make_shards(mesh.shape["dp"], mesh.shape["etp"])
    return jax.shard_map(shards, mesh=mesh, in_specs=in_specs, out_specs=out_specs, check_vma=False)
```

```python
import functools

import jax
import jax.numpy as jnp
from jax import lax
from jax.experimental import pallas as pl
from jax.experimental.pallas import tpu as pltpu
from jax.sharding import PartitionSpec as P

F32 = jnp.float32
BF16 = jnp.bfloat16


def split_dp(dp):
    outer = 1
    while 4 * outer * outer <= 2 * dp:
        outer *= 2
    return outer, dp // outer


def after(value, *others):
    return lax.optimization_barrier((value,) + others)[0]


def gate_kernel(steps, order_ref, pre_ref, prob_ref, cot_ref, *refs):
    part_refs, (hidden_ref, grad_ref) = refs[:-2], refs[-2:]
    rows, width = cot_ref.shape
    cap = rows // steps
    for i in range(steps):
        here = pl.ds(i * cap, cap)
        there = pl.ds(pl.multiple_of(order_ref[i] * cap, cap), cap)
        total = pre_ref[here, :]
        for part_ref in part_refs:
            total = total + part_ref[here, :].astype(F32)
        gate, up = total[:, :width], total[:, width:]
        prob = prob_ref[here, :].astype(F32)
        sig = jax.nn.sigmoid(gate)
        act = gate * sig
        hidden_ref[there, :] = (prob * act * up).astype(BF16)
        scaled = cot_ref[there, :].astype(F32) * prob
        grad_ref[here, :width] = (scaled * up * sig * (1.0 + gate * (1.0 - sig))).astype(BF16)
        grad_ref[here, width:] = (scaled * act).astype(BF16)


def gate_call(order, pre, prob, cotangent, parts):
    rows, width = cotangent.shape
    steps = order.shape[0]
    vmem = pl.BlockSpec(memory_space=pltpu.VMEM)
    return pl.pallas_call(
        functools.partial(gate_kernel, steps),
        out_shape=(
            jax.ShapeDtypeStruct((rows, width), BF16),
            jax.ShapeDtypeStruct((rows, 2 * width), BF16),
        ),
        in_specs=[pl.BlockSpec(memory_space=pltpu.SMEM)] + [vmem] * (3 + len(parts)),
        out_specs=(vmem, vmem),
        compiler_params=pltpu.CompilerParams(vmem_limit_bytes=24 * 2**20),
        cost_estimate=pl.CostEstimate(
            flops=20 * rows * width, bytes_accessed=rows * width * 30, transcendentals=rows * width
        ),
    )(order, pre, prob, cotangent, *parts)


def make_shards(dp_size, etp_size):
    outer, inner = split_dp(dp_size)

    def over_outer(value, k):
        pairs = [(i, i ^ (k * inner)) for i in range(dp_size)]
        return lax.ppermute(value, "dp", pairs)

    def over_inner(value, j):
        pairs = [(i, i ^ j) for i in range(dp_size)]
        return lax.ppermute(value, "dp", pairs)

    def over_etp(value, e):
        pairs = [(i, i ^ e) for i in range(etp_size)]
        return lax.ppermute(value, "etp", pairs)

    chunk_order = [0]
    bit = etp_size // 2
    bits = []
    while bit:
        bits.append(bit)
        chunk_order = chunk_order + [c ^ bit for c in chunk_order]
        bit //= 2

    def gather_etp(value, ties=()):
        for i, b in enumerate(bits):
            value = after(value, *ties[i]) if i < len(ties) else value
            value = jnp.concatenate([value, over_etp(value, b)], axis=0)
        return value

    def reduce_etp(*values):
        for b in reversed(bits):
            half = values[0].shape[0] // 2
            leaving = [value[half:].astype(BF16) for value in values]
            got = over_etp(jnp.concatenate(leaving, axis=0) if len(leaving) > 1 else leaving[0], b)
            values = [v[:half] + got[i * half : (i + 1) * half].astype(F32) for i, v in enumerate(values)]
        return [value.astype(BF16) for value in values]

    near_first = sorted(range(1, outer))
    far_first = near_first[::-1]
    keys = [0] + near_first
    relay = outer == 4

    def outer_pairs(value, pairs):
        pairs = [(s * inner + i, t * inner + i) for s, t in pairs for i in range(inner)]
        return lax.ppermute(value, "dp", pairs)

    swap = [(0, 1), (1, 0), (2, 3), (3, 2)]
    cycle = [(0, 2), (2, 3), (3, 1), (1, 0)]
    back = [(t, s) for s, t in cycle]
    middle = [(1, 2), (2, 1)]
    inward = [(0, 2), (3, 1)]
    outward = [(2, 0), (1, 3)]

    def shards(tokens, slots, gate_probs, w_gate, w_up, d_hidden):
        dp = lax.axis_index("dp")
        etp = lax.axis_index("etp")
        a, b = dp // inner, dp % inner
        at_end = (a == 0) | (a == outer - 1)
        depth, width = w_gate.shape
        cap = slots.shape[0]
        tok = tokens.shape[0]
        span = depth * inner

        def pick(first, second):
            return jnp.where(at_end, first, second)

        weights = [jnp.concatenate([w_gate, w_up], axis=1)]
        weights += [over_inner(weights[0], j) for j in range(1, inner)]
        weights = lax.optimization_barrier(jnp.concatenate(weights, axis=0))

        onehot = (slots[:, None] == jnp.arange(tok, dtype=slots.dtype)[None, :]).astype(BF16)
        rows = jnp.dot(onehot, tokens, preferred_element_type=F32).astype(BF16)
        pieces = {}
        for k in keys:
            blocks = [
                lax.dynamic_slice(rows, (0, (a ^ k) * span + (b ^ j) * depth), (cap, depth))
                for j in range(inner)
            ]
            pieces[k] = jnp.concatenate(blocks, axis=1)
        got = {k: over_outer(pieces[k], k) for k in far_first}
        if relay:
            got[3], got[1] = pick(got[3], got[1]), pick(got[1], got[3])
        got[0] = pieces[0]

        x_chunks = {}

        def multiply(k, *ties):
            x_chunks[k] = after(x_chunks[k], *ties)
            return jnp.dot(x_chunks[k], weights, preferred_element_type=F32)

        if relay:
            x_chunks[3] = gather_etp(got[3])
            x_chunks[1] = gather_etp(got[1])
            far = multiply(3).astype(BF16)
            swapped = outer_pairs(far, swap)
            near = after(multiply(1, far).astype(BF16), far)
            crossed = outer_pairs(near, middle)
            x_chunks[2] = gather_etp(got[2], [[], [near]])
            two = lax.optimization_barrier(multiply(2, near))
            x_chunks[0] = gather_etp(after(got[0], two))
            inwards = outer_pairs(two.astype(BF16), inward)
            relayed = pick(near, (after(two, swapped) + swapped.astype(F32)).astype(BF16))
            cycled = outer_pairs(relayed, back)
            own = multiply(0, relayed) + crossed.astype(F32) + inwards.astype(F32)
            own = own + jnp.where(at_end, swapped.astype(F32), 0.0)
            parts = [cycled]
            last = relayed
        else:
            last, parts = rows, []
            x_chunks[0] = gather_etp(got[0])
            for k in far_first:
                x_chunks[k] = gather_etp(got[k], [[last]])
                last = multiply(k).astype(BF16)
                parts.append(over_outer(last, k))
            own = multiply(0, last)
        probs = gather_etp(after(gate_probs, rows))
        order = etp ^ jnp.array(chunk_order, jnp.int32)
        hidden, paired = gate_call(order, own, probs[:, None], d_hidden, parts)

        grads, sums = {0: paired}, {}

        def advance(ks, last):
            partials = [
                lax.dot_general(
                    after(grads[k], last), weights, (((1,), (1,)), ((), ())), preferred_element_type=F32
                )
                for k in ks
            ]
            sums.update(zip(ks, reduce_etp(*partials)))
            return partials[-1]

        def weight_grad(ks, j, last):
            x_part = jnp.concatenate([x_chunks[k][:, j * depth : (j + 1) * depth] for k in ks], axis=0)
            grad_part = jnp.concatenate([grads[k] for k in ks], axis=0)
            return lax.dot_general(
                x_part, after(grad_part, last), (((0,), (0,)), ((), ())), preferred_element_type=F32
            )

        if relay:
            cycled = outer_pairs(paired, cycle)
            last = advance([0], paired)
            crossed = outer_pairs(after(paired, last), middle)
            outwards = outer_pairs(after(paired, last), outward)
            turn = after(pick(paired, cycled), paired)
            grads[3] = outer_pairs(turn, swap)
            grads[2] = pick(outwards, after(cycled, turn))
            grads[1] = pick(after(cycled, grads[2]), crossed)
            sequence = [0, 2, 3, 1]
            early, late = [0, 2], [3, 1]
            last = turn
        else:
            for k in near_first:
                grads[k] = over_outer(paired, k)
            sequence = keys
            early, late = keys[: max(outer - 1, 1)], keys[max(outer - 1, 1) :]
            last = grads[near_first[0]] if outer > 1 else paired
        for k in early:
            last = advance([k], last) if k not in sums else last

        leaving = []
        for j in range(1, inner):
            value = weight_grad(early, j, last)
            if late:
                value = after(value, last) + weight_grad(late, j, value)
            leaving.append(value.astype(BF16))
        arriving = [over_inner(leaving[j - 1], j) for j in range(1, inner)]
        last = leaving[0] if inner > 1 else last
        if late:
            last = advance(late, last)
        total = weight_grad(sequence, 0, last)
        gate_total, up_total = total[:, :width], total[:, width:]
        for part in arriving:
            gate_total = gate_total + part[:, :width].astype(F32)
            up_total = up_total + part[:, width:].astype(F32)

        last = sums[sequence[-1]]
        if relay:
            sums[3], sums[1] = pick(sums[3], sums[1]), pick(sums[1], sums[3])
        dx = jnp.zeros((cap, outer * span), BF16)
        for k in keys:
            own = over_outer(sums[k], k) if k else sums[k]
            if k != sequence[-1]:
                own = after(own, last)
            for j in range(inner):
                block = own[:, j * depth : (j + 1) * depth]
                dx = lax.dynamic_update_slice(dx, block, (0, (a ^ k) * span + (b ^ j) * depth))
        grad_tokens = lax.dot_general(
            onehot, dx, (((0,), (0,)), ((), ())), preferred_element_type=F32
        ).astype(BF16)
        return (hidden, grad_tokens, gate_total, up_total)

    return shards


def solution(mesh):
    in_specs = (
        P(("dp", "etp"), None),
        P(("dp", "etp")),
        P(("dp", "etp")),
        P("dp", "etp"),
        P("dp", "etp"),
        P("dp", "etp"),
    )
    out_specs = (P("dp", "etp"), P(("dp", "etp"), None), P("dp", "etp"), P("dp", "etp"))
    shards = make_shards(mesh.shape["dp"], mesh.shape["etp"])
    return jax.shard_map(shards, mesh=mesh, in_specs=in_specs, out_specs=out_specs, check_vma=False)
```

```python
import functools

import jax
import jax.numpy as jnp
from jax import lax
from jax.experimental import pallas as pl
from jax.experimental.pallas import tpu as pltpu
from jax.sharding import PartitionSpec as P

F32 = jnp.float32
BF16 = jnp.bfloat16


def split_dp(dp):
    outer = 1
    while 4 * outer * outer <= 2 * dp:
        outer *= 2
    return outer, dp // outer


def after(value, *others):
    return lax.optimization_barrier((value,) + others)[0]


def gate_kernel(steps, order_ref, pre_ref, prob_ref, cot_ref, *refs):
    part_refs, (hidden_ref, grad_ref) = refs[:-2], refs[-2:]
    rows, width = cot_ref.shape
    cap = rows // steps
    for i in range(steps):
        here = pl.ds(i * cap, cap)
        there = pl.ds(pl.multiple_of(order_ref[i] * cap, cap), cap)
        total = pre_ref[here, :]
        for part_ref in part_refs:
            total = total + part_ref[here, :].astype(F32)
        gate, up = total[:, :width], total[:, width:]
        prob = prob_ref[here, :].astype(F32)
        sig = jax.nn.sigmoid(gate)
        act = gate * sig
        hidden_ref[there, :] = (prob * act * up).astype(BF16)
        scaled = cot_ref[there, :].astype(F32) * prob
        grad_ref[here, :width] = (scaled * up * sig * (1.0 + gate * (1.0 - sig))).astype(BF16)
        grad_ref[here, width:] = (scaled * act).astype(BF16)


def gate_call(order, pre, prob, cotangent, parts):
    rows, width = cotangent.shape
    steps = order.shape[0]
    vmem = pl.BlockSpec(memory_space=pltpu.VMEM)
    return pl.pallas_call(
        functools.partial(gate_kernel, steps),
        out_shape=(
            jax.ShapeDtypeStruct((rows, width), BF16),
            jax.ShapeDtypeStruct((rows, 2 * width), BF16),
        ),
        in_specs=[pl.BlockSpec(memory_space=pltpu.SMEM)] + [vmem] * (3 + len(parts)),
        out_specs=(vmem, vmem),
        compiler_params=pltpu.CompilerParams(vmem_limit_bytes=24 * 2**20),
        cost_estimate=pl.CostEstimate(
            flops=20 * rows * width, bytes_accessed=rows * width * 30, transcendentals=rows * width
        ),
    )(order, pre, prob, cotangent, *parts)


def make_shards(dp_size, etp_size):
    outer, inner = split_dp(dp_size)

    def over_outer(value, k):
        pairs = [(i, i ^ (k * inner)) for i in range(dp_size)]
        return lax.ppermute(value, "dp", pairs)

    def over_inner(value, j):
        pairs = [(i, i ^ j) for i in range(dp_size)]
        return lax.ppermute(value, "dp", pairs)

    def over_etp(value, e):
        pairs = [(i, i ^ e) for i in range(etp_size)]
        return lax.ppermute(value, "etp", pairs)

    chunk_order = [0]
    bit = etp_size // 2
    bits = []
    while bit:
        bits.append(bit)
        chunk_order = chunk_order + [c ^ bit for c in chunk_order]
        bit //= 2

    def gather_etp(value, ties=()):
        for i, b in enumerate(bits):
            value = after(value, *ties[i]) if i < len(ties) else value
            value = jnp.concatenate([value, over_etp(value, b)], axis=0)
        return value

    def reduce_etp(*values):
        for b in reversed(bits):
            half = values[0].shape[0] // 2
            leaving = [value[half:].astype(BF16) for value in values]
            got = over_etp(jnp.concatenate(leaving, axis=0) if len(leaving) > 1 else leaving[0], b)
            values = [v[:half] + got[i * half : (i + 1) * half].astype(F32) for i, v in enumerate(values)]
        return [value.astype(BF16) for value in values]

    near_first = sorted(range(1, outer))
    far_first = near_first[::-1]
    keys = [0] + near_first
    relay = outer == 4

    def outer_pairs(value, pairs):
        pairs = [(s * inner + i, t * inner + i) for s, t in pairs for i in range(inner)]
        return lax.ppermute(value, "dp", pairs)

    swap = [(0, 1), (1, 0), (2, 3), (3, 2)]
    cycle = [(0, 2), (2, 3), (3, 1), (1, 0)]
    back = [(t, s) for s, t in cycle]
    middle = [(1, 2), (2, 1)]
    outward = [(2, 0), (1, 3)]

    def shards(tokens, slots, gate_probs, w_gate, w_up, d_hidden):
        dp = lax.axis_index("dp")
        etp = lax.axis_index("etp")
        a, b = dp // inner, dp % inner
        at_end = (a == 0) | (a == outer - 1)
        depth, width = w_gate.shape
        cap = slots.shape[0]
        tok = tokens.shape[0]
        span = depth * inner

        def pick(first, second):
            return jnp.where(at_end, first, second)

        weights = [jnp.concatenate([w_gate, w_up], axis=1)]
        for j in range(1, inner):
            weights.append(jnp.concatenate([over_inner(w_gate, j), over_inner(w_up, j)], axis=1))
        weights = jnp.concatenate(weights, axis=0)

        onehot = (slots[:, None] == jnp.arange(tok, dtype=slots.dtype)[None, :]).astype(BF16)
        rows = jnp.dot(onehot, tokens, preferred_element_type=F32).astype(BF16)
        pieces = {}
        for k in keys:
            blocks = [
                lax.dynamic_slice(rows, (0, (a ^ k) * span + (b ^ j) * depth), (cap, depth))
                for j in range(inner)
            ]
            pieces[k] = jnp.concatenate(blocks, axis=1)
        got = {k: over_outer(pieces[k], k) for k in far_first}
        got[0] = pieces[0]

        x_chunks = {}

        parts, last = [], None
        for k in far_first + [0]:
            x_chunks[k] = gather_etp(got[k] if last is None else after(got[k], last))
            product = jnp.dot(x_chunks[k], weights, preferred_element_type=F32)
            if k:
                last = product.astype(BF16)
                parts.append(over_outer(last, k))
        own = product
        for part in parts[:-1]:
            own = own + part.astype(F32)
        parts = parts[-1:]
        probs = gather_etp(after(gate_probs, product))
        order = etp ^ jnp.array(chunk_order, jnp.int32)
        hidden, paired = gate_call(order, own, probs[:, None], d_hidden, parts)

        grads, sums = {0: paired}, {}

        def advance(ks, last):
            partials = [
                lax.dot_general(
                    after(grads[k], last), weights, (((1,), (1,)), ((), ())), preferred_element_type=F32
                )
                for k in ks
            ]
            sums.update(zip(ks, reduce_etp(*partials)))
            return partials[-1]

        def weight_grad(ks, j, last):
            x_part = jnp.concatenate([x_chunks[k][:, j * depth : (j + 1) * depth] for k in ks], axis=0)
            grad_part = jnp.concatenate([grads[k] for k in ks], axis=0)
            return lax.dot_general(
                x_part, after(grad_part, last), (((0,), (0,)), ((), ())), preferred_element_type=F32
            )

        if relay:
            x_chunks[3], x_chunks[1] = pick(x_chunks[3], x_chunks[1]), pick(x_chunks[1], x_chunks[3])
            cycled = outer_pairs(paired, cycle)
            last = advance([0], paired)
            crossed = outer_pairs(after(paired, last), middle)
            outwards = outer_pairs(after(paired, last), outward)
            turn = after(pick(paired, cycled), paired)
            grads[3] = outer_pairs(turn, swap)
            grads[2] = pick(outwards, after(cycled, turn))
            grads[1] = pick(after(cycled, grads[2]), crossed)
            sequence = [0, 2, 3, 1]
            early, late = [0, 2], [3, 1]
            last = turn
        else:
            for k in near_first:
                grads[k] = over_outer(paired, k)
            sequence = keys
            early, late = keys[: max(outer - 1, 1)], keys[max(outer - 1, 1) :]
            last = grads[near_first[0]] if outer > 1 else paired
        for k in early:
            last = advance([k], last) if k not in sums else last

        leaving = []
        for j in range(1, inner):
            value = weight_grad(early, j, last)
            if late:
                value = after(value, last) + weight_grad(late, j, value)
            leaving.append(value.astype(BF16))
        arriving = [over_inner(leaving[j - 1], j) for j in range(1, inner)]
        last = leaving[0] if inner > 1 else last
        if late:
            last = advance(late, last)
        total = weight_grad(sequence, 0, last)
        gate_total, up_total = total[:, :width], total[:, width:]
        for part in arriving:
            gate_total = gate_total + part[:, :width].astype(F32)
            up_total = up_total + part[:, width:].astype(F32)

        last = sums[sequence[-1]]
        if relay:
            sums[3], sums[1] = pick(sums[3], sums[1]), pick(sums[1], sums[3])
        dx = jnp.zeros((cap, outer * span), BF16)
        for k in keys:
            own = over_outer(sums[k], k) if k else sums[k]
            if k != sequence[-1]:
                own = after(own, last)
            for j in range(inner):
                block = own[:, j * depth : (j + 1) * depth]
                dx = lax.dynamic_update_slice(dx, block, (0, (a ^ k) * span + (b ^ j) * depth))
        grad_tokens = lax.dot_general(
            onehot, dx, (((0,), (0,)), ((), ())), preferred_element_type=F32
        ).astype(BF16)
        return (hidden, grad_tokens, gate_total, up_total)

    return shards


def solution(mesh):
    in_specs = (
        P(("dp", "etp"), None),
        P(("dp", "etp")),
        P(("dp", "etp")),
        P("dp", "etp"),
        P("dp", "etp"),
        P("dp", "etp"),
    )
    out_specs = (P("dp", "etp"), P(("dp", "etp"), None), P("dp", "etp"), P("dp", "etp"))
    shards = make_shards(mesh.shape["dp"], mesh.shape["etp"])
    return jax.shard_map(shards, mesh=mesh, in_specs=in_specs, out_specs=out_specs, check_vma=False)
```

```python
import functools

import jax
import jax.numpy as jnp
from jax import lax
from jax.experimental import pallas as pl
from jax.experimental.pallas import tpu as pltpu
from jax.sharding import PartitionSpec as P

F32 = jnp.float32
BF16 = jnp.bfloat16


def split_dp(dp):
    outer = 1
    while 4 * outer * outer <= 2 * dp:
        outer *= 2
    return outer, dp // outer


def after(value, *others):
    return lax.optimization_barrier((value,) + others)[0]


def gate_kernel(steps, order_ref, pre_ref, prob_ref, cot_ref, *refs):
    part_refs, (hidden_ref, grad_ref) = refs[:-2], refs[-2:]
    rows, width = cot_ref.shape
    cap = rows // steps
    for i in range(steps):
        here = pl.ds(i * cap, cap)
        there = pl.ds(pl.multiple_of(order_ref[i] * cap, cap), cap)
        total = pre_ref[here, :]
        for part_ref in part_refs:
            total = total + part_ref[here, :].astype(F32)
        gate, up = total[:, :width], total[:, width:]
        prob = prob_ref[here, :].astype(F32)
        sig = jax.nn.sigmoid(gate)
        act = gate * sig
        hidden_ref[there, :] = (prob * act * up).astype(BF16)
        scaled = cot_ref[there, :].astype(F32) * prob
        grad_ref[here, :width] = (scaled * up * sig * (1.0 + gate * (1.0 - sig))).astype(BF16)
        grad_ref[here, width:] = (scaled * act).astype(BF16)


def gate_call(order, pre, prob, cotangent, parts):
    rows, width = cotangent.shape
    steps = order.shape[0]
    vmem = pl.BlockSpec(memory_space=pltpu.VMEM)
    return pl.pallas_call(
        functools.partial(gate_kernel, steps),
        out_shape=(
            jax.ShapeDtypeStruct((rows, width), BF16),
            jax.ShapeDtypeStruct((rows, 2 * width), BF16),
        ),
        in_specs=[pl.BlockSpec(memory_space=pltpu.SMEM)] + [vmem] * (3 + len(parts)),
        out_specs=(vmem, vmem),
        compiler_params=pltpu.CompilerParams(vmem_limit_bytes=24 * 2**20),
        cost_estimate=pl.CostEstimate(
            flops=20 * rows * width, bytes_accessed=rows * width * 30, transcendentals=rows * width
        ),
    )(order, pre, prob, cotangent, *parts)


def make_shards(dp_size, etp_size):
    outer, inner = split_dp(dp_size)

    def over_outer(value, k):
        pairs = [(i, i ^ (k * inner)) for i in range(dp_size)]
        return lax.ppermute(value, "dp", pairs)

    def over_inner(value, j):
        pairs = [(i, i ^ j) for i in range(dp_size)]
        return lax.ppermute(value, "dp", pairs)

    def over_etp(value, e):
        pairs = [(i, i ^ e) for i in range(etp_size)]
        return lax.ppermute(value, "etp", pairs)

    chunk_order = [0]
    bit = etp_size // 2
    bits = []
    while bit:
        bits.append(bit)
        chunk_order = chunk_order + [c ^ bit for c in chunk_order]
        bit //= 2

    def gather_etp(value, ties=()):
        for i, b in enumerate(bits):
            value = after(value, *ties[i]) if i < len(ties) else value
            value = jnp.concatenate([value, over_etp(value, b)], axis=0)
        return value

    def reduce_etp(*values):
        for b in reversed(bits):
            half = values[0].shape[0] // 2
            leaving = [value[half:].astype(BF16) for value in values]
            got = over_etp(jnp.concatenate(leaving, axis=0) if len(leaving) > 1 else leaving[0], b)
            values = [v[:half] + got[i * half : (i + 1) * half].astype(F32) for i, v in enumerate(values)]
        return [value.astype(BF16) for value in values]

    near_first = sorted(range(1, outer))
    far_first = near_first[::-1]
    keys = [0] + near_first
    relay = outer == 4

    def outer_pairs(value, pairs):
        pairs = [(s * inner + i, t * inner + i) for s, t in pairs for i in range(inner)]
        return lax.ppermute(value, "dp", pairs)

    swap = [(0, 1), (1, 0), (2, 3), (3, 2)]
    cycle = [(0, 2), (2, 3), (3, 1), (1, 0)]
    back = [(t, s) for s, t in cycle]
    middle = [(1, 2), (2, 1)]
    outward = [(2, 0), (1, 3)]

    def shards(tokens, slots, gate_probs, w_gate, w_up, d_hidden):
        dp = lax.axis_index("dp")
        etp = lax.axis_index("etp")
        a, b = dp // inner, dp % inner
        at_end = (a == 0) | (a == outer - 1)
        depth, width = w_gate.shape
        cap = slots.shape[0]
        tok = tokens.shape[0]
        span = depth * inner

        def pick(first, second):
            return jnp.where(at_end, first, second)

        weights = [jnp.concatenate([w_gate, w_up], axis=1)]
        for j in range(1, inner):
            weights.append(jnp.concatenate([over_inner(w_gate, j), over_inner(w_up, j)], axis=1))
        weights = jnp.concatenate(weights, axis=0)

        onehot = (slots[:, None] == jnp.arange(tok, dtype=slots.dtype)[None, :]).astype(BF16)
        rows = jnp.dot(onehot, tokens, preferred_element_type=F32).astype(BF16)
        pieces = {}
        for k in keys:
            blocks = [
                lax.dynamic_slice(rows, (0, (a ^ k) * span + (b ^ j) * depth), (cap, depth))
                for j in range(inner)
            ]
            pieces[k] = jnp.concatenate(blocks, axis=1)
        got = {k: over_outer(pieces[k], k) for k in far_first}
        got[0] = pieces[0]

        x_chunks = {k: gather_etp(got[k]) for k in [0] + far_first}
        each = cap * etp_size
        product = jnp.dot(
            jnp.concatenate([x_chunks[k] for k in [0] + far_first], axis=0),
            weights,
            preferred_element_type=F32,
        )
        products = {k: product[i * each : (i + 1) * each] for i, k in enumerate([0] + far_first)}
        parts = [over_outer(products[k].astype(BF16), k) for k in far_first]
        probs = gather_etp(after(gate_probs, product))
        own = products[0]
        for part in parts[:-1]:
            own = own + part.astype(F32)
        parts = parts[-1:]
        order = etp ^ jnp.array(chunk_order, jnp.int32)
        hidden, paired = gate_call(order, own, probs[:, None], d_hidden, parts)

        grads, sums = {0: paired}, {}

        def advance(ks, last):
            partials = [
                lax.dot_general(
                    after(grads[k], last), weights, (((1,), (1,)), ((), ())), preferred_element_type=F32
                )
                for k in ks
            ]
            sums.update(zip(ks, reduce_etp(*partials)))
            return partials[-1]

        def weight_grad(ks, j, last):
            x_part = jnp.concatenate([x_chunks[k][:, j * depth : (j + 1) * depth] for k in ks], axis=0)
            grad_part = jnp.concatenate([grads[k] for k in ks], axis=0)
            return lax.dot_general(
                x_part, after(grad_part, last), (((0,), (0,)), ((), ())), preferred_element_type=F32
            )

        if relay:
            x_chunks[3], x_chunks[1] = pick(x_chunks[3], x_chunks[1]), pick(x_chunks[1], x_chunks[3])
            cycled = outer_pairs(paired, cycle)
            last = advance([0], paired)
            crossed = outer_pairs(after(paired, last), middle)
            outwards = outer_pairs(after(paired, last), outward)
            turn = after(pick(paired, cycled), paired)
            grads[3] = outer_pairs(turn, swap)
            grads[2] = pick(outwards, after(cycled, turn))
            grads[1] = pick(after(cycled, grads[2]), crossed)
            sequence = [0, 2, 3, 1]
            early, late = [0, 2], [3, 1]
            last = turn
        else:
            for k in near_first:
                grads[k] = over_outer(paired, k)
            sequence = keys
            early, late = keys[: max(outer - 1, 1)], keys[max(outer - 1, 1) :]
            last = grads[near_first[0]] if outer > 1 else paired
        for k in early:
            last = advance([k], last) if k not in sums else last

        leaving = []
        for j in range(1, inner):
            value = weight_grad(early, j, last)
            if late:
                value = after(value, last) + weight_grad(late, j, value)
            leaving.append(value.astype(BF16))
        arriving = [over_inner(leaving[j - 1], j) for j in range(1, inner)]
        last = leaving[0] if inner > 1 else last
        if late:
            last = advance(late, last)
        total = weight_grad(sequence, 0, last)
        gate_total, up_total = total[:, :width], total[:, width:]
        for part in arriving:
            gate_total = gate_total + part[:, :width].astype(F32)
            up_total = up_total + part[:, width:].astype(F32)

        last = sums[sequence[-1]]
        if relay:
            sums[3], sums[1] = pick(sums[3], sums[1]), pick(sums[1], sums[3])
        dx = jnp.zeros((cap, outer * span), BF16)
        for k in keys:
            own = over_outer(sums[k], k) if k else sums[k]
            if k != sequence[-1]:
                own = after(own, last)
            for j in range(inner):
                block = own[:, j * depth : (j + 1) * depth]
                dx = lax.dynamic_update_slice(dx, block, (0, (a ^ k) * span + (b ^ j) * depth))
        grad_tokens = lax.dot_general(
            onehot, dx, (((0,), (0,)), ((), ())), preferred_element_type=F32
        ).astype(BF16)
        return (hidden, grad_tokens, gate_total, up_total)

    return shards


def solution(mesh):
    in_specs = (
        P(("dp", "etp"), None),
        P(("dp", "etp")),
        P(("dp", "etp")),
        P("dp", "etp"),
        P("dp", "etp"),
        P("dp", "etp"),
    )
    out_specs = (P("dp", "etp"), P(("dp", "etp"), None), P("dp", "etp"), P("dp", "etp"))
    shards = make_shards(mesh.shape["dp"], mesh.shape["etp"])
    return jax.shard_map(shards, mesh=mesh, in_specs=in_specs, out_specs=out_specs, check_vma=False)
```

```python
import functools

import jax
import jax.numpy as jnp
from jax import lax
from jax.experimental import pallas as pl
from jax.experimental.pallas import tpu as pltpu
from jax.sharding import PartitionSpec as P

F32 = jnp.float32
BF16 = jnp.bfloat16


def split_dp(dp):
    outer = 1
    while 4 * outer * outer <= 2 * dp:
        outer *= 2
    return outer, dp // outer


def after(value, *others):
    return lax.optimization_barrier((value,) + others)[0]


def gate_kernel(steps, order_ref, pre_ref, prob_ref, cot_ref, *refs):
    part_refs, (hidden_ref, grad_ref) = refs[:-2], refs[-2:]
    rows, width = cot_ref.shape
    cap = rows // steps
    for i in range(steps):
        here = pl.ds(i * cap, cap)
        there = pl.ds(pl.multiple_of(order_ref[i] * cap, cap), cap)
        total = pre_ref[here, :]
        for part_ref in part_refs:
            total = total + part_ref[here, :].astype(F32)
        gate, up = total[:, :width], total[:, width:]
        prob = prob_ref[here, :].astype(F32)
        sig = jax.nn.sigmoid(gate)
        act = gate * sig
        hidden_ref[there, :] = (prob * act * up).astype(BF16)
        scaled = cot_ref[there, :].astype(F32) * prob
        grad_ref[here, :width] = (scaled * up * sig * (1.0 + gate * (1.0 - sig))).astype(BF16)
        grad_ref[here, width:] = (scaled * act).astype(BF16)


def gate_call(order, pre, prob, cotangent, parts):
    rows, width = cotangent.shape
    steps = order.shape[0]
    vmem = pl.BlockSpec(memory_space=pltpu.VMEM)
    return pl.pallas_call(
        functools.partial(gate_kernel, steps),
        out_shape=(
            jax.ShapeDtypeStruct((rows, width), BF16),
            jax.ShapeDtypeStruct((rows, 2 * width), BF16),
        ),
        in_specs=[pl.BlockSpec(memory_space=pltpu.SMEM)] + [vmem] * (3 + len(parts)),
        out_specs=(vmem, vmem),
        compiler_params=pltpu.CompilerParams(vmem_limit_bytes=24 * 2**20),
        cost_estimate=pl.CostEstimate(
            flops=20 * rows * width, bytes_accessed=rows * width * 30, transcendentals=rows * width
        ),
    )(order, pre, prob, cotangent, *parts)


def make_shards(dp_size, etp_size):
    outer, inner = split_dp(dp_size)

    def over_outer(value, k):
        pairs = [(i, i ^ (k * inner)) for i in range(dp_size)]
        return lax.ppermute(value, "dp", pairs)

    def over_inner(value, j):
        pairs = [(i, i ^ j) for i in range(dp_size)]
        return lax.ppermute(value, "dp", pairs)

    def over_etp(value, e):
        pairs = [(i, i ^ e) for i in range(etp_size)]
        return lax.ppermute(value, "etp", pairs)

    chunk_order = [0]
    bit = etp_size // 2
    bits = []
    while bit:
        bits.append(bit)
        chunk_order = chunk_order + [c ^ bit for c in chunk_order]
        bit //= 2

    def gather_etp(value, ties=()):
        for i, b in enumerate(bits):
            value = after(value, *ties[i]) if i < len(ties) else value
            value = jnp.concatenate([value, over_etp(value, b)], axis=0)
        return value

    def reduce_etp(*values):
        for b in reversed(bits):
            half = values[0].shape[0] // 2
            leaving = [value[half:].astype(BF16) for value in values]
            got = over_etp(jnp.concatenate(leaving, axis=0) if len(leaving) > 1 else leaving[0], b)
            values = [v[:half] + got[i * half : (i + 1) * half].astype(F32) for i, v in enumerate(values)]
        return [value.astype(BF16) for value in values]

    near_first = sorted(range(1, outer))
    far_first = near_first[::-1]
    keys = [0] + near_first
    relay = outer == 4

    def outer_pairs(value, pairs):
        pairs = [(s * inner + i, t * inner + i) for s, t in pairs for i in range(inner)]
        return lax.ppermute(value, "dp", pairs)

    swap = [(0, 1), (1, 0), (2, 3), (3, 2)]
    cycle = [(0, 2), (2, 3), (3, 1), (1, 0)]
    back = [(t, s) for s, t in cycle]
    middle = [(1, 2), (2, 1)]
    inward = [(0, 2), (3, 1)]
    outward = [(2, 0), (1, 3)]

    def shards(tokens, slots, gate_probs, w_gate, w_up, d_hidden):
        dp = lax.axis_index("dp")
        etp = lax.axis_index("etp")
        a, b = dp // inner, dp % inner
        at_end = (a == 0) | (a == outer - 1)
        depth, width = w_gate.shape
        cap = slots.shape[0]
        tok = tokens.shape[0]
        span = depth * inner

        def pick(first, second):
            return jnp.where(at_end, first, second)

        weights = [jnp.concatenate([w_gate, w_up], axis=1)]
        for j in range(1, inner):
            weights.append(jnp.concatenate([over_inner(w_gate, j), over_inner(w_up, j)], axis=1))
        weights = jnp.concatenate(weights, axis=0)

        onehot = (slots[:, None] == jnp.arange(tok, dtype=slots.dtype)[None, :]).astype(BF16)
        rows = jnp.dot(onehot, tokens, preferred_element_type=F32).astype(BF16)
        pieces = {}
        for k in keys:
            blocks = [
                lax.dynamic_slice(rows, (0, (a ^ k) * span + (b ^ j) * depth), (cap, depth))
                for j in range(inner)
            ]
            pieces[k] = jnp.concatenate(blocks, axis=1)
        got = {k: over_outer(pieces[k], k) for k in far_first}
        if relay:
            got[3], got[1] = pick(got[3], got[1]), pick(got[1], got[3])
        got[0] = pieces[0]

        x_chunks = {}

        def multiply(k, *ties):
            x_chunks[k] = after(x_chunks[k], *ties)
            return jnp.dot(x_chunks[k], weights, preferred_element_type=F32)

        if relay:
            x_chunks[3] = gather_etp(got[3])
            x_chunks[1] = gather_etp(got[1])
            far = multiply(3).astype(BF16)
            swapped = outer_pairs(far, swap)
            near = after(multiply(1, far).astype(BF16), far)
            crossed = outer_pairs(near, middle)
            x_chunks[2] = gather_etp(got[2], [[], [near]])
            x_chunks[0] = gather_etp(after(got[0], near))
            two = after(multiply(2, swapped, crossed), swapped)
            inwards = outer_pairs(two.astype(BF16), inward)
            relayed = pick(near, (after(two, swapped) + swapped.astype(F32)).astype(BF16))
            cycled = outer_pairs(relayed, back)
            own = multiply(0, relayed) + crossed.astype(F32) + inwards.astype(F32)
            own = own + jnp.where(at_end, swapped.astype(F32), 0.0)
            parts = [cycled]
            last = relayed
        else:
            last, parts = rows, []
            x_chunks[0] = gather_etp(got[0])
            for k in far_first:
                x_chunks[k] = gather_etp(got[k], [[last]])
                last = multiply(k).astype(BF16)
                parts.append(over_outer(last, k))
            own = multiply(0, last)
        probs = gather_etp(after(gate_probs, rows))
        order = etp ^ jnp.array(chunk_order, jnp.int32)
        hidden, paired = gate_call(order, own, probs[:, None], d_hidden, parts)

        grads, sums = {0: paired}, {}

        def advance(ks, last):
            partials = [
                lax.dot_general(
                    after(grads[k], last), weights, (((1,), (1,)), ((), ())), preferred_element_type=F32
                )
                for k in ks
            ]
            sums.update(zip(ks, reduce_etp(*partials)))
            return partials[-1]

        def weight_grad(ks, j, last):
            x_part = jnp.concatenate([x_chunks[k][:, j * depth : (j + 1) * depth] for k in ks], axis=0)
            grad_part = jnp.concatenate([grads[k] for k in ks], axis=0)
            return lax.dot_general(
                x_part, after(grad_part, last), (((0,), (0,)), ((), ())), preferred_element_type=F32
            )

        if relay:
            cycled = outer_pairs(paired, cycle)
            last = advance([0], paired)
            crossed = outer_pairs(after(paired, last), middle)
            outwards = outer_pairs(after(paired, last), outward)
            turn = after(pick(paired, cycled), paired)
            grads[3] = outer_pairs(turn, swap)
            grads[2] = pick(outwards, after(cycled, turn))
            grads[1] = pick(after(cycled, grads[2]), crossed)
            sequence = [0, 2, 3, 1]
            early, late = [0, 2], [3, 1]
            last = turn
        else:
            for k in near_first:
                grads[k] = over_outer(paired, k)
            sequence = keys
            early, late = keys[: max(outer - 1, 1)], keys[max(outer - 1, 1) :]
            last = grads[near_first[0]] if outer > 1 else paired
        for k in early:
            last = advance([k], last) if k not in sums else last

        leaving = []
        for j in range(1, inner):
            value = weight_grad(early, j, last)
            if late:
                value = after(value, last) + weight_grad(late, j, value)
            leaving.append(value.astype(BF16))
        arriving = [over_inner(leaving[j - 1], j) for j in range(1, inner)]
        last = leaving[0] if inner > 1 else last
        if late:
            last = advance(late, last)
        total = weight_grad(sequence, 0, last)
        gate_total, up_total = total[:, :width], total[:, width:]
        for part in arriving:
            gate_total = gate_total + part[:, :width].astype(F32)
            up_total = up_total + part[:, width:].astype(F32)

        last = sums[sequence[-1]]
        if relay:
            sums[3], sums[1] = pick(sums[3], sums[1]), pick(sums[1], sums[3])
        dx = jnp.zeros((cap, outer * span), BF16)
        for k in keys:
            own = over_outer(sums[k], k) if k else sums[k]
            if k != sequence[-1]:
                own = after(own, last)
            for j in range(inner):
                block = own[:, j * depth : (j + 1) * depth]
                dx = lax.dynamic_update_slice(dx, block, (0, (a ^ k) * span + (b ^ j) * depth))
        grad_tokens = lax.dot_general(
            onehot, dx, (((0,), (0,)), ((), ())), preferred_element_type=F32
        ).astype(BF16)
        return (hidden, grad_tokens, gate_total, up_total)

    return shards


def solution(mesh):
    in_specs = (
        P(("dp", "etp"), None),
        P(("dp", "etp")),
        P(("dp", "etp")),
        P("dp", "etp"),
        P("dp", "etp"),
        P("dp", "etp"),
    )
    out_specs = (P("dp", "etp"), P(("dp", "etp"), None), P("dp", "etp"), P("dp", "etp"))
    shards = make_shards(mesh.shape["dp"], mesh.shape["etp"])
    return jax.shard_map(shards, mesh=mesh, in_specs=in_specs, out_specs=out_specs, check_vma=False)
```

```python
import functools

import jax
import jax.numpy as jnp
from jax import lax
from jax.experimental import pallas as pl
from jax.experimental.pallas import tpu as pltpu
from jax.sharding import PartitionSpec as P

F32 = jnp.float32
BF16 = jnp.bfloat16


def split_dp(dp):
    outer = 1
    while 4 * outer * outer <= 2 * dp:
        outer *= 2
    return outer, dp // outer


def after(value, *others):
    return lax.optimization_barrier((value,) + others)[0]


def behind(value, *others):
    anywhere = pl.BlockSpec(memory_space=pl.ANY)
    return pl.pallas_call(
        lambda *refs: None,
        out_shape=jax.ShapeDtypeStruct(value.shape, value.dtype),
        in_specs=[anywhere] * (1 + len(others)),
        out_specs=anywhere,
        input_output_aliases={0: 0},
        cost_estimate=pl.CostEstimate(flops=0, bytes_accessed=0, transcendentals=0),
    )(value, *others)


def gate_kernel(steps, order_ref, pre_ref, prob_ref, cot_ref, *refs):
    part_refs, (hidden_ref, grad_ref) = refs[:-2], refs[-2:]
    rows, width = cot_ref.shape
    cap = rows // steps
    for i in range(steps):
        here = pl.ds(i * cap, cap)
        there = pl.ds(pl.multiple_of(order_ref[i] * cap, cap), cap)
        total = pre_ref[here, :]
        for part_ref in part_refs:
            total = total + part_ref[here, :].astype(F32)
        gate, up = total[:, :width], total[:, width:]
        prob = prob_ref[here, :].astype(F32)
        sig = jax.nn.sigmoid(gate)
        act = gate * sig
        hidden_ref[there, :] = (prob * act * up).astype(BF16)
        scaled = cot_ref[there, :].astype(F32) * prob
        grad_ref[here, :width] = (scaled * up * sig * (1.0 + gate * (1.0 - sig))).astype(BF16)
        grad_ref[here, width:] = (scaled * act).astype(BF16)


def gate_call(order, pre, prob, cotangent, parts):
    rows, width = cotangent.shape
    steps = order.shape[0]
    vmem = pl.BlockSpec(memory_space=pltpu.VMEM)
    return pl.pallas_call(
        functools.partial(gate_kernel, steps),
        out_shape=(
            jax.ShapeDtypeStruct((rows, width), BF16),
            jax.ShapeDtypeStruct((rows, 2 * width), BF16),
        ),
        in_specs=[pl.BlockSpec(memory_space=pltpu.SMEM)] + [vmem] * (3 + len(parts)),
        out_specs=(vmem, vmem),
        compiler_params=pltpu.CompilerParams(vmem_limit_bytes=24 * 2**20),
        cost_estimate=pl.CostEstimate(
            flops=20 * rows * width, bytes_accessed=rows * width * 30, transcendentals=rows * width
        ),
    )(order, pre, prob, cotangent, *parts)


def make_shards(dp_size, etp_size):
    outer, inner = split_dp(dp_size)

    def over_outer(value, k):
        pairs = [(i, i ^ (k * inner)) for i in range(dp_size)]
        return lax.ppermute(value, "dp", pairs)

    def over_inner(value, j):
        pairs = [(i, i ^ j) for i in range(dp_size)]
        return lax.ppermute(value, "dp", pairs)

    def over_etp(value, e):
        pairs = [(i, i ^ e) for i in range(etp_size)]
        return lax.ppermute(value, "etp", pairs)

    chunk_order = [0]
    bit = etp_size // 2
    bits = []
    while bit:
        bits.append(bit)
        chunk_order = chunk_order + [c ^ bit for c in chunk_order]
        bit //= 2

    def gather_etp(value, ties=()):
        for i, b in enumerate(bits):
            value = after(value, *ties[i]) if i < len(ties) else value
            value = jnp.concatenate([value, over_etp(value, b)], axis=0)
        return value

    def reduce_etp(values, last=()):
        for b in reversed(bits):
            half = values[0].shape[0] // 2
            leaving = [value[half:].astype(BF16) for value in values]
            leaving = jnp.concatenate(leaving, axis=0) if len(leaving) > 1 else leaving[0]
            got = over_etp(behind(leaving, *last) if last and b == bits[0] else leaving, b)
            values = [v[:half] + got[i * half : (i + 1) * half].astype(F32) for i, v in enumerate(values)]
        return [value.astype(BF16) for value in values]

    near_first = sorted(range(1, outer))
    far_first = near_first[::-1]
    keys = [0] + near_first
    relay = outer == 4

    def outer_pairs(value, pairs):
        pairs = [(s * inner + i, t * inner + i) for s, t in pairs for i in range(inner)]
        return lax.ppermute(value, "dp", pairs)

    swap = [(0, 1), (1, 0), (2, 3), (3, 2)]
    cycle = [(0, 2), (2, 3), (3, 1), (1, 0)]
    back = [(t, s) for s, t in cycle]
    middle = [(1, 2), (2, 1)]
    inward = [(0, 2), (3, 1)]
    outward = [(2, 0), (1, 3)]

    def shards(tokens, slots, gate_probs, w_gate, w_up, d_hidden):
        dp = lax.axis_index("dp")
        etp = lax.axis_index("etp")
        a, b = dp // inner, dp % inner
        at_end = (a == 0) | (a == outer - 1)
        depth, width = w_gate.shape
        cap = slots.shape[0]
        tok = tokens.shape[0]
        span = depth * inner

        def pick(first, second):
            return jnp.where(at_end, first, second)

        weights = [jnp.concatenate([w_gate, w_up], axis=1)]
        for j in range(1, inner):
            weights.append(jnp.concatenate([over_inner(w_gate, j), over_inner(w_up, j)], axis=1))
        weights = jnp.concatenate(weights, axis=0)

        onehot = (slots[:, None] == jnp.arange(tok, dtype=slots.dtype)[None, :]).astype(BF16)
        rows = jnp.dot(onehot, tokens, preferred_element_type=F32).astype(BF16)
        pieces = {}
        for k in keys:
            blocks = [
                lax.dynamic_slice(rows, (0, (a ^ k) * span + (b ^ j) * depth), (cap, depth))
                for j in range(inner)
            ]
            pieces[k] = jnp.concatenate(blocks, axis=1)
        got = {k: over_outer(pieces[k], k) for k in far_first}
        if relay:
            got[3], got[1] = pick(got[3], got[1]), pick(got[1], got[3])
        got[0] = pieces[0]

        x_chunks = {}

        def multiply(k, *ties):
            x_chunks[k] = after(x_chunks[k], *ties)
            return jnp.dot(x_chunks[k], weights, preferred_element_type=F32)

        if relay:
            x_chunks[1] = gather_etp(got[1])
            x_chunks[3] = gather_etp(got[3])
            near = multiply(1).astype(BF16)
            crossed = outer_pairs(near, middle)
            far = after(multiply(3, near).astype(BF16), near)
            swapped = outer_pairs(far, swap)
            x_chunks[2] = gather_etp(got[2], [[], [far]])
            x_chunks[0] = gather_etp(after(got[0], far))
            two = after(multiply(2, swapped, crossed), swapped)
            inwards = outer_pairs(two.astype(BF16), inward)
            relayed = pick(near, (after(two, swapped) + swapped.astype(F32)).astype(BF16))
            cycled = outer_pairs(relayed, back)
            own = multiply(0, relayed) + crossed.astype(F32) + inwards.astype(F32)
            own = own + jnp.where(at_end, swapped.astype(F32), 0.0)
            parts = [cycled]
            last = relayed
        else:
            last, parts = rows, []
            x_chunks[0] = gather_etp(got[0])
            for k in far_first:
                x_chunks[k] = gather_etp(got[k], [[last]])
                last = multiply(k).astype(BF16)
                parts.append(over_outer(last, k))
            own = multiply(0, last)
        probs = gather_etp(after(gate_probs, rows))
        order = etp ^ jnp.array(chunk_order, jnp.int32)
        hidden, paired = gate_call(order, own, probs[:, None], d_hidden, parts)

        grads, sums = {0: paired}, {}

        def advance(ks, last, before=()):
            partials = [
                lax.dot_general(
                    after(grads[k], last), weights, (((1,), (1,)), ((), ())), preferred_element_type=F32
                )
                for k in ks
            ]
            sums.update(zip(ks, reduce_etp(partials, before)))
            return partials[-1]

        def weight_grad(ks, j, last):
            x_part = jnp.concatenate([x_chunks[k][:, j * depth : (j + 1) * depth] for k in ks], axis=0)
            grad_part = jnp.concatenate([grads[k] for k in ks], axis=0)
            return lax.dot_general(
                x_part, after(grad_part, last), (((0,), (0,)), ((), ())), preferred_element_type=F32
            )

        if relay:
            cycled = outer_pairs(paired, cycle)
            last = advance([0], paired)
            crossed = outer_pairs(after(paired, last), middle)
            outwards = outer_pairs(after(paired, last), outward)
            turn = after(pick(paired, cycled), paired)
            grads[3] = outer_pairs(turn, swap)
            grads[2] = pick(outwards, after(cycled, turn))
            grads[1] = pick(after(cycled, grads[2]), crossed)
            sequence = [0, 2, 3, 1]
            early, late = [0, 2], [3, 1]
            last = turn
        else:
            for k in near_first:
                grads[k] = over_outer(paired, k)
            sequence = keys
            early, late = keys[: max(outer - 1, 1)], keys[max(outer - 1, 1) :]
            last = grads[near_first[0]] if outer > 1 else paired
        for k in early:
            last = advance([k], last) if k not in sums else last

        leaving = []
        for j in range(1, inner):
            value = weight_grad(early, j, last)
            if late:
                value = after(value, last) + weight_grad(late, j, value)
            leaving.append(value.astype(BF16))
        arriving = [over_inner(leaving[j - 1], j) for j in range(1, inner)]
        last = leaving[0] if inner > 1 else last
        if late:
            last = advance(late, last, [sums[k] for k in early[1:]])
        total = weight_grad(sequence, 0, last)
        gate_total, up_total = total[:, :width], total[:, width:]
        for part in arriving:
            gate_total = gate_total + part[:, :width].astype(F32)
            up_total = up_total + part[:, width:].astype(F32)

        last = sums[sequence[-1]]
        if relay:
            sums[3], sums[1] = pick(sums[3], sums[1]), pick(sums[1], sums[3])
        dx = jnp.zeros((cap, outer * span), BF16)
        for k in keys:
            own = over_outer(sums[k], k) if k else sums[k]
            if k != sequence[-1]:
                own = after(own, last)
            for j in range(inner):
                block = own[:, j * depth : (j + 1) * depth]
                dx = lax.dynamic_update_slice(dx, block, (0, (a ^ k) * span + (b ^ j) * depth))
        grad_tokens = lax.dot_general(
            onehot, dx, (((0,), (0,)), ((), ())), preferred_element_type=F32
        ).astype(BF16)
        return (hidden, grad_tokens, gate_total, up_total)

    return shards


def solution(mesh):
    in_specs = (
        P(("dp", "etp"), None),
        P(("dp", "etp")),
        P(("dp", "etp")),
        P("dp", "etp"),
        P("dp", "etp"),
        P("dp", "etp"),
    )
    out_specs = (P("dp", "etp"), P(("dp", "etp"), None), P("dp", "etp"), P("dp", "etp"))
    shards = make_shards(mesh.shape["dp"], mesh.shape["etp"])
    return jax.shard_map(shards, mesh=mesh, in_specs=in_specs, out_specs=out_specs, check_vma=False)
```

```python
import functools

import jax
import jax.numpy as jnp
from jax import lax
from jax.experimental import pallas as pl
from jax.experimental.pallas import tpu as pltpu
from jax.sharding import PartitionSpec as P

F32 = jnp.float32
BF16 = jnp.bfloat16


def split_dp(dp):
    outer = 1
    while 4 * outer * outer <= 2 * dp:
        outer *= 2
    return outer, dp // outer


def after(value, *others):
    return lax.optimization_barrier((value,) + others)[0]


def behind(value, *others):
    anywhere = pl.BlockSpec(memory_space=pl.ANY)
    return pl.pallas_call(
        lambda *refs: None,
        out_shape=jax.ShapeDtypeStruct(value.shape, value.dtype),
        in_specs=[anywhere] * (1 + len(others)),
        out_specs=anywhere,
        input_output_aliases={0: 0},
        cost_estimate=pl.CostEstimate(flops=0, bytes_accessed=0, transcendentals=0),
    )(value, *others)


def gate_kernel(steps, order_ref, pre_ref, prob_ref, cot_ref, *refs):
    part_refs, (hidden_ref, grad_ref) = refs[:-2], refs[-2:]
    rows, width = cot_ref.shape
    cap = rows // steps
    for i in range(steps):
        here = pl.ds(i * cap, cap)
        there = pl.ds(pl.multiple_of(order_ref[i] * cap, cap), cap)
        total = pre_ref[here, :]
        for part_ref in part_refs:
            total = total + part_ref[here, :].astype(F32)
        gate, up = total[:, :width], total[:, width:]
        prob = prob_ref[here, :].astype(F32)
        sig = jax.nn.sigmoid(gate)
        act = gate * sig
        hidden_ref[there, :] = (prob * act * up).astype(BF16)
        scaled = cot_ref[there, :].astype(F32) * prob
        grad_ref[here, :width] = (scaled * up * sig * (1.0 + gate * (1.0 - sig))).astype(BF16)
        grad_ref[here, width:] = (scaled * act).astype(BF16)


def gate_call(order, pre, prob, cotangent, parts):
    rows, width = cotangent.shape
    steps = order.shape[0]
    vmem = pl.BlockSpec(memory_space=pltpu.VMEM)
    return pl.pallas_call(
        functools.partial(gate_kernel, steps),
        out_shape=(
            jax.ShapeDtypeStruct((rows, width), BF16),
            jax.ShapeDtypeStruct((rows, 2 * width), BF16),
        ),
        in_specs=[pl.BlockSpec(memory_space=pltpu.SMEM)] + [vmem] * (3 + len(parts)),
        out_specs=(vmem, vmem),
        compiler_params=pltpu.CompilerParams(vmem_limit_bytes=24 * 2**20),
        cost_estimate=pl.CostEstimate(
            flops=20 * rows * width, bytes_accessed=rows * width * 30, transcendentals=rows * width
        ),
    )(order, pre, prob, cotangent, *parts)


def make_shards(dp_size, etp_size):
    outer, inner = split_dp(dp_size)

    def over_outer(value, k):
        pairs = [(i, i ^ (k * inner)) for i in range(dp_size)]
        return lax.ppermute(value, "dp", pairs)

    def over_inner(value, j):
        pairs = [(i, i ^ j) for i in range(dp_size)]
        return lax.ppermute(value, "dp", pairs)

    def over_etp(value, e):
        pairs = [(i, i ^ e) for i in range(etp_size)]
        return lax.ppermute(value, "etp", pairs)

    chunk_order = [0]
    bit = etp_size // 2
    bits = []
    while bit:
        bits.append(bit)
        chunk_order = chunk_order + [c ^ bit for c in chunk_order]
        bit //= 2

    def gather_etp(value, ties=(), arrived=None):
        arrived = [] if arrived is None else arrived
        for i, b in enumerate(bits):
            value = after(value, *ties[i]) if i < len(ties) else value
            arrived.append(over_etp(value, b))
            value = jnp.concatenate([value, arrived[-1]], axis=0)
        return value

    def reduce_etp(*values):
        for b in reversed(bits):
            half = values[0].shape[0] // 2
            leaving = [value[half:].astype(BF16) for value in values]
            got = over_etp(jnp.concatenate(leaving, axis=0) if len(leaving) > 1 else leaving[0], b)
            values = [v[:half] + got[i * half : (i + 1) * half].astype(F32) for i, v in enumerate(values)]
        return [value.astype(BF16) for value in values]

    near_first = sorted(range(1, outer))
    far_first = near_first[::-1]
    keys = [0] + near_first
    relay = outer == 4

    def outer_pairs(value, pairs):
        pairs = [(s * inner + i, t * inner + i) for s, t in pairs for i in range(inner)]
        return lax.ppermute(value, "dp", pairs)

    swap = [(0, 1), (1, 0), (2, 3), (3, 2)]
    cycle = [(0, 2), (2, 3), (3, 1), (1, 0)]
    back = [(t, s) for s, t in cycle]
    middle = [(1, 2), (2, 1)]
    inward = [(0, 2), (3, 1)]
    outward = [(2, 0), (1, 3)]

    def shards(tokens, slots, gate_probs, w_gate, w_up, d_hidden):
        dp = lax.axis_index("dp")
        etp = lax.axis_index("etp")
        a, b = dp // inner, dp % inner
        at_end = (a == 0) | (a == outer - 1)
        depth, width = w_gate.shape
        cap = slots.shape[0]
        tok = tokens.shape[0]
        span = depth * inner

        def pick(first, second):
            return jnp.where(at_end, first, second)

        weights = [jnp.concatenate([w_gate, w_up], axis=1)]
        for j in range(1, inner):
            weights.append(jnp.concatenate([over_inner(w_gate, j), over_inner(w_up, j)], axis=1))
        weights = jnp.concatenate(weights, axis=0)

        onehot = (slots[:, None] == jnp.arange(tok, dtype=slots.dtype)[None, :]).astype(BF16)
        rows = jnp.dot(onehot, tokens, preferred_element_type=F32).astype(BF16)
        pieces = {}
        for k in keys:
            blocks = [
                lax.dynamic_slice(rows, (0, (a ^ k) * span + (b ^ j) * depth), (cap, depth))
                for j in range(inner)
            ]
            pieces[k] = jnp.concatenate(blocks, axis=1)
        got = {k: over_outer(pieces[k], k) for k in far_first}
        if relay:
            got[3], got[1] = pick(got[3], got[1]), pick(got[1], got[3])
        got[0] = jnp.concatenate(
            [pieces[0], jnp.broadcast_to(gate_probs[:, None], (cap, 128))], axis=1
        )

        x_chunks = {}

        def multiply(k, *ties):
            x_chunks[k] = after(x_chunks[k], *ties)
            return jnp.dot(x_chunks[k], weights, preferred_element_type=F32)

        if relay:
            arrived = []
            x_chunks[3] = gather_etp(got[3])
            x_chunks[1] = gather_etp(got[1], (), arrived)
            far = multiply(3).astype(BF16)
            swapped = outer_pairs(far, swap)
            near = after(multiply(1, far).astype(BF16), far)
            crossed = outer_pairs(near, middle)
            x_chunks[2] = gather_etp(got[2], [[], [near]])
            joined = gather_etp(behind(got[0], arrived[0]))
            x_chunks[0], probs = joined[:, :span], joined[:, span : span + 1]
            two = after(multiply(2, near), near)
            inwards = outer_pairs(two.astype(BF16), inward)
            relayed = pick(near, (after(two, swapped, crossed) + swapped.astype(F32)).astype(BF16))
            cycled = outer_pairs(relayed, back)
            own = multiply(0, relayed) + crossed.astype(F32) + inwards.astype(F32)
            own = own + jnp.where(at_end, swapped.astype(F32), 0.0)
            parts = [cycled]
            last = relayed
        else:
            last, parts = rows, []
            joined = gather_etp(got[0])
            x_chunks[0], probs = joined[:, :span], joined[:, span : span + 1]
            for k in far_first:
                x_chunks[k] = gather_etp(got[k], [[last]])
                last = multiply(k).astype(BF16)
                parts.append(over_outer(last, k))
            own = multiply(0, last)
        order = etp ^ jnp.array(chunk_order, jnp.int32)
        hidden, paired = gate_call(order, own, probs, d_hidden, parts)

        grads, sums = {0: paired}, {}

        def advance(ks, last):
            partials = [
                lax.dot_general(
                    after(grads[k], last), weights, (((1,), (1,)), ((), ())), preferred_element_type=F32
                )
                for k in ks
            ]
            sums.update(zip(ks, reduce_etp(*partials)))
            return partials[-1]

        def weight_grad(ks, j, last):
            x_part = jnp.concatenate([x_chunks[k][:, j * depth : (j + 1) * depth] for k in ks], axis=0)
            grad_part = jnp.concatenate([grads[k] for k in ks], axis=0)
            return lax.dot_general(
                x_part, after(grad_part, last), (((0,), (0,)), ((), ())), preferred_element_type=F32
            )

        if relay:
            cycled = outer_pairs(paired, cycle)
            last = advance([0], paired)
            crossed = outer_pairs(after(paired, last), middle)
            outwards = outer_pairs(after(paired, last), outward)
            turn = after(pick(paired, cycled), paired)
            grads[3] = outer_pairs(turn, swap)
            grads[2] = pick(outwards, after(cycled, turn))
            grads[1] = pick(after(cycled, grads[2]), crossed)
            sequence = [0, 2, 3, 1]
            early, late = [0, 2], [3, 1]
            last = turn
        else:
            for k in near_first:
                grads[k] = over_outer(paired, k)
            sequence = keys
            early, late = keys[: max(outer - 1, 1)], keys[max(outer - 1, 1) :]
            last = grads[near_first[0]] if outer > 1 else paired
        for k in early:
            last = advance([k], last) if k not in sums else last

        leaving = []
        for j in range(1, inner):
            value = weight_grad(early, j, last)
            if late:
                value = after(value, last) + weight_grad(late, j, value)
            leaving.append(value.astype(BF16))
        arriving = [over_inner(leaving[j - 1], j) for j in range(1, inner)]
        last = leaving[0] if inner > 1 else last
        if late:
            last = advance(late, last)
        total = weight_grad(sequence, 0, last)
        gate_total, up_total = total[:, :width], total[:, width:]
        for part in arriving:
            gate_total = gate_total + part[:, :width].astype(F32)
            up_total = up_total + part[:, width:].astype(F32)

        last = sums[sequence[-1]]
        if relay:
            sums[3], sums[1] = pick(sums[3], sums[1]), pick(sums[1], sums[3])
        dx = jnp.zeros((cap, outer * span), BF16)
        for k in keys:
            own = over_outer(sums[k], k) if k else sums[k]
            if k != sequence[-1]:
                own = after(own, last)
            for j in range(inner):
                block = own[:, j * depth : (j + 1) * depth]
                dx = lax.dynamic_update_slice(dx, block, (0, (a ^ k) * span + (b ^ j) * depth))
        grad_tokens = lax.dot_general(
            onehot, dx, (((0,), (0,)), ((), ())), preferred_element_type=F32
        ).astype(BF16)
        return (hidden, grad_tokens, gate_total, up_total)

    return shards


def solution(mesh):
    in_specs = (
        P(("dp", "etp"), None),
        P(("dp", "etp")),
        P(("dp", "etp")),
        P("dp", "etp"),
        P("dp", "etp"),
        P("dp", "etp"),
    )
    out_specs = (P("dp", "etp"), P(("dp", "etp"), None), P("dp", "etp"), P("dp", "etp"))
    shards = make_shards(mesh.shape["dp"], mesh.shape["etp"])
    return jax.shard_map(shards, mesh=mesh, in_specs=in_specs, out_specs=out_specs, check_vma=False)
```

```python
import functools

import jax
import jax.numpy as jnp
from jax import lax
from jax.experimental import pallas as pl
from jax.experimental.pallas import tpu as pltpu
from jax.sharding import PartitionSpec as P

F32 = jnp.float32
BF16 = jnp.bfloat16


def split_dp(dp):
    outer = 1
    while 4 * outer * outer <= 2 * dp:
        outer *= 2
    return outer, dp // outer


def after(value, *others):
    return lax.optimization_barrier((value,) + others)[0]


def behind(value, *others):
    anywhere = pl.BlockSpec(memory_space=pl.ANY)
    return pl.pallas_call(
        lambda *refs: None,
        out_shape=jax.ShapeDtypeStruct(value.shape, value.dtype),
        in_specs=[anywhere] * (1 + len(others)),
        out_specs=anywhere,
        input_output_aliases={0: 0},
        cost_estimate=pl.CostEstimate(flops=0, bytes_accessed=0, transcendentals=0),
    )(value, *others)


def gate_kernel(steps, order_ref, pre_ref, prob_ref, cot_ref, *refs):
    part_refs, (hidden_ref, grad_ref) = refs[:-2], refs[-2:]
    rows, width = cot_ref.shape
    cap = rows // steps
    for i in range(steps):
        here = pl.ds(i * cap, cap)
        there = pl.ds(pl.multiple_of(order_ref[i] * cap, cap), cap)
        total = pre_ref[here, :]
        for part_ref in part_refs:
            total = total + part_ref[here, :].astype(F32)
        gate, up = total[:, :width], total[:, width:]
        prob = prob_ref[here, :].astype(F32)
        sig = jax.nn.sigmoid(gate)
        act = gate * sig
        hidden_ref[there, :] = (prob * act * up).astype(BF16)
        scaled = cot_ref[there, :].astype(F32) * prob
        grad_ref[here, :width] = (scaled * up * sig * (1.0 + gate * (1.0 - sig))).astype(BF16)
        grad_ref[here, width:] = (scaled * act).astype(BF16)


def gate_call(order, pre, prob, cotangent, parts):
    rows, width = cotangent.shape
    steps = order.shape[0]
    vmem = pl.BlockSpec(memory_space=pltpu.VMEM)
    return pl.pallas_call(
        functools.partial(gate_kernel, steps),
        out_shape=(
            jax.ShapeDtypeStruct((rows, width), BF16),
            jax.ShapeDtypeStruct((rows, 2 * width), BF16),
        ),
        in_specs=[pl.BlockSpec(memory_space=pltpu.SMEM)] + [vmem] * (3 + len(parts)),
        out_specs=(vmem, vmem),
        compiler_params=pltpu.CompilerParams(vmem_limit_bytes=24 * 2**20),
        cost_estimate=pl.CostEstimate(
            flops=20 * rows * width, bytes_accessed=rows * width * 30, transcendentals=rows * width
        ),
    )(order, pre, prob, cotangent, *parts)


def make_shards(dp_size, etp_size):
    outer, inner = split_dp(dp_size)

    def over_outer(value, k):
        pairs = [(i, i ^ (k * inner)) for i in range(dp_size)]
        return lax.ppermute(value, "dp", pairs)

    def over_inner(value, j):
        pairs = [(i, i ^ j) for i in range(dp_size)]
        return lax.ppermute(value, "dp", pairs)

    def over_etp(value, e):
        pairs = [(i, i ^ e) for i in range(etp_size)]
        return lax.ppermute(value, "etp", pairs)

    chunk_order = [0]
    bit = etp_size // 2
    bits = []
    while bit:
        bits.append(bit)
        chunk_order = chunk_order + [c ^ bit for c in chunk_order]
        bit //= 2

    def gather_etp(value, ties=(), arrived=None):
        arrived = [] if arrived is None else arrived
        for i, b in enumerate(bits):
            value = after(value, *ties[i]) if i < len(ties) else value
            arrived.append(over_etp(value, b))
            value = jnp.concatenate([value, arrived[-1]], axis=0)
        return value

    def reduce_etp(*values):
        for b in reversed(bits):
            half = values[0].shape[0] // 2
            leaving = [value[half:].astype(BF16) for value in values]
            got = over_etp(jnp.concatenate(leaving, axis=0) if len(leaving) > 1 else leaving[0], b)
            values = [v[:half] + got[i * half : (i + 1) * half].astype(F32) for i, v in enumerate(values)]
        return [value.astype(BF16) for value in values]

    near_first = sorted(range(1, outer))
    far_first = near_first[::-1]
    keys = [0] + near_first
    relay = outer == 4

    def outer_pairs(value, pairs):
        pairs = [(s * inner + i, t * inner + i) for s, t in pairs for i in range(inner)]
        return lax.ppermute(value, "dp", pairs)

    swap = [(0, 1), (1, 0), (2, 3), (3, 2)]
    cycle = [(0, 2), (2, 3), (3, 1), (1, 0)]
    back = [(t, s) for s, t in cycle]
    middle = [(1, 2), (2, 1)]
    inward = [(0, 2), (3, 1)]
    outward = [(2, 0), (1, 3)]

    def shards(tokens, slots, gate_probs, w_gate, w_up, d_hidden):
        dp = lax.axis_index("dp")
        etp = lax.axis_index("etp")
        a, b = dp // inner, dp % inner
        at_end = (a == 0) | (a == outer - 1)
        depth, width = w_gate.shape
        cap = slots.shape[0]
        tok = tokens.shape[0]
        span = depth * inner

        def pick(first, second):
            return jnp.where(at_end, first, second)

        weights = [jnp.concatenate([w_gate, w_up], axis=1)]
        for j in range(1, inner):
            weights.append(jnp.concatenate([over_inner(w_gate, j), over_inner(w_up, j)], axis=1))
        weights = jnp.concatenate(weights, axis=0)

        onehot = (slots[:, None] == jnp.arange(tok, dtype=slots.dtype)[None, :]).astype(BF16)
        rows = jnp.dot(onehot, tokens, preferred_element_type=F32).astype(BF16)
        pieces = {}
        for k in keys:
            blocks = [
                lax.dynamic_slice(rows, (0, (a ^ k) * span + (b ^ j) * depth), (cap, depth))
                for j in range(inner)
            ]
            pieces[k] = jnp.concatenate(blocks, axis=1)
        got = {k: over_outer(pieces[k], k) for k in far_first}
        if relay:
            got[3], got[1] = pick(got[3], got[1]), pick(got[1], got[3])
        got[0] = jnp.concatenate(
            [pieces[0], jnp.broadcast_to(gate_probs[:, None], (cap, 128))], axis=1
        )

        x_chunks = {}

        def multiply(k, *ties):
            x_chunks[k] = after(x_chunks[k], *ties)
            return jnp.dot(x_chunks[k], weights, preferred_element_type=F32)

        if relay:
            arrived = []
            x_chunks[3] = gather_etp(got[3])
            x_chunks[1] = gather_etp(got[1], (), arrived)
            far = multiply(3).astype(BF16)
            swapped = outer_pairs(far, swap)
            near = after(multiply(1, far).astype(BF16), far)
            crossed = outer_pairs(near, middle)
            x_chunks[2] = gather_etp(got[2], [[], [near]])
            joined = gather_etp(behind(got[0], arrived[0]))
            x_chunks[0], probs = joined[:, :span], joined[:, span : span + 1]
            two = after(multiply(2, near), near)
            inwards = outer_pairs(two.astype(BF16), inward)
            relayed = pick(near, (after(two, swapped) + swapped.astype(F32)).astype(BF16))
            cycled = outer_pairs(relayed, back)
            own = multiply(0, relayed) + crossed.astype(F32) + inwards.astype(F32)
            own = own + jnp.where(at_end, swapped.astype(F32), 0.0)
            parts = [cycled]
            last = relayed
        else:
            last, parts = rows, []
            joined = gather_etp(got[0])
            x_chunks[0], probs = joined[:, :span], joined[:, span : span + 1]
            for k in far_first:
                x_chunks[k] = gather_etp(got[k], [[last]])
                last = multiply(k).astype(BF16)
                parts.append(over_outer(last, k))
            own = multiply(0, last)
        order = etp ^ jnp.array(chunk_order, jnp.int32)
        hidden, paired = gate_call(order, own, probs, d_hidden, parts)

        grads, sums = {0: paired}, {}

        def advance(ks, last):
            partials = [
                lax.dot_general(
                    after(grads[k], last), weights, (((1,), (1,)), ((), ())), preferred_element_type=F32
                )
                for k in ks
            ]
            sums.update(zip(ks, reduce_etp(*partials)))
            return partials[-1]

        def weight_grad(ks, j, last):
            x_part = jnp.concatenate([x_chunks[k][:, j * depth : (j + 1) * depth] for k in ks], axis=0)
            grad_part = jnp.concatenate([grads[k] for k in ks], axis=0)
            return lax.dot_general(
                x_part, after(grad_part, last), (((0,), (0,)), ((), ())), preferred_element_type=F32
            )

        if relay:
            cycled = outer_pairs(paired, cycle)
            last = advance([0], paired)
            crossed = outer_pairs(after(paired, last), middle)
            outwards = outer_pairs(after(paired, last), outward)
            turn = after(pick(paired, cycled), paired)
            grads[3] = outer_pairs(turn, swap)
            grads[2] = pick(outwards, after(cycled, turn))
            grads[1] = pick(after(cycled, grads[2]), crossed)
            sequence = [0, 2, 3, 1]
            early, late = [0, 2], [3, 1]
            last = turn
        else:
            for k in near_first:
                grads[k] = over_outer(paired, k)
            sequence = keys
            early, late = keys[: max(outer - 1, 1)], keys[max(outer - 1, 1) :]
            last = grads[near_first[0]] if outer > 1 else paired
        for k in early:
            last = advance([k], last) if k not in sums else last

        leaving = []
        for j in range(1, inner):
            value = weight_grad(early, j, last)
            if late:
                value = after(value, last) + weight_grad(late, j, value)
            leaving.append(value.astype(BF16))
        arriving = [over_inner(leaving[j - 1], j) for j in range(1, inner)]
        last = leaving[0] if inner > 1 else last
        if late:
            last = advance(late, last)
        total = weight_grad(sequence, 0, last)
        gate_total, up_total = total[:, :width], total[:, width:]
        for part in arriving:
            gate_total = gate_total + part[:, :width].astype(F32)
            up_total = up_total + part[:, width:].astype(F32)

        last = sums[sequence[-1]]
        if relay:
            sums[3], sums[1] = pick(sums[3], sums[1]), pick(sums[1], sums[3])
        dx = jnp.zeros((cap, outer * span), BF16)
        for k in keys:
            own = over_outer(sums[k], k) if k else sums[k]
            if k != sequence[-1]:
                own = after(own, last)
            for j in range(inner):
                block = own[:, j * depth : (j + 1) * depth]
                dx = lax.dynamic_update_slice(dx, block, (0, (a ^ k) * span + (b ^ j) * depth))
        grad_tokens = lax.dot_general(
            onehot, dx, (((0,), (0,)), ((), ())), preferred_element_type=F32
        ).astype(BF16)
        return (hidden, grad_tokens, gate_total, up_total)

    return shards


def solution(mesh):
    in_specs = (
        P(("dp", "etp"), None),
        P(("dp", "etp")),
        P(("dp", "etp")),
        P("dp", "etp"),
        P("dp", "etp"),
        P("dp", "etp"),
    )
    out_specs = (P("dp", "etp"), P(("dp", "etp"), None), P("dp", "etp"), P("dp", "etp"))
    shards = make_shards(mesh.shape["dp"], mesh.shape["etp"])
    return jax.shard_map(shards, mesh=mesh, in_specs=in_specs, out_specs=out_specs, check_vma=False)
```

```python
import functools

import jax
import jax.numpy as jnp
from jax import lax
from jax.experimental import pallas as pl
from jax.experimental.pallas import tpu as pltpu
from jax.sharding import PartitionSpec as P

F32 = jnp.float32
BF16 = jnp.bfloat16


def split_dp(dp):
    outer = 1
    while 4 * outer * outer <= 2 * dp:
        outer *= 2
    return outer, dp // outer


def after(value, *others):
    return lax.optimization_barrier((value,) + others)[0]


def gate_kernel(steps, order_ref, pre_ref, prob_ref, cot_ref, *refs):
    part_refs, (hidden_ref, grad_ref) = refs[:-2], refs[-2:]
    rows, width = cot_ref.shape
    cap = rows // steps
    for i in range(steps):
        here = pl.ds(i * cap, cap)
        there = pl.ds(pl.multiple_of(order_ref[i] * cap, cap), cap)
        total = pre_ref[here, :]
        for part_ref in part_refs:
            total = total + part_ref[here, :].astype(F32)
        gate, up = total[:, :width], total[:, width:]
        prob = prob_ref[here, :].astype(F32)
        sig = jax.nn.sigmoid(gate)
        act = gate * sig
        hidden_ref[there, :] = (prob * act * up).astype(BF16)
        scaled = cot_ref[there, :].astype(F32) * prob
        grad_ref[here, :width] = (scaled * up * sig * (1.0 + gate * (1.0 - sig))).astype(BF16)
        grad_ref[here, width:] = (scaled * act).astype(BF16)


def gate_call(order, pre, prob, cotangent, parts):
    rows, width = cotangent.shape
    steps = order.shape[0]
    vmem = pl.BlockSpec(memory_space=pltpu.VMEM)
    return pl.pallas_call(
        functools.partial(gate_kernel, steps),
        out_shape=(
            jax.ShapeDtypeStruct((rows, width), BF16),
            jax.ShapeDtypeStruct((rows, 2 * width), BF16),
        ),
        in_specs=[pl.BlockSpec(memory_space=pltpu.SMEM)] + [vmem] * (3 + len(parts)),
        out_specs=(vmem, vmem),
        compiler_params=pltpu.CompilerParams(vmem_limit_bytes=24 * 2**20),
        cost_estimate=pl.CostEstimate(
            flops=20 * rows * width, bytes_accessed=rows * width * 30, transcendentals=rows * width
        ),
    )(order, pre, prob, cotangent, *parts)


def make_shards(dp_size, etp_size):
    outer, inner = split_dp(dp_size)

    def over_outer(value, k):
        pairs = [(i, i ^ (k * inner)) for i in range(dp_size)]
        return lax.ppermute(value, "dp", pairs)

    def over_inner(value, j):
        pairs = [(i, i ^ j) for i in range(dp_size)]
        return lax.ppermute(value, "dp", pairs)

    def over_etp(value, e):
        pairs = [(i, i ^ e) for i in range(etp_size)]
        return lax.ppermute(value, "etp", pairs)

    chunk_order = [0]
    bit = etp_size // 2
    bits = []
    while bit:
        bits.append(bit)
        chunk_order = chunk_order + [c ^ bit for c in chunk_order]
        bit //= 2

    def gather_etp(value, ties=()):
        for i, b in enumerate(bits):
            value = after(value, *ties[i]) if i < len(ties) else value
            value = jnp.concatenate([value, over_etp(value, b)], axis=0)
        return value

    def reduce_etp(*values):
        for b in reversed(bits):
            half = values[0].shape[0] // 2
            leaving = [value[half:].astype(BF16) for value in values]
            got = over_etp(jnp.concatenate(leaving, axis=0) if len(leaving) > 1 else leaving[0], b)
            values = [v[:half] + got[i * half : (i + 1) * half].astype(F32) for i, v in enumerate(values)]
        return [value.astype(BF16) for value in values]

    near_first = sorted(range(1, outer))
    far_first = near_first[::-1]
    keys = [0] + near_first
    relay = outer == 4

    def outer_pairs(value, pairs):
        pairs = [(s * inner + i, t * inner + i) for s, t in pairs for i in range(inner)]
        return lax.ppermute(value, "dp", pairs)

    swap = [(0, 1), (1, 0), (2, 3), (3, 2)]
    cycle = [(0, 2), (2, 3), (3, 1), (1, 0)]
    back = [(t, s) for s, t in cycle]
    middle = [(1, 2), (2, 1)]
    inward = [(0, 2), (3, 1)]
    outward = [(2, 0), (1, 3)]

    def shards(tokens, slots, gate_probs, w_gate, w_up, d_hidden):
        dp = lax.axis_index("dp")
        etp = lax.axis_index("etp")
        a, b = dp // inner, dp % inner
        at_end = (a == 0) | (a == outer - 1)
        depth, width = w_gate.shape
        cap = slots.shape[0]
        tok = tokens.shape[0]
        span = depth * inner

        def pick(first, second):
            return jnp.where(at_end, first, second)

        weights = [jnp.concatenate([w_gate, w_up], axis=1)]
        for j in range(1, inner):
            weights.append(jnp.concatenate([over_inner(w_gate, j), over_inner(w_up, j)], axis=1))
        weights = jnp.concatenate(weights, axis=0)

        onehot = (slots[:, None] == jnp.arange(tok, dtype=slots.dtype)[None, :]).astype(BF16)
        rows = jnp.dot(onehot, tokens, preferred_element_type=F32).astype(BF16)
        pieces = {}
        for k in keys:
            blocks = [
                lax.dynamic_slice(rows, (0, (a ^ k) * span + (b ^ j) * depth), (cap, depth))
                for j in range(inner)
            ]
            pieces[k] = jnp.concatenate(blocks, axis=1)
        got = {k: over_outer(pieces[k], k) for k in far_first}
        if relay:
            got[3], got[1] = pick(got[3], got[1]), pick(got[1], got[3])
        got[0] = pieces[0]

        x_chunks = {}

        def multiply(k, *ties):
            x_chunks[k] = after(x_chunks[k], *ties)
            return jnp.dot(x_chunks[k], weights, preferred_element_type=F32)

        if relay:
            x_chunks[3] = gather_etp(got[3])
            x_chunks[1] = gather_etp(got[1])
            far = multiply(3).astype(BF16)
            swapped = outer_pairs(far, swap)
            near = after(multiply(1, far).astype(BF16), far)
            crossed = outer_pairs(near, middle)
            x_chunks[2] = gather_etp(got[2], [[], [near]])
            x_chunks[0] = gather_etp(after(got[0], near))
            two = after(multiply(2, swapped), swapped)
            inwards = outer_pairs(two.astype(BF16), inward)
            relayed = pick(near, (after(two, swapped) + swapped.astype(F32)).astype(BF16))
            cycled = outer_pairs(relayed, back)
            own = multiply(0, relayed) + crossed.astype(F32) + inwards.astype(F32)
            own = own + jnp.where(at_end, swapped.astype(F32), 0.0)
            parts = [cycled]
            last = relayed
        else:
            last, parts = rows, []
            x_chunks[0] = gather_etp(got[0])
            for k in far_first:
                x_chunks[k] = gather_etp(got[k], [[last]])
                last = multiply(k).astype(BF16)
                parts.append(over_outer(last, k))
            own = multiply(0, last)
        probs = gather_etp(after(gate_probs, rows))
        order = etp ^ jnp.array(chunk_order, jnp.int32)
        hidden, paired = gate_call(order, own, probs[:, None], d_hidden, parts)

        grads, sums = {0: paired}, {}

        def advance(ks, last):
            partials = [
                lax.dot_general(
                    after(grads[k], last), weights, (((1,), (1,)), ((), ())), preferred_element_type=F32
                )
                for k in ks
            ]
            sums.update(zip(ks, reduce_etp(*partials)))
            return partials[-1]

        def weight_grad(ks, j, last):
            x_part = jnp.concatenate([x_chunks[k][:, j * depth : (j + 1) * depth] for k in ks], axis=0)
            grad_part = jnp.concatenate([grads[k] for k in ks], axis=0)
            return lax.dot_general(
                x_part, after(grad_part, last), (((0,), (0,)), ((), ())), preferred_element_type=F32
            )

        if relay:
            cycled = outer_pairs(paired, cycle)
            last = advance([0], paired)
            crossed = outer_pairs(after(paired, last), middle)
            outwards = outer_pairs(after(paired, last), outward)
            turn = after(pick(paired, cycled), paired)
            grads[3] = outer_pairs(turn, swap)
            grads[2] = pick(outwards, after(cycled, turn))
            grads[1] = pick(after(cycled, grads[2]), crossed)
            sequence = [0, 2, 3, 1]
            early, late = [0, 2], [3, 1]
            last = turn
        else:
            for k in near_first:
                grads[k] = over_outer(paired, k)
            sequence = keys
            early, late = keys[: max(outer - 1, 1)], keys[max(outer - 1, 1) :]
            last = grads[near_first[0]] if outer > 1 else paired
        for k in early:
            last = advance([k], last) if k not in sums else last

        leaving = []
        for j in range(1, inner):
            value = weight_grad(early, j, last)
            if late:
                value = after(value, last) + weight_grad(late, j, value)
            leaving.append(value.astype(BF16))
        arriving = [over_inner(leaving[j - 1], j) for j in range(1, inner)]
        last = leaving[0] if inner > 1 else last
        if late:
            last = advance(late, last)
        total = weight_grad(sequence, 0, last)
        gate_total, up_total = total[:, :width], total[:, width:]
        for part in arriving:
            gate_total = gate_total + part[:, :width].astype(F32)
            up_total = up_total + part[:, width:].astype(F32)

        last = sums[sequence[-1]]
        if relay:
            sums[3], sums[1] = pick(sums[3], sums[1]), pick(sums[1], sums[3])
        dx = jnp.zeros((cap, outer * span), BF16)
        for k in keys:
            own = over_outer(sums[k], k) if k else sums[k]
            if k != sequence[-1]:
                own = after(own, last)
            for j in range(inner):
                block = own[:, j * depth : (j + 1) * depth]
                dx = lax.dynamic_update_slice(dx, block, (0, (a ^ k) * span + (b ^ j) * depth))
        grad_tokens = lax.dot_general(
            onehot, dx, (((0,), (0,)), ((), ())), preferred_element_type=F32
        ).astype(BF16)
        return (hidden, grad_tokens, gate_total, up_total)

    return shards


def solution(mesh):
    in_specs = (
        P(("dp", "etp"), None),
        P(("dp", "etp")),
        P(("dp", "etp")),
        P("dp", "etp"),
        P("dp", "etp"),
        P("dp", "etp"),
    )
    out_specs = (P("dp", "etp"), P(("dp", "etp"), None), P("dp", "etp"), P("dp", "etp"))
    shards = make_shards(mesh.shape["dp"], mesh.shape["etp"])
    return jax.shard_map(shards, mesh=mesh, in_specs=in_specs, out_specs=out_specs, check_vma=False)
```

```python
import functools

import jax
import jax.numpy as jnp
from jax import lax
from jax.experimental import pallas as pl
from jax.experimental.pallas import tpu as pltpu
from jax.sharding import PartitionSpec as P

F32 = jnp.float32
BF16 = jnp.bfloat16


def split_dp(dp):
    outer = 1
    while 4 * outer * outer <= 2 * dp:
        outer *= 2
    return outer, dp // outer


def after(value, *others):
    return lax.optimization_barrier((value,) + others)[0]


def gate_kernel(steps, order_ref, pre_ref, prob_ref, cot_ref, *refs):
    part_refs, (hidden_ref, grad_ref) = refs[:-2], refs[-2:]
    rows, width = cot_ref.shape
    cap = rows // steps
    for i in range(steps):
        here = pl.ds(i * cap, cap)
        there = pl.ds(pl.multiple_of(order_ref[i] * cap, cap), cap)
        total = pre_ref[here, :]
        for part_ref in part_refs:
            total = total + part_ref[here, :].astype(F32)
        gate, up = total[:, :width], total[:, width:]
        prob = prob_ref[here, :].astype(F32)
        sig = jax.nn.sigmoid(gate)
        act = gate * sig
        hidden_ref[there, :] = (prob * act * up).astype(BF16)
        scaled = cot_ref[there, :].astype(F32) * prob
        grad_ref[here, :width] = (scaled * up * sig * (1.0 + gate * (1.0 - sig))).astype(BF16)
        grad_ref[here, width:] = (scaled * act).astype(BF16)


def gate_call(order, pre, prob, cotangent, parts):
    rows, width = cotangent.shape
    steps = order.shape[0]
    vmem = pl.BlockSpec(memory_space=pltpu.VMEM)
    return pl.pallas_call(
        functools.partial(gate_kernel, steps),
        out_shape=(
            jax.ShapeDtypeStruct((rows, width), BF16),
            jax.ShapeDtypeStruct((rows, 2 * width), BF16),
        ),
        in_specs=[pl.BlockSpec(memory_space=pltpu.SMEM)] + [vmem] * (3 + len(parts)),
        out_specs=(vmem, vmem),
        compiler_params=pltpu.CompilerParams(vmem_limit_bytes=24 * 2**20),
        cost_estimate=pl.CostEstimate(
            flops=20 * rows * width, bytes_accessed=rows * width * 30, transcendentals=rows * width
        ),
    )(order, pre, prob, cotangent, *parts)


def make_shards(dp_size, etp_size):
    outer, inner = split_dp(dp_size)

    def over_outer(value, k):
        pairs = [(i, i ^ (k * inner)) for i in range(dp_size)]
        return lax.ppermute(value, "dp", pairs)

    def over_inner(value, j):
        pairs = [(i, i ^ j) for i in range(dp_size)]
        return lax.ppermute(value, "dp", pairs)

    def over_etp(value, e):
        pairs = [(i, i ^ e) for i in range(etp_size)]
        return lax.ppermute(value, "etp", pairs)

    chunk_order = [0]
    bit = etp_size // 2
    bits = []
    while bit:
        bits.append(bit)
        chunk_order = chunk_order + [c ^ bit for c in chunk_order]
        bit //= 2

    def gather_etp(value, ties=()):
        for i, b in enumerate(bits):
            value = after(value, *ties[i]) if i < len(ties) else value
            value = jnp.concatenate([value, over_etp(value, b)], axis=0)
        return value

    def reduce_etp(*values):
        for b in reversed(bits):
            half = values[0].shape[0] // 2
            leaving = [value[half:].astype(BF16) for value in values]
            got = over_etp(jnp.concatenate(leaving, axis=0) if len(leaving) > 1 else leaving[0], b)
            values = [v[:half] + got[i * half : (i + 1) * half].astype(F32) for i, v in enumerate(values)]
        return [value.astype(BF16) for value in values]

    near_first = sorted(range(1, outer))
    far_first = near_first[::-1]
    keys = [0] + near_first
    relay = outer == 4

    def outer_pairs(value, pairs):
        pairs = [(s * inner + i, t * inner + i) for s, t in pairs for i in range(inner)]
        return lax.ppermute(value, "dp", pairs)

    swap = [(0, 1), (1, 0), (2, 3), (3, 2)]
    cycle = [(0, 2), (2, 3), (3, 1), (1, 0)]
    back = [(t, s) for s, t in cycle]
    middle = [(1, 2), (2, 1)]
    inward = [(0, 2), (3, 1)]
    outward = [(2, 0), (1, 3)]

    def shards(tokens, slots, gate_probs, w_gate, w_up, d_hidden):
        dp = lax.axis_index("dp")
        etp = lax.axis_index("etp")
        a, b = dp // inner, dp % inner
        at_end = (a == 0) | (a == outer - 1)
        depth, width = w_gate.shape
        cap = slots.shape[0]
        tok = tokens.shape[0]
        span = depth * inner

        def pick(first, second):
            return jnp.where(at_end, first, second)

        weights = [jnp.concatenate([w_gate, w_up], axis=1)]
        for j in range(1, inner):
            weights.append(jnp.concatenate([over_inner(w_gate, j), over_inner(w_up, j)], axis=1))
        weights = jnp.concatenate(weights, axis=0)

        onehot = (slots[:, None] == jnp.arange(tok, dtype=slots.dtype)[None, :]).astype(BF16)
        rows = jnp.dot(onehot, tokens, preferred_element_type=F32).astype(BF16)
        pieces = {}
        for k in keys:
            blocks = [
                lax.dynamic_slice(rows, (0, (a ^ k) * span + (b ^ j) * depth), (cap, depth))
                for j in range(inner)
            ]
            pieces[k] = jnp.concatenate(blocks, axis=1)
        got = {k: over_outer(pieces[k], k) for k in far_first}
        if relay:
            got[3], got[1] = pick(got[3], got[1]), pick(got[1], got[3])
        got[0] = pieces[0]

        x_chunks = {}

        def multiply(k, *ties):
            x_chunks[k] = after(x_chunks[k], *ties)
            return jnp.dot(x_chunks[k], weights, preferred_element_type=F32)

        if relay:
            x_chunks[3] = gather_etp(got[3])
            x_chunks[1] = gather_etp(got[1])
            far = multiply(3).astype(BF16)
            swapped = outer_pairs(far, swap)
            near = after(multiply(1, far).astype(BF16), far)
            crossed = outer_pairs(near, middle)
            x_chunks[2] = gather_etp(got[2], [[], [near]])
            x_chunks[0] = gather_etp(after(got[0], near))
            two = after(multiply(2, swapped), swapped)
            inwards = outer_pairs(two.astype(BF16), inward)
            relayed = pick(near, (after(two, swapped) + swapped.astype(F32)).astype(BF16))
            cycled = outer_pairs(relayed, back)
            own = multiply(0, relayed) + crossed.astype(F32) + inwards.astype(F32)
            own = own + jnp.where(at_end, swapped.astype(F32), 0.0)
            parts = [cycled]
            last = relayed
        else:
            last, parts = rows, []
            x_chunks[0] = gather_etp(got[0])
            for k in far_first:
                x_chunks[k] = gather_etp(got[k], [[last]])
                last = multiply(k).astype(BF16)
                parts.append(over_outer(last, k))
            own = multiply(0, last)
        probs = gather_etp(after(gate_probs, rows))
        order = etp ^ jnp.array(chunk_order, jnp.int32)
        hidden, paired = gate_call(order, own, probs[:, None], d_hidden, parts)

        grads, sums = {0: paired}, {}

        def advance(ks, last):
            partials = [
                lax.dot_general(
                    after(grads[k], last), weights, (((1,), (1,)), ((), ())), preferred_element_type=F32
                )
                for k in ks
            ]
            sums.update(zip(ks, reduce_etp(*partials)))
            return partials[-1]

        def weight_grad(ks, j, last):
            x_part = jnp.concatenate([x_chunks[k][:, j * depth : (j + 1) * depth] for k in ks], axis=0)
            grad_part = jnp.concatenate([grads[k] for k in ks], axis=0)
            return lax.dot_general(
                x_part, after(grad_part, last), (((0,), (0,)), ((), ())), preferred_element_type=F32
            )

        if relay:
            cycled = outer_pairs(paired, cycle)
            last = advance([0], paired)
            crossed = outer_pairs(after(paired, last), middle)
            outwards = outer_pairs(after(paired, last), outward)
            turn = after(pick(paired, cycled), paired)
            grads[3] = outer_pairs(turn, swap)
            grads[2] = pick(outwards, after(cycled, turn))
            grads[1] = pick(after(cycled, grads[2]), crossed)
            sequence = [0, 2, 3, 1]
            early, late = [0, 2], [3, 1]
            last = turn
        else:
            for k in near_first:
                grads[k] = over_outer(paired, k)
            sequence = keys
            early, late = keys[: max(outer - 1, 1)], keys[max(outer - 1, 1) :]
            last = grads[near_first[0]] if outer > 1 else paired
        for k in early:
            last = advance([k], last) if k not in sums else last

        leaving = []
        for j in range(1, inner):
            value = weight_grad(early, j, last)
            if late:
                value = after(value, last) + weight_grad(late, j, value)
            leaving.append(value.astype(BF16))
        arriving = [over_inner(leaving[j - 1], j) for j in range(1, inner)]
        last = leaving[0] if inner > 1 else last
        if late:
            last = advance(late, after(last, *[sums[k] for k in early]))
        total = weight_grad(sequence, 0, last)
        last = sums[sequence[-1]]
        returned = {0: sums[0]}
        if relay:
            returned[2] = over_outer(sums[2], 2)
            sums[3], sums[1] = pick(sums[3], sums[1]), pick(sums[1], sums[3])
            sums[3], sums[1] = after(sums[3], returned[2]), after(sums[1], returned[2])
        dx = jnp.zeros((cap, outer * span), BF16)
        for k in keys:
            own = returned[k] if k in returned else over_outer(sums[k], k)
            if k != sequence[-1]:
                own = after(own, last)
            for j in range(inner):
                block = own[:, j * depth : (j + 1) * depth]
                dx = lax.dynamic_update_slice(dx, block, (0, (a ^ k) * span + (b ^ j) * depth))
        grad_tokens = lax.dot_general(
            onehot, dx, (((0,), (0,)), ((), ())), preferred_element_type=F32
        ).astype(BF16)
        gate_total, up_total = total[:, :width], total[:, width:]
        for part in arriving:
            part = after(part, grad_tokens)
            gate_total = gate_total + part[:, :width].astype(F32)
            up_total = up_total + part[:, width:].astype(F32)
        return (hidden, grad_tokens, gate_total, up_total)

    return shards


def solution(mesh):
    in_specs = (
        P(("dp", "etp"), None),
        P(("dp", "etp")),
        P(("dp", "etp")),
        P("dp", "etp"),
        P("dp", "etp"),
        P("dp", "etp"),
    )
    out_specs = (P("dp", "etp"), P(("dp", "etp"), None), P("dp", "etp"), P("dp", "etp"))
    shards = make_shards(mesh.shape["dp"], mesh.shape["etp"])
    return jax.shard_map(shards, mesh=mesh, in_specs=in_specs, out_specs=out_specs, check_vma=False)
```

```python
import functools

import jax
import jax.numpy as jnp
from jax import lax
from jax.experimental import pallas as pl
from jax.experimental.pallas import tpu as pltpu
from jax.sharding import PartitionSpec as P

F32 = jnp.float32
BF16 = jnp.bfloat16


def split_dp(dp):
    outer = 1
    while 4 * outer * outer <= 2 * dp:
        outer *= 2
    return outer, dp // outer


def after(value, *others):
    return lax.optimization_barrier((value,) + others)[0]


def gate_kernel(steps, order_ref, pre_ref, prob_ref, cot_ref, *refs):
    part_refs, (hidden_ref, grad_ref) = refs[:-2], refs[-2:]
    rows, width = cot_ref.shape
    cap = rows // steps
    for i in range(steps):
        here = pl.ds(i * cap, cap)
        there = pl.ds(pl.multiple_of(order_ref[i] * cap, cap), cap)
        total = pre_ref[here, :]
        for part_ref in part_refs:
            total = total + part_ref[here, :].astype(F32)
        gate, up = total[:, :width], total[:, width:]
        prob = prob_ref[here, :].astype(F32)
        sig = jax.nn.sigmoid(gate)
        act = gate * sig
        hidden_ref[there, :] = (prob * act * up).astype(BF16)
        scaled = cot_ref[there, :].astype(F32) * prob
        grad_ref[here, :width] = (scaled * up * sig * (1.0 + gate * (1.0 - sig))).astype(BF16)
        grad_ref[here, width:] = (scaled * act).astype(BF16)


def gate_call(order, pre, prob, cotangent, parts):
    rows, width = cotangent.shape
    steps = order.shape[0]
    vmem = pl.BlockSpec(memory_space=pltpu.VMEM)
    return pl.pallas_call(
        functools.partial(gate_kernel, steps),
        out_shape=(
            jax.ShapeDtypeStruct((rows, width), BF16),
            jax.ShapeDtypeStruct((rows, 2 * width), BF16),
        ),
        in_specs=[pl.BlockSpec(memory_space=pltpu.SMEM)] + [vmem] * (3 + len(parts)),
        out_specs=(vmem, vmem),
        compiler_params=pltpu.CompilerParams(vmem_limit_bytes=24 * 2**20),
        cost_estimate=pl.CostEstimate(
            flops=20 * rows * width, bytes_accessed=rows * width * 30, transcendentals=rows * width
        ),
    )(order, pre, prob, cotangent, *parts)


def make_shards(dp_size, etp_size):
    outer, inner = split_dp(dp_size)

    def over_outer(value, k):
        pairs = [(i, i ^ (k * inner)) for i in range(dp_size)]
        return lax.ppermute(value, "dp", pairs)

    def over_inner(value, j):
        pairs = [(i, i ^ j) for i in range(dp_size)]
        return lax.ppermute(value, "dp", pairs)

    def over_etp(value, e):
        pairs = [(i, i ^ e) for i in range(etp_size)]
        return lax.ppermute(value, "etp", pairs)

    chunk_order = [0]
    bit = etp_size // 2
    bits = []
    while bit:
        bits.append(bit)
        chunk_order = chunk_order + [c ^ bit for c in chunk_order]
        bit //= 2

    def gather_etp(value, ties=()):
        for i, b in enumerate(bits):
            value = after(value, *ties[i]) if i < len(ties) else value
            value = jnp.concatenate([value, over_etp(value, b)], axis=0)
        return value

    def reduce_etp(*values):
        for b in reversed(bits):
            half = values[0].shape[0] // 2
            leaving = [value[half:].astype(BF16) for value in values]
            got = over_etp(jnp.concatenate(leaving, axis=0) if len(leaving) > 1 else leaving[0], b)
            values = [v[:half] + got[i * half : (i + 1) * half].astype(F32) for i, v in enumerate(values)]
        return [value.astype(BF16) for value in values]

    near_first = sorted(range(1, outer))
    far_first = near_first[::-1]
    keys = [0] + near_first
    relay = outer == 4

    def outer_pairs(value, pairs):
        pairs = [(s * inner + i, t * inner + i) for s, t in pairs for i in range(inner)]
        return lax.ppermute(value, "dp", pairs)

    swap = [(0, 1), (1, 0), (2, 3), (3, 2)]
    cycle = [(0, 2), (2, 3), (3, 1), (1, 0)]
    back = [(t, s) for s, t in cycle]
    middle = [(1, 2), (2, 1)]
    inward = [(0, 2), (3, 1)]
    outward = [(2, 0), (1, 3)]

    def shards(tokens, slots, gate_probs, w_gate, w_up, d_hidden):
        dp = lax.axis_index("dp")
        etp = lax.axis_index("etp")
        a, b = dp // inner, dp % inner
        at_end = (a == 0) | (a == outer - 1)
        depth, width = w_gate.shape
        cap = slots.shape[0]
        tok = tokens.shape[0]
        span = depth * inner

        def pick(first, second):
            return jnp.where(at_end, first, second)

        weights = [jnp.concatenate([w_gate, w_up], axis=1)]
        for j in range(1, inner):
            weights.append(jnp.concatenate([over_inner(w_gate, j), over_inner(w_up, j)], axis=1))
        weights = jnp.concatenate(weights, axis=0)

        onehot = (slots[:, None] == jnp.arange(tok, dtype=slots.dtype)[None, :]).astype(BF16)
        rows = jnp.dot(onehot, tokens, preferred_element_type=F32).astype(BF16)
        pieces = {}
        for k in keys:
            blocks = [
                lax.dynamic_slice(rows, (0, (a ^ k) * span + (b ^ j) * depth), (cap, depth))
                for j in range(inner)
            ]
            pieces[k] = jnp.concatenate(blocks, axis=1)
        got = {k: over_outer(pieces[k], k) for k in far_first}
        if relay:
            got[3], got[1] = pick(got[3], got[1]), pick(got[1], got[3])
        got[0] = pieces[0]

        x_chunks = {}

        def multiply(k, *ties):
            x_chunks[k] = after(x_chunks[k], *ties)
            return jnp.dot(x_chunks[k], weights, preferred_element_type=F32)

        if relay:
            x_chunks[3] = gather_etp(got[3])
            x_chunks[1] = gather_etp(got[1])
            far = multiply(3).astype(BF16)
            swapped = outer_pairs(far, swap)
            near = after(multiply(1, far).astype(BF16), far)
            crossed = outer_pairs(near, middle)
            x_chunks[2] = gather_etp(got[2], [[], [near]])
            x_chunks[0] = gather_etp(after(got[0], near))
            two = after(multiply(2, swapped), swapped)
            inwards = outer_pairs(two.astype(BF16), inward)
            relayed = pick(near, (after(two, swapped) + swapped.astype(F32)).astype(BF16))
            cycled = outer_pairs(relayed, back)
            own = multiply(0, relayed) + crossed.astype(F32) + inwards.astype(F32)
            own = own + jnp.where(at_end, swapped.astype(F32), 0.0)
            parts = [cycled]
            last = relayed
        else:
            last, parts = rows, []
            x_chunks[0] = gather_etp(got[0])
            for k in far_first:
                x_chunks[k] = gather_etp(got[k], [[last]])
                last = multiply(k).astype(BF16)
                parts.append(over_outer(last, k))
            own = multiply(0, last)
        probs = gather_etp(after(gate_probs, rows))
        order = etp ^ jnp.array(chunk_order, jnp.int32)
        hidden, paired = gate_call(order, own, probs[:, None], d_hidden, parts)

        grads, sums = {0: paired}, {}

        def advance(ks, last):
            partials = [
                lax.dot_general(
                    after(grads[k], last), weights, (((1,), (1,)), ((), ())), preferred_element_type=F32
                )
                for k in ks
            ]
            sums.update(zip(ks, reduce_etp(*partials)))
            return partials[-1]

        def weight_grad(ks, j, last):
            x_part = jnp.concatenate([x_chunks[k][:, j * depth : (j + 1) * depth] for k in ks], axis=0)
            grad_part = jnp.concatenate([grads[k] for k in ks], axis=0)
            return lax.dot_general(
                x_part, after(grad_part, last), (((0,), (0,)), ((), ())), preferred_element_type=F32
            )

        if relay:
            cycled = outer_pairs(paired, cycle)
            last = advance([0], paired)
            crossed = outer_pairs(after(paired, last), middle)
            outwards = outer_pairs(after(paired, last), outward)
            turn = after(pick(paired, cycled), paired)
            grads[3] = outer_pairs(turn, swap)
            grads[2] = pick(outwards, after(cycled, turn))
            grads[1] = pick(after(cycled, grads[2]), crossed)
            sequence = [0, 2, 3, 1]
            early, late = [0, 2], [3, 1]
            last = turn
        else:
            for k in near_first:
                grads[k] = over_outer(paired, k)
            sequence = keys
            early, late = keys[: max(outer - 1, 1)], keys[max(outer - 1, 1) :]
            last = grads[near_first[0]] if outer > 1 else paired
        for k in early:
            last = advance([k], last) if k not in sums else last

        leaving = []
        for j in range(1, inner):
            value = weight_grad(early, j, last)
            if late:
                value = after(value, last) + weight_grad(late, j, value)
            leaving.append(value.astype(BF16))
        arriving = [over_inner(leaving[j - 1], j) for j in range(1, inner)]
        last = leaving[0] if inner > 1 else last
        if late:
            last = advance(late, last)
        total = weight_grad(sequence, 0, last)
        last = sums[sequence[-1]]
        returned = {0: sums[0]}
        if relay:
            returned[2] = over_outer(sums[2], 2)
            sums[3], sums[1] = pick(sums[3], sums[1]), pick(sums[1], sums[3])
            sums[3], sums[1] = after(sums[3], returned[2]), after(sums[1], returned[2])
        dx = jnp.zeros((cap, outer * span), BF16)
        for k in keys:
            own = returned[k] if k in returned else over_outer(sums[k], k)
            if k != sequence[-1]:
                own = after(own, last)
            for j in range(inner):
                block = own[:, j * depth : (j + 1) * depth]
                dx = lax.dynamic_update_slice(dx, block, (0, (a ^ k) * span + (b ^ j) * depth))
        grad_tokens = lax.dot_general(
            onehot, dx, (((0,), (0,)), ((), ())), preferred_element_type=F32
        ).astype(BF16)
        gate_total, up_total = total[:, :width], total[:, width:]
        for part in arriving:
            part = after(part, grad_tokens)
            gate_total = gate_total + part[:, :width].astype(F32)
            up_total = up_total + part[:, width:].astype(F32)
        return (hidden, grad_tokens, gate_total, up_total)

    return shards


def solution(mesh):
    in_specs = (
        P(("dp", "etp"), None),
        P(("dp", "etp")),
        P(("dp", "etp")),
        P("dp", "etp"),
        P("dp", "etp"),
        P("dp", "etp"),
    )
    out_specs = (P("dp", "etp"), P(("dp", "etp"), None), P("dp", "etp"), P("dp", "etp"))
    shards = make_shards(mesh.shape["dp"], mesh.shape["etp"])
    return jax.shard_map(shards, mesh=mesh, in_specs=in_specs, out_specs=out_specs, check_vma=False)
```

```python
import functools

import jax
import jax.numpy as jnp
from jax import lax
from jax.experimental import pallas as pl
from jax.experimental.pallas import tpu as pltpu
from jax.sharding import PartitionSpec as P

F32 = jnp.float32
BF16 = jnp.bfloat16


def split_dp(dp):
    outer = 1
    while 4 * outer * outer <= 2 * dp:
        outer *= 2
    return outer, dp // outer


def after(value, *others):
    return lax.optimization_barrier((value,) + others)[0]


def gate_kernel(steps, order_ref, pre_ref, prob_ref, cot_ref, *refs):
    part_refs, (hidden_ref, grad_ref) = refs[:-2], refs[-2:]
    rows, width = cot_ref.shape
    cap = rows // steps
    for i in range(steps):
        here = pl.ds(i * cap, cap)
        there = pl.ds(pl.multiple_of(order_ref[i] * cap, cap), cap)
        total = pre_ref[here, :]
        for part_ref in part_refs:
            total = total + part_ref[here, :].astype(F32)
        gate, up = total[:, :width], total[:, width:]
        prob = prob_ref[here, :].astype(F32)
        sig = jax.nn.sigmoid(gate)
        act = gate * sig
        hidden_ref[there, :] = (prob * act * up).astype(BF16)
        scaled = cot_ref[there, :].astype(F32) * prob
        grad_ref[here, :width] = (scaled * up * sig * (1.0 + gate * (1.0 - sig))).astype(BF16)
        grad_ref[here, width:] = (scaled * act).astype(BF16)


def gate_call(order, pre, prob, cotangent, parts):
    rows, width = cotangent.shape
    steps = order.shape[0]
    vmem = pl.BlockSpec(memory_space=pltpu.VMEM)
    return pl.pallas_call(
        functools.partial(gate_kernel, steps),
        out_shape=(
            jax.ShapeDtypeStruct((rows, width), BF16),
            jax.ShapeDtypeStruct((rows, 2 * width), BF16),
        ),
        in_specs=[pl.BlockSpec(memory_space=pltpu.SMEM)] + [vmem] * (3 + len(parts)),
        out_specs=(vmem, vmem),
        compiler_params=pltpu.CompilerParams(vmem_limit_bytes=24 * 2**20),
        cost_estimate=pl.CostEstimate(
            flops=20 * rows * width, bytes_accessed=rows * width * 30, transcendentals=rows * width
        ),
    )(order, pre, prob, cotangent, *parts)


def make_shards(dp_size, etp_size):
    outer, inner = split_dp(dp_size)

    def over_outer(value, k):
        pairs = [(i, i ^ (k * inner)) for i in range(dp_size)]
        return lax.ppermute(value, "dp", pairs)

    def over_inner(value, j):
        pairs = [(i, i ^ j) for i in range(dp_size)]
        return lax.ppermute(value, "dp", pairs)

    def over_etp(value, e):
        pairs = [(i, i ^ e) for i in range(etp_size)]
        return lax.ppermute(value, "etp", pairs)

    chunk_order = [0]
    bit = etp_size // 2
    bits = []
    while bit:
        bits.append(bit)
        chunk_order = chunk_order + [c ^ bit for c in chunk_order]
        bit //= 2

    def gather_etp(value, ties=()):
        for i, b in enumerate(bits):
            value = after(value, *ties[i]) if i < len(ties) else value
            value = jnp.concatenate([value, over_etp(value, b)], axis=0)
        return value

    def reduce_etp(*values):
        for b in reversed(bits):
            half = values[0].shape[0] // 2
            leaving = [value[half:].astype(BF16) for value in values]
            got = over_etp(jnp.concatenate(leaving, axis=0) if len(leaving) > 1 else leaving[0], b)
            values = [v[:half] + got[i * half : (i + 1) * half].astype(F32) for i, v in enumerate(values)]
        return [value.astype(BF16) for value in values]

    near_first = sorted(range(1, outer))
    far_first = near_first[::-1]
    keys = [0] + near_first
    relay = outer == 4

    def outer_pairs(value, pairs):
        pairs = [(s * inner + i, t * inner + i) for s, t in pairs for i in range(inner)]
        return lax.ppermute(value, "dp", pairs)

    swap = [(0, 1), (1, 0), (2, 3), (3, 2)]
    cycle = [(0, 2), (2, 3), (3, 1), (1, 0)]
    back = [(t, s) for s, t in cycle]
    middle = [(1, 2), (2, 1)]
    inward = [(0, 2), (3, 1)]
    outward = [(2, 0), (1, 3)]

    def shards(tokens, slots, gate_probs, w_gate, w_up, d_hidden):
        dp = lax.axis_index("dp")
        etp = lax.axis_index("etp")
        a, b = dp // inner, dp % inner
        at_end = (a == 0) | (a == outer - 1)
        depth, width = w_gate.shape
        cap = slots.shape[0]
        tok = tokens.shape[0]
        span = depth * inner

        def pick(first, second):
            return jnp.where(at_end, first, second)

        weights = [jnp.concatenate([w_gate, w_up], axis=1)]
        for j in range(1, inner):
            weights.append(jnp.concatenate([over_inner(w_gate, j), over_inner(w_up, j)], axis=1))
        weights = jnp.concatenate(weights, axis=0)

        onehot = (slots[:, None] == jnp.arange(tok, dtype=slots.dtype)[None, :]).astype(BF16)
        rows = jnp.dot(onehot, tokens, preferred_element_type=F32).astype(BF16)
        pieces = {}
        for k in keys:
            blocks = [
                lax.dynamic_slice(rows, (0, (a ^ k) * span + (b ^ j) * depth), (cap, depth))
                for j in range(inner)
            ]
            pieces[k] = jnp.concatenate(blocks, axis=1)
        got = {k: over_outer(pieces[k], k) for k in far_first}
        if relay:
            got[3], got[1] = pick(got[3], got[1]), pick(got[1], got[3])
        got[0] = jnp.concatenate(
            [pieces[0], jnp.broadcast_to(gate_probs[:, None], (cap, 128))], axis=1
        )

        x_chunks = {}

        def multiply(k, *ties):
            x_chunks[k] = after(x_chunks[k], *ties)
            return jnp.dot(x_chunks[k], weights, preferred_element_type=F32)

        if relay:
            x_chunks[3] = gather_etp(got[3])
            x_chunks[1] = gather_etp(got[1])
            far = multiply(3).astype(BF16)
            swapped = outer_pairs(far, swap)
            near = after(multiply(1, far).astype(BF16), far)
            crossed = outer_pairs(near, middle)
            x_chunks[2] = gather_etp(got[2], [[], [near]])
            joined = gather_etp(after(got[0], near))
            x_chunks[0], probs = joined[:, :span], joined[:, span : span + 1]
            two = after(multiply(2, swapped), swapped)
            inwards = outer_pairs(two.astype(BF16), inward)
            relayed = pick(near, (after(two, swapped) + swapped.astype(F32)).astype(BF16))
            cycled = outer_pairs(relayed, back)
            own = multiply(0, relayed) + crossed.astype(F32) + inwards.astype(F32)
            own = own + jnp.where(at_end, swapped.astype(F32), 0.0)
            parts = [cycled]
            last = relayed
        else:
            last, parts = rows, []
            joined = gather_etp(got[0])
            x_chunks[0], probs = joined[:, :span], joined[:, span : span + 1]
            for k in far_first:
                x_chunks[k] = gather_etp(got[k], [[last]])
                last = multiply(k).astype(BF16)
                parts.append(over_outer(last, k))
            own = multiply(0, last)
        order = etp ^ jnp.array(chunk_order, jnp.int32)
        hidden, paired = gate_call(order, own, probs, d_hidden, parts)

        grads, sums = {0: paired}, {}

        def advance(ks, last):
            partials = [
                lax.dot_general(
                    after(grads[k], last), weights, (((1,), (1,)), ((), ())), preferred_element_type=F32
                )
                for k in ks
            ]
            sums.update(zip(ks, reduce_etp(*partials)))
            return partials[-1]

        def weight_grad(ks, j, last):
            x_part = jnp.concatenate([x_chunks[k][:, j * depth : (j + 1) * depth] for k in ks], axis=0)
            grad_part = jnp.concatenate([grads[k] for k in ks], axis=0)
            return lax.dot_general(
                x_part, after(grad_part, last), (((0,), (0,)), ((), ())), preferred_element_type=F32
            )

        if relay:
            cycled = outer_pairs(paired, cycle)
            last = advance([0], paired)
            crossed = outer_pairs(after(paired, last), middle)
            outwards = outer_pairs(after(paired, last), outward)
            turn = after(pick(paired, cycled), paired)
            grads[3] = outer_pairs(turn, swap)
            grads[2] = pick(outwards, after(cycled, turn))
            grads[1] = pick(after(cycled, grads[2]), crossed)
            sequence = [0, 2, 3, 1]
            early, late = [0, 2], [3, 1]
            last = turn
        else:
            for k in near_first:
                grads[k] = over_outer(paired, k)
            sequence = keys
            early, late = keys[: max(outer - 1, 1)], keys[max(outer - 1, 1) :]
            last = grads[near_first[0]] if outer > 1 else paired
        for k in early:
            last = advance([k], last) if k not in sums else last

        leaving = []
        for j in range(1, inner):
            value = weight_grad(early, j, last)
            if late:
                value = after(value, last) + weight_grad(late, j, value)
            leaving.append(value.astype(BF16))
        arriving = [over_inner(leaving[j - 1], j) for j in range(1, inner)]
        last = leaving[0] if inner > 1 else last
        if late:
            last = advance(late, last)
        total = weight_grad(sequence, 0, last)
        gate_total, up_total = total[:, :width], total[:, width:]
        for part in arriving:
            gate_total = gate_total + part[:, :width].astype(F32)
            up_total = up_total + part[:, width:].astype(F32)

        last = sums[sequence[-1]]
        if relay:
            sums[3], sums[1] = pick(sums[3], sums[1]), pick(sums[1], sums[3])
        dx = jnp.zeros((cap, outer * span), BF16)
        for k in keys:
            own = over_outer(sums[k], k) if k else sums[k]
            if k != sequence[-1]:
                own = after(own, last)
            for j in range(inner):
                block = own[:, j * depth : (j + 1) * depth]
                dx = lax.dynamic_update_slice(dx, block, (0, (a ^ k) * span + (b ^ j) * depth))
        grad_tokens = lax.dot_general(
            onehot, dx, (((0,), (0,)), ((), ())), preferred_element_type=F32
        ).astype(BF16)
        return (hidden, grad_tokens, gate_total, up_total)

    return shards


def solution(mesh):
    in_specs = (
        P(("dp", "etp"), None),
        P(("dp", "etp")),
        P(("dp", "etp")),
        P("dp", "etp"),
        P("dp", "etp"),
        P("dp", "etp"),
    )
    out_specs = (P("dp", "etp"), P(("dp", "etp"), None), P("dp", "etp"), P("dp", "etp"))
    shards = make_shards(mesh.shape["dp"], mesh.shape["etp"])
    return jax.shard_map(shards, mesh=mesh, in_specs=in_specs, out_specs=out_specs, check_vma=False)
```
